128 devices in a mesh: dp: 8 (over x, core), wide: 16 (over z, y).
Axes of the slice: x: 4, y: 4, z: 4, core: 2. Of those that a mesh axis runs over, the one named last changes fastest.
Arguments:
- volume: bfloat16 [8, 32, 16, 16, 128], P('dp', 'wide'), may hold values from -6 to 6
- kernel_five: bfloat16 [3, 3, 3, 128, 256], replicated, may hold values from -0.109375 to 0.109375
- kernel_six: bfloat16 [3, 3, 3, 256, 256], replicated, may hold values from -0.078125 to 0.078125
- cotangent: bfloat16 [8, 8, 4, 4, 256], P('dp', None, None, None, 'wide'), may hold values from -6 to 6
Outputs:
- next_input: bfloat16 [8, 8, 4, 4, 256], P('dp', None, None, None, 'wide')
- kernel_five_grad: float32 [3, 3, 3, 128, 256], P(None, None, None, None, 'wide')
- kernel_six_grad: float32 [3, 3, 3, 256, 256], P(None, None, None, None, 'wide')
The draws below stay inside these ranges and needn't reach their ends.
All inputs are finite; a program needn't handle non-finite values.
Results may differ from the reference program's by a relative error of at most 0.01.
Values may be sent and summed in bfloat16 or wider, within the bound.
No kernel may reach another device: no remote copies, remote signals or barrier semaphores. Data moves between devices by JAX's collectives and lax.ppermute only.
A program may use at most 128 MiB of HBM per device.

```python
import jax
import jax.numpy as jnp
from jax import lax

C5 = 128
C6 = 256
SIDE = 16
VOLS = 8
DEPTH = 32


def steps_of(key, shape, shards, least, high):
    gain = 1.0
    for position, parts in shards:
        steps = jax.random.uniform(jax.random.fold_in(jax.random.fold_in(key, 6), position), (parts,), jnp.float32, least / len(shards), high / len(shards))
        gain = gain * jnp.repeat(jnp.exp(steps), shape[position] // parts).reshape((-1,) + (1,) * (len(shape) - 1 - position))
    return gain


def normal_values(key, shape, scale, most, split=(), kind=jnp.bfloat16):
    result = scale * jax.random.normal(key, shape, jnp.float32)
    if split:
        result = result * steps_of(key, shape, split, -0.22, 0.18)
    return jnp.clip(result, -most, most).astype(kind)


def setup_inputs(seed: int = 0) -> dict:
    arg_keys = jax.random.split(jax.random.key(seed), 5)
    volume = normal_values(arg_keys[0], (VOLS, DEPTH, SIDE, SIDE, C5), 1.0, 6.0, ((0, 8), (1, 16)))
    kernel_five = normal_values(arg_keys[1], (3, 3, 3, C5, C6), (27 * C5) ** -0.5, 0.109375)
    kernel_six = normal_values(arg_keys[2], (3, 3, 3, C6, C6), (27 * C6) ** -0.5, 0.078125)
    cotangent = normal_values(arg_keys[3], (VOLS, DEPTH // 4, SIDE // 4, SIDE // 4, C6), 1.0, 6.0, ((0, 8), (4, 16)))
    return {"volume": volume, "kernel_five": kernel_five, "kernel_six": kernel_six, "cotangent": cotangent}


SLOPE = 0.3

def activate(value):
    return SLOPE * value + (1.0 - SLOPE) * value * jax.nn.sigmoid(value)

def slope_of(value):
    sigma = jax.nn.sigmoid(value)
    return SLOPE + (1.0 - SLOPE) * (sigma + value * sigma * (1.0 - sigma))

def convolve(field, kernel):
    return lax.conv_general_dilated(field[None], kernel, (1, 1, 1), 'SAME', dimension_numbers=('NDHWC', 'DHWIO', 'NDHWC'), precision=lax.Precision.HIGHEST)[0]

def shrink(field):
    return field.reshape(field.shape[0] // 2, 2, field.shape[1] // 2, 2, field.shape[2] // 2, 2, field.shape[3]).mean(axis=(1, 3, 5))

def expand(field):
    grown = jnp.broadcast_to(field[:, None, :, None, :, None, :], (field.shape[0], 2, field.shape[1], 2, field.shape[2], 2, field.shape[3]))
    return grown.reshape(2 * field.shape[0], 2 * field.shape[1], 2 * field.shape[2], field.shape[3])

def reference(volume, kernel_five, kernel_six, cotangent):
    five = kernel_five.astype(jnp.float32)
    six = kernel_six.astype(jnp.float32)

    def one_volume(carry, inputs):
        field = inputs[0].astype(jnp.float32)
        upstream = inputs[1].astype(jnp.float32)
        pre_five = convolve(field, five)
        pooled = shrink(activate(pre_five)).astype(jnp.bfloat16)
        pooled_wide = lax.optimization_barrier(pooled).astype(jnp.float32)
        pre_six = convolve(pooled_wide, six)
        next_input = shrink(activate(pre_six)).astype(jnp.bfloat16)
        grad_six = (expand(upstream) * 0.125 * slope_of(pre_six)).astype(jnp.bfloat16)
        grad_six = lax.optimization_barrier(grad_six).astype(jnp.float32)
        _, pull_six = jax.vjp(lambda field_in, kernel: convolve(field_in, kernel), pooled_wide, six)
        grad_pooled, weight_six = pull_six(grad_six)
        grad_five = (expand(grad_pooled) * 0.125 * slope_of(pre_five)).astype(jnp.bfloat16)
        grad_five = lax.optimization_barrier(grad_five).astype(jnp.float32)
        _, pull_five = jax.vjp(lambda kernel: convolve(field, kernel), five)
        weight_five = pull_five(grad_five)[0]
        return ((carry[0] + weight_five, carry[1] + weight_six), next_input)
    start = (jnp.zeros(five.shape, jnp.float32), jnp.zeros(six.shape, jnp.float32))
    totals, next_inputs = lax.scan(one_volume, start, (volume, cotangent))
    return (next_inputs, totals[0], totals[1])
```

```python
import jax
import jax.numpy as jnp
from jax import lax
from jax.sharding import PartitionSpec as P

SLOPE = 0.3
HALF_TAPS = 14


def activate(value):
    return SLOPE * value + (1.0 - SLOPE) * value * jax.nn.sigmoid(value)


def slope_of(value):
    sigma = jax.nn.sigmoid(value)
    return SLOPE + (1.0 - SLOPE) * (sigma + value * sigma * (1.0 - sigma))


def shrink(values):
    planes, rows, cols, channels = values.shape
    return values.reshape(planes // 2, 2, rows // 2, 2, cols // 2, 2, channels).mean(
        axis=(1, 3, 5)
    )


def expand(values):
    planes, rows, cols, channels = values.shape
    grown = jnp.broadcast_to(
        values[:, None, :, None, :, None, :], (planes, 2, rows, 2, cols, 2, channels)
    )
    return grown.reshape(2 * planes, 2 * rows, 2 * cols, channels)


def pad_sides(values):
    return jnp.pad(values, ((0, 0), (1, 1), (1, 1), (0, 0)))


def window(padded, tap, planes, side):
    depth_tap, row_tap, col_tap = tap // 9, (tap // 3) % 3, tap % 3
    return padded[
        depth_tap : depth_tap + planes, row_tap : row_tap + side, col_tap : col_tap + side, :
    ].reshape(planes * side * side, -1)


def convolve(padded, kernel, planes, side):
    wide = jnp.concatenate([window(padded, tap, planes, side) for tap in range(27)], axis=-1)
    return jnp.dot(wide, kernel.reshape(-1, kernel.shape[-1]), preferred_element_type=jnp.float32)


def shift_perm(axis, step):
    count = lax.axis_size(axis)
    return [(i, i + step) for i in range(count) if 0 <= i + step < count]


def forward_five(slab, low, high, kernel, cot_rows):
    planes, side = slab.shape[0], slab.shape[1]
    padded = pad_sides(jnp.concatenate([low, slab, high], axis=0))
    pre = convolve(padded, kernel, planes, side)
    pooled = shrink(activate(pre).reshape(planes, side, side, -1)).astype(jnp.bfloat16)
    cells = pooled.reshape(-1, pooled.shape[-1])
    message = jnp.concatenate([cells[:, :128], cells[:, 128:], cot_rows], axis=0)
    return pre, message, padded


def to_all(message, axis):
    count = lax.axis_size(axis)
    copies = jnp.broadcast_to(message[None], (count,) + message.shape)
    return lax.all_to_all(copies, axis, split_axis=0, concat_axis=0, tiled=True)


def back_five(pooled, cot, kernel, pre_five, position):
    filters = pooled.shape[-1]
    ring = jnp.pad(pooled, ((2, 2), (0, 0), (0, 0), (0, 0)))
    near = lax.dynamic_slice_in_dim(ring, position, 5, 0)
    pre_six = convolve(pad_sides(near), kernel, 3, 8).reshape(3, 8, 8, filters)
    up = jnp.pad(expand(cot), ((1, 1), (0, 0), (0, 0), (0, 0)))
    upstream = lax.dynamic_slice_in_dim(up, position, 3, 0).astype(jnp.float32)
    grad_six = (upstream * 0.125 * slope_of(pre_six)).astype(jnp.bfloat16)
    flipped = jnp.flip(kernel, (0, 1, 2)).transpose(0, 1, 2, 4, 3)
    grad_pooled = convolve(pad_sides(grad_six), flipped, 1, 8).reshape(1, 8, 8, filters)
    grown = expand(grad_pooled).reshape(-1, filters)
    grad_five = (grown * 0.125 * slope_of(pre_five)).astype(jnp.bfloat16)
    return grad_five


def weight_five(padded, grad_five, half):
    planes = padded.shape[0] - 2
    side = padded.shape[1] - 2
    rows = grad_five.T
    pieces = [
        jnp.dot(rows, window(padded, tap, planes, side), preferred_element_type=jnp.float32)
        for tap in range(27)
    ]
    pieces.append(jnp.zeros_like(pieces[0]))
    full = jnp.stack(pieces).astype(jnp.bfloat16)
    mine = lax.dynamic_slice_in_dim(full, half * HALF_TAPS, HALF_TAPS, 0)
    theirs = lax.dynamic_slice_in_dim(full, (1 - half) * HALF_TAPS, HALF_TAPS, 0)

    def by_target(values):
        return values.reshape(HALF_TAPS, 16, 16, 128).transpose(1, 0, 2, 3)

    return by_target(mine), by_target(theirs)


def six_own(pooled, kernel, cot_own, position, half):
    depth, side = pooled.shape[0], pooled.shape[1]
    share = cot_own.shape[-1]
    own = lax.dynamic_slice_in_dim(kernel, position * share, share, 4)
    padded = jnp.pad(pooled, ((1, 1), (1, 1), (1, 1), (0, 0)))
    pre = convolve(padded, own, depth, side).reshape(depth, side, side, share)
    next_input = shrink(activate(pre)).astype(jnp.bfloat16)
    upstream = expand(cot_own).astype(jnp.float32)
    grad = (upstream * 0.125 * slope_of(pre)).astype(jnp.bfloat16).reshape(-1, share)
    rows = grad.T
    pieces = [
        jnp.dot(rows, window(padded, tap, depth, side), preferred_element_type=jnp.float32)
        for tap in range(27)
    ]
    pieces.append(jnp.zeros_like(pieces[0]))
    full = jnp.stack(pieces).astype(jnp.bfloat16)
    mine = lax.dynamic_slice_in_dim(full, half * HALF_TAPS, HALF_TAPS, 0)
    theirs = lax.dynamic_slice_in_dim(full, (1 - half) * HALF_TAPS, HALF_TAPS, 0)
    return next_input, mine, theirs


def core_swap(values):
    count = lax.axis_size("dp")
    return lax.ppermute(values, "dp", [(i, i ^ 1) for i in range(count)])


def sum_over_chips(values):
    count = lax.axis_size("dp")
    total = values.astype(jnp.float32)
    for step in range(1, count // 2):
        pairs = [(i, (i + 2 * step) % count) for i in range(count)]
        total = total + lax.ppermute(values, "dp", pairs).astype(jnp.float32)
    return total


def shards(volume, kernel_five, kernel_six, cotangent):
    position = lax.axis_index("wide")
    half = lax.axis_index("dp") % 2
    slab = volume[0]
    low = lax.ppermute(slab[-1:], "wide", shift_perm("wide", 1))
    high = lax.ppermute(slab[:1], "wide", shift_perm("wide", -1))
    cot_own = cotangent[0]
    cot_rows = cot_own.reshape(128, 16).T
    pre_five, message, padded = forward_five(slab, low, high, kernel_five, cot_rows)
    gathered = to_all(message, "wide")
    pooled = jnp.concatenate([gathered[:, :64], gathered[:, 64:128]], axis=-1)
    pooled = pooled.reshape(16, 8, 8, 256)
    cot = gathered[:, 128:].reshape(256, 128).T.reshape(8, 4, 4, 256)
    grad_five = back_five(pooled, cot, kernel_six, pre_five, position)
    mine_five, theirs_five = weight_five(padded, grad_five, half)
    next_input, mine_six, theirs_six = six_own(pooled, kernel_six, cot_own, position, half)
    got_five = core_swap(theirs_five)
    got_six = core_swap(theirs_six)
    pair_five = mine_five + got_five
    pair_six = mine_six + got_six
    spread = lax.all_to_all(pair_five, "wide", split_axis=0, concat_axis=0, tiled=True)
    depth_five = spread.astype(jnp.float32).sum(0).astype(jnp.bfloat16)
    both = jnp.concatenate([depth_five, pair_six], axis=-1)
    total = sum_over_chips(both).astype(jnp.bfloat16)
    other = core_swap(total)
    first = jnp.where(half == 0, total, other)
    second = jnp.where(half == 0, other, total)
    whole = jnp.concatenate([first, second], axis=0)[:27].astype(jnp.float32)
    out_five = whole[:, :, :128].transpose(0, 2, 1).reshape(3, 3, 3, 128, 16)
    out_six = whole[:, :, 128:].transpose(0, 2, 1).reshape(3, 3, 3, 256, 16)
    return (next_input[None], out_five, out_six)


def solution(mesh):
    in_specs = (P("dp", "wide", None, None, None), P(), P(), P("dp", None, None, None, "wide"))
    out_specs = (
        P("dp", None, None, None, "wide"),
        P(None, None, None, None, "wide"),
        P(None, None, None, None, "wide"),
    )
    return jax.shard_map(shards, mesh=mesh, in_specs=in_specs, out_specs=out_specs, check_vma=False)
```

```python
import jax
import jax.numpy as jnp
from jax import lax
from jax.experimental import pallas as pl
from jax.experimental.pallas import tpu as pltpu
from jax.sharding import PartitionSpec as P

SLOPE = 0.3
HALF_TAPS = 14
VMEM = pltpu.VMEM
NT = (((1,), (1,)), ((), ()))


def both_of(value):
    sigma = 1.0 / (1.0 + jnp.exp(-value))
    act = value * (SLOPE + (1.0 - SLOPE) * sigma)
    slope = 0.125 * SLOPE + (0.125 * (1.0 - SLOPE)) * (sigma + value * sigma * (1.0 - sigma))
    return act, slope


def call(body, out_shape, scratch, operands, scalars=(), flops=0, limit=32):
    specs = [pl.BlockSpec(memory_space=pltpu.SMEM)] * len(scalars)
    specs += [pl.BlockSpec(memory_space=VMEM)] * len(operands)
    outs = jax.tree.map(lambda _: pl.BlockSpec(memory_space=VMEM), out_shape)
    return pl.pallas_call(
        body,
        out_shape=out_shape,
        in_specs=specs,
        out_specs=outs,
        scratch_shapes=scratch,
        compiler_params=pltpu.CompilerParams(vmem_limit_bytes=limit * 1024 * 1024),
        cost_estimate=pl.CostEstimate(flops=flops, bytes_accessed=4_000_000, transcendentals=0),
    )(*scalars, *operands)


def shape(dims, kind):
    return jax.ShapeDtypeStruct(dims, kind)


def shifted_rows(values, step, period):
    if step == 0:
        return values
    count = values.shape[0]
    column = lax.broadcasted_iota(jnp.int32, values.shape, 0) % period
    rolled = pltpu.roll(values, (-step) % count, 0)
    inside = (column + step >= 0) & (column + step < period)
    return jnp.where(inside, rolled, 0.0)


def forward_five_kernel(slab, low, high, kernel, cot, message, slope, padded, tall):
    for plane in range(4):
        if plane == 0:
            source = low[...]
        elif plane == 3:
            source = high[...]
        else:
            source = slab[plane - 1]
        values = source.astype(jnp.float32)
        padded[plane, 0:16, :] = jnp.zeros((16, 384), jnp.bfloat16)
        padded[plane, 272:288, :] = jnp.zeros((16, 384), jnp.bfloat16)
        padded[plane, 16:272, 0:128] = shifted_rows(values, -1, 16).astype(jnp.bfloat16)
        padded[plane, 16:272, 128:256] = source
        padded[plane, 16:272, 256:384] = shifted_rows(values, 1, 16).astype(jnp.bfloat16)
    acts = []
    for plane in range(2):
        total = jnp.zeros((256, 256), jnp.float32)
        for depth_tap in range(3):
            for row_tap in range(3):
                start = (depth_tap * 3 + row_tap) * 384
                total += jnp.dot(
                    padded[plane + depth_tap, 16 * row_tap : 16 * row_tap + 256, :],
                    kernel[start : start + 384, :],
                    preferred_element_type=jnp.float32,
                )
        act, slant = both_of(total)
        slope[plane * 256 : (plane + 1) * 256, :] = slant
        acts.append(act)
    two = (acts[0] + acts[1]).reshape(8, 2, 16, 256)
    pairs = (two[:, 0] + two[:, 1]).reshape(128, 256)
    pooled = []
    for side in range(2):
        tall[side] = pairs[:, side * 128 : (side + 1) * 128]
        even = tall[side, pl.ds(0, 64, stride=2), :]
        odd = tall[side, pl.ds(1, 64, stride=2), :]
        pooled.append(((even + odd) * 0.125).astype(jnp.bfloat16))
    marks = cot[...]
    for target in range(16):
        message[target, 0:64, :] = pooled[0]
        message[target, 64:128, :] = pooled[1]
        message[target, 128:144, :] = marks


def forward_five(slab, low, high, kernel, cot_rows):
    return call(
        forward_five_kernel,
        (
            shape((16, 144, 128), jnp.bfloat16),
            shape((512, 256), jnp.float32),
            shape((4, 288, 384), jnp.bfloat16),
        ),
        [VMEM((2, 128, 128), jnp.float32)],
        (
            slab.reshape(2, 256, 128),
            low.reshape(256, 128),
            high.reshape(256, 128),
            kernel.reshape(3456, 256),
            cot_rows,
        ),
        flops=900_000_000,
    )


def own_taps_kernel(position, kernel, own):
    rows = lax.broadcasted_iota(jnp.int32, (16, 256), 0) + position[0] * 16
    lanes = lax.broadcasted_iota(jnp.int32, (16, 256), 1)
    pick = jnp.where(rows == lanes, 1.0, 0.0).astype(jnp.bfloat16)
    for tap in range(27):
        chosen = lax.dot_general(pick, kernel[tap], NT, preferred_element_type=jnp.float32)
        own[tap] = chosen.astype(jnp.bfloat16)


def own_taps(kernel, position):
    return call(
        own_taps_kernel,
        shape((27, 16, 256), jnp.bfloat16),
        [],
        (kernel.reshape(27, 256, 256),),
        (position,),
        flops=900_000_000,
    )


def six_to_five(position, gathered, kernel, slope, rows_out, near, tall):
    for plane in range(5):
        where = position[0] + (plane - 2)
        inside = (where >= 0) & (where < 16)
        index = jnp.clip(where, 0, 15)
        left = gathered[index, 0:64, :]
        right = gathered[index, 64:128, :]
        values = jnp.concatenate([left, right], axis=1).astype(jnp.float32)
        values = jnp.where(inside, values, 0.0)
        blank = jnp.zeros((8, 256), jnp.float32)
        for col_tap in range(3):
            moved = shifted_rows(values, col_tap - 1, 8)
            for row_tap in range(3):
                if row_tap == 0:
                    cells = jnp.concatenate([blank, moved[:56]], axis=0)
                elif row_tap == 1:
                    cells = moved
                else:
                    cells = jnp.concatenate([moved[8:], blank], axis=0)
                lane = (row_tap * 3 + col_tap) * 256
                near[plane, :, lane : lane + 256] = cells.astype(jnp.bfloat16)
    pre_six = jnp.zeros((192, 256), jnp.float32)
    for depth_tap in range(3):
        taps = kernel[depth_tap * 9 : depth_tap * 9 + 9].reshape(2304, 256)
        cells = near[depth_tap : depth_tap + 3].reshape(192, 2304)
        pre_six += jnp.dot(cells, taps, preferred_element_type=jnp.float32)
    _, slant = both_of(pre_six)
    cell = lax.broadcasted_iota(jnp.int32, (192, 128), 0)
    lanes = lax.broadcasted_iota(jnp.int32, (192, 128), 1)
    depth = cell // 64 + position[0] - 1
    small = (depth >> 1) * 16 + ((cell % 64) >> 4) * 4 + ((cell % 8) >> 1)
    hit = (small == lanes) & (depth >= 0) & (depth < 16)
    grow = jnp.where(hit, 1.0, 0.0).astype(jnp.bfloat16)
    cot = gathered[:, 128:144, :].reshape(256, 128)
    upstream = lax.dot_general(grow, cot, NT, preferred_element_type=jnp.float32)
    grad_six = (upstream * slant).astype(jnp.bfloat16).astype(jnp.float32)
    grad_pooled = jnp.zeros((64, 256), jnp.float32)
    blank = jnp.zeros((8, 256), jnp.float32)
    for depth_tap in range(3):
        values = grad_six[(2 - depth_tap) * 64 : (3 - depth_tap) * 64]
        for col_tap in range(3):
            moved = shifted_rows(values, 1 - col_tap, 8)
            for row_tap in range(3):
                if row_tap == 0:
                    cells = jnp.concatenate([moved[8:], blank], axis=0)
                elif row_tap == 1:
                    cells = moved
                else:
                    cells = jnp.concatenate([blank, moved[:56]], axis=0)
                grad_pooled += lax.dot_general(
                    cells.astype(jnp.bfloat16),
                    kernel[depth_tap * 9 + row_tap * 3 + col_tap],
                    NT,
                    preferred_element_type=jnp.float32,
                )
    for side in range(2):
        tall[side, pl.ds(0, 64, stride=2), :] = grad_pooled[:, side * 128 : (side + 1) * 128]
        tall[side, pl.ds(1, 64, stride=2), :] = grad_pooled[:, side * 128 : (side + 1) * 128]
    both = jnp.concatenate([tall[0], tall[1]], axis=1)
    wide = jnp.broadcast_to(both.reshape(8, 1, 16, 256), (8, 2, 16, 256)).reshape(256, 256)
    for plane in range(2):
        grad = wide * slope[plane * 256 : (plane + 1) * 256, :]
        rows_out[:, plane * 256 : (plane + 1) * 256] = grad.T.astype(jnp.bfloat16)


def half_of_five(first, rows, padded, out):
    for step in range(HALF_TAPS):
        tap = jnp.minimum(first + step, 26)
        depth_tap, row_tap, col_tap = tap // 9, (tap // 3) % 3, tap % 3
        total = jnp.zeros((256, 128), jnp.float32)
        for plane in range(2):
            cells = padded[
                plane + depth_tap,
                pl.ds(pl.multiple_of(row_tap * 16, 16), 256),
                pl.ds(pl.multiple_of(col_tap * 128, 128), 128),
            ]
            total += jnp.dot(
                rows[:, plane * 256 : (plane + 1) * 256],
                cells,
                preferred_element_type=jnp.float32,
            )
        out[:, step] = total.astype(jnp.bfloat16).reshape(16, 16, 128)


def back_kernel(position, half, gathered, kernel, slope, padded, rows, theirs, near, tall):
    six_to_five(position, gathered, kernel, slope, rows, near, tall)
    half_of_five((1 - half[0]) * HALF_TAPS, rows, padded, theirs)


def back_five(gathered, kernel, slope, padded, position, half):
    return call(
        back_kernel,
        (shape((256, 512), jnp.bfloat16), shape((16, HALF_TAPS, 16, 128), jnp.bfloat16)),
        [VMEM((5, 64, 2304), jnp.bfloat16), VMEM((2, 128, 128), jnp.float32)],
        (gathered, kernel.reshape(27, 256, 256), slope, padded),
        (position, half),
        flops=3_000_000_000,
    )


def mine_kernel(half, rows, padded, mine):
    half_of_five(half[0] * HALF_TAPS, rows, padded, mine)


def mine_of_five(rows, padded, half):
    return call(
        mine_kernel,
        shape((16, HALF_TAPS, 16, 128), jnp.bfloat16),
        [],
        (rows, padded),
        (half,),
        flops=900_000_000,
    )


def shifted_lanes(values, step, period, inner):
    if step == 0:
        return values
    count = values.shape[1]
    place = (lax.broadcasted_iota(jnp.int32, values.shape, 1) // inner) % period
    rolled = pltpu.roll(values, (-step * inner) % count, 1)
    inside = (place + step >= 0) & (place + step < period)
    return jnp.where(inside, rolled, 0.0)


def six_kernel(half, gathered, own, cot, next_rows, mine, theirs, cells, grads, whole):
    blank = jnp.zeros((64, 256), jnp.bfloat16)
    cells[0:64, :] = blank
    cells[1088:1152, :] = blank
    cells[64:1088, 0:128] = gathered[:, 0:64, :].reshape(1024, 128)
    cells[64:1088, 128:256] = gathered[:, 64:128, :].reshape(1024, 128)
    taps = jnp.zeros((144, 1024), jnp.float32)
    for depth_tap in range(3):
        taps += lax.dot_general(
            own[depth_tap * 9 : depth_tap * 9 + 9].reshape(144, 256),
            cells[depth_tap * 64 : depth_tap * 64 + 1024, :],
            NT,
            preferred_element_type=jnp.float32,
        )
    pre = jnp.zeros((16, 1024), jnp.float32)
    for row_tap in range(3):
        line = jnp.zeros((16, 1024), jnp.float32)
        for col_tap in range(3):
            start = (row_tap * 3 + col_tap) * 16
            line += shifted_lanes(taps[start : start + 16], col_tap - 1, 8, 1)
        pre += shifted_lanes(line, row_tap - 1, 8, 8)
    act, slant = both_of(pre)
    small = lax.broadcasted_iota(jnp.int32, (128, 1024), 0)
    cell = lax.broadcasted_iota(jnp.int32, (128, 1024), 1)
    target = (cell >> 7) * 16 + ((cell % 64) >> 4) * 4 + ((cell % 8) >> 1)
    grow = jnp.where(small == target, 1.0, 0.0).astype(jnp.bfloat16)
    upstream = jnp.dot(cot[...], grow, preferred_element_type=jnp.float32)
    high = act.astype(jnp.bfloat16)
    rest = act - high.astype(jnp.float32)
    middle = rest.astype(jnp.bfloat16)
    low = (rest - middle.astype(jnp.float32)).astype(jnp.bfloat16)
    sums = lax.dot_general(
        jnp.concatenate([high, middle, low], axis=0), grow, NT, preferred_element_type=jnp.float32
    )
    next_rows[...] = ((sums[0:16] + sums[16:32] + sums[32:48]) * 0.125).astype(jnp.bfloat16)
    grad = (upstream * slant).astype(jnp.bfloat16).astype(jnp.float32)
    for row_tap in range(3):
        line = shifted_lanes(grad, 1 - row_tap, 8, 8)
        for col_tap in range(3):
            start = (row_tap * 3 + col_tap) * 16
            moved = shifted_lanes(line, 1 - col_tap, 8, 1)
            grads[start : start + 16, :] = moved.astype(jnp.bfloat16)
    for depth_tap in range(3):
        part = jnp.dot(
            grads[...],
            cells[depth_tap * 64 : depth_tap * 64 + 1024, :],
            preferred_element_type=jnp.float32,
        )
        whole[depth_tap * 9 : depth_tap * 9 + 9] = part.astype(jnp.bfloat16).reshape(9, 16, 256)
    whole[27] = jnp.zeros((16, 256), jnp.bfloat16)
    mine[...] = whole[pl.ds(half[0] * HALF_TAPS, HALF_TAPS)]
    theirs[...] = whole[pl.ds((1 - half[0]) * HALF_TAPS, HALF_TAPS)]


def six_own(gathered, own, cot_rows, half):
    part = shape((HALF_TAPS, 16, 256), jnp.bfloat16)
    return call(
        six_kernel,
        (shape((16, 128), jnp.bfloat16), part, part),
        [
            VMEM((1152, 256), jnp.bfloat16),
            VMEM((144, 1024), jnp.bfloat16),
            VMEM((28, 16, 256), jnp.bfloat16),
        ],
        (gathered, own, cot_rows),
        (half,),
        flops=2_000_000_000,
    )


def shift_perm(axis, step):
    count = lax.axis_size(axis)
    return [(i, i + step) for i in range(count) if 0 <= i + step < count]


def core_swap(values):
    count = lax.axis_size("dp")
    return lax.ppermute(values, "dp", [(i, i ^ 1) for i in range(count)])


def sum_over_chips(values):
    count = lax.axis_size("dp")
    total = values.astype(jnp.float32)
    for step in range(1, count // 2):
        pairs = [(i, (i + 2 * step) % count) for i in range(count)]
        total = total + lax.ppermute(values, "dp", pairs).astype(jnp.float32)
    return total


def shards(volume, kernel_five, kernel_six, cotangent):
    position = lax.axis_index("wide").astype(jnp.int32).reshape(1)
    half = (lax.axis_index("dp") % 2).astype(jnp.int32).reshape(1)
    slab = volume[0]
    low = lax.ppermute(slab[-1:], "wide", shift_perm("wide", 1))
    high = lax.ppermute(slab[:1], "wide", shift_perm("wide", -1))
    cot_rows = cotangent[0].reshape(128, 16).T
    own = own_taps(kernel_six, position)
    message, slope, padded = forward_five(slab, low, high, kernel_five, cot_rows)
    gathered = lax.all_to_all(message, "wide", split_axis=0, concat_axis=0, tiled=True)
    rows, theirs_five = back_five(gathered, kernel_six, slope, padded, position, half)
    got_five = core_swap(theirs_five)
    mine_five = mine_of_five(rows, padded, half)
    pair_five = mine_five + got_five
    spread = lax.all_to_all(pair_five, "wide", split_axis=0, concat_axis=0, tiled=True)
    next_rows, mine_six, theirs_six = six_own(gathered, own, cot_rows, half)
    pair_six = mine_six + core_swap(theirs_six)
    depth_five = spread.astype(jnp.float32).sum(0).astype(jnp.bfloat16)
    both = jnp.concatenate([depth_five, pair_six], axis=-1)
    total = sum_over_chips(both).astype(jnp.bfloat16)
    other = core_swap(total)
    first = jnp.where(half == 0, total, other)
    second = jnp.where(half == 0, other, total)
    whole = jnp.concatenate([first, second], axis=0)[:27].astype(jnp.float32)
    out_five = whole[:, :, :128].transpose(0, 2, 1).reshape(3, 3, 3, 128, 16)
    out_six = whole[:, :, 128:].transpose(0, 2, 1).reshape(3, 3, 3, 256, 16)
    return (next_rows.T.reshape(1, 8, 4, 4, 16), out_five, out_six)


def solution(mesh):
    in_specs = (P("dp", "wide", None, None, None), P(), P(), P("dp", None, None, None, "wide"))
    out_specs = (
        P("dp", None, None, None, "wide"),
        P(None, None, None, None, "wide"),
        P(None, None, None, None, "wide"),
    )
    return jax.shard_map(shards, mesh=mesh, in_specs=in_specs, out_specs=out_specs, check_vma=False)
```

```python
import jax
import jax.numpy as jnp
from jax import lax
from jax.experimental import pallas as pl
from jax.experimental.pallas import tpu as pltpu
from jax.sharding import PartitionSpec as P

SLOPE = 0.3
HALF_TAPS = 14
VMEM = pltpu.VMEM
NT = (((1,), (1,)), ((), ()))


def both_of(value):
    sigma = 1.0 / (1.0 + jnp.exp(-value))
    act = value * (SLOPE + (1.0 - SLOPE) * sigma)
    slope = 0.125 * SLOPE + (0.125 * (1.0 - SLOPE)) * (sigma + value * sigma * (1.0 - sigma))
    return act, slope


def call(body, out_shape, scratch, operands, scalars=(), flops=0, limit=16, space=VMEM):
    specs = [pl.BlockSpec(memory_space=pltpu.SMEM)] * len(scalars)
    specs += [pl.BlockSpec(memory_space=space)] * len(operands)
    outs = jax.tree.map(lambda _: pl.BlockSpec(memory_space=VMEM), out_shape)
    return pl.pallas_call(
        body,
        out_shape=out_shape,
        in_specs=specs,
        out_specs=outs,
        scratch_shapes=scratch,
        compiler_params=pltpu.CompilerParams(vmem_limit_bytes=limit * 1024 * 1024),
        cost_estimate=pl.CostEstimate(flops=flops, bytes_accessed=4_000_000, transcendentals=0),
    )(*scalars, *operands)


def shape(dims, kind):
    return jax.ShapeDtypeStruct(dims, kind)


def shifted_rows(values, step, period):
    if step == 0:
        return values
    count = values.shape[0]
    column = lax.broadcasted_iota(jnp.int32, values.shape, 0) % period
    rolled = pltpu.roll(values, (-step) % count, 0)
    inside = (column + step >= 0) & (column + step < period)
    return jnp.where(inside, rolled, 0.0)


def columns_of(padded, index, source):
    values = source.astype(jnp.float32)
    padded[index, 0:16, :] = jnp.zeros((16, 384), jnp.bfloat16)
    padded[index, 272:288, :] = jnp.zeros((16, 384), jnp.bfloat16)
    padded[index, 16:272, 0:128] = shifted_rows(values, -1, 16).astype(jnp.bfloat16)
    padded[index, 16:272, 128:256] = source
    padded[index, 16:272, 256:384] = shifted_rows(values, 1, 16).astype(jnp.bfloat16)


def depth_term(padded, index, kernel, depth_tap):
    total = jnp.zeros((256, 256), jnp.float32)
    for row_tap in range(3):
        start = (depth_tap * 3 + row_tap) * 384
        total += jnp.dot(
            padded[index, 16 * row_tap : 16 * row_tap + 256, :],
            kernel[start : start + 384, :],
            preferred_element_type=jnp.float32,
        )
    return total


def inner_kernel(slab_far, kernel_far, part, padded, kernel, slab, marks):
    loads = [pltpu.make_async_copy(slab_far, slab, marks.at[3])]
    loads[0].start()
    takes = {}
    for depth_tap in (1, 2, 0):
        rows = pl.ds(depth_tap * 1152, 1152)
        takes[depth_tap] = pltpu.make_async_copy(
            kernel_far.at[rows], kernel.at[rows], marks.at[depth_tap]
        )
        takes[depth_tap].start()
    loads[0].wait()
    for plane in range(2):
        columns_of(padded, plane, slab[plane])
    takes[1].wait()
    for plane in range(2):
        part[plane * 256 : (plane + 1) * 256, :] = depth_term(padded, plane, kernel, 1)
    takes[2].wait()
    part[0:256, :] += depth_term(padded, 1, kernel, 2)
    takes[0].wait()
    part[256:512, :] += depth_term(padded, 0, kernel, 0)


def inner_five(slab, kernel):
    return call(
        inner_kernel,
        (
            shape((512, 256), jnp.float32),
            shape((2, 288, 384), jnp.bfloat16),
            shape((3456, 256), jnp.bfloat16),
        ),
        [VMEM((2, 256, 128), jnp.bfloat16), pltpu.SemaphoreType.DMA((4,))],
        (slab.reshape(2, 256, 128), kernel.reshape(3456, 256)),
        flops=600_000_000,
        space=pltpu.HBM,
    )


def outer_kernel(low, high, kernel, part, inner, cot, message, slope, padded, tall):
    columns_of(padded, 0, low[1])
    columns_of(padded, 3, high[0])
    padded[1:3] = inner[...]
    acts = []
    for plane in range(2):
        total = part[plane * 256 : (plane + 1) * 256, :]
        total += depth_term(padded, 3 * plane, kernel, 2 * plane)
        act, slant = both_of(total)
        slope[plane * 256 : (plane + 1) * 256, :] = slant
        acts.append(act)
    two = (acts[0] + acts[1]).reshape(8, 2, 16, 256)
    pairs = (two[:, 0] + two[:, 1]).reshape(128, 256)
    pooled = []
    for side in range(2):
        tall[side] = pairs[:, side * 128 : (side + 1) * 128]
        even = tall[side, pl.ds(0, 64, stride=2), :]
        odd = tall[side, pl.ds(1, 64, stride=2), :]
        pooled.append(((even + odd) * 0.125).astype(jnp.bfloat16))
    marks = cot[...]
    for target in range(16):
        message[target, 0:64, :] = pooled[0]
        message[target, 64:128, :] = pooled[1]
        message[target, 128:144, :] = marks


def outer_five(low, high, kernel, part, inner, cot_rows):
    return call(
        outer_kernel,
        (
            shape((16, 144, 128), jnp.bfloat16),
            shape((512, 256), jnp.float32),
            shape((4, 288, 384), jnp.bfloat16),
        ),
        [VMEM((2, 128, 128), jnp.float32)],
        (
            low.reshape(2, 256, 128),
            high.reshape(2, 256, 128),
            kernel,
            part,
            inner,
            cot_rows,
        ),
        flops=300_000_000,
    )


def own_taps_kernel(position, kernel, own):
    rows = lax.broadcasted_iota(jnp.int32, (16, 256), 0) + position[0] * 16
    lanes = lax.broadcasted_iota(jnp.int32, (16, 256), 1)
    pick = jnp.where(rows == lanes, 1.0, 0.0).astype(jnp.bfloat16)
    for tap in range(27):
        chosen = lax.dot_general(pick, kernel[tap], NT, preferred_element_type=jnp.float32)
        own[tap] = chosen.astype(jnp.bfloat16)


def own_taps(kernel, position):
    return call(
        own_taps_kernel,
        shape((27, 16, 256), jnp.bfloat16),
        [],
        (kernel.reshape(27, 256, 256),),
        (position,),
        flops=900_000_000,
    )


def six_to_five(position, gathered, kernel, slope, rows_out, near, tall):
    for plane in range(5):
        where = position[0] + (plane - 2)
        inside = (where >= 0) & (where < 16)
        index = jnp.clip(where, 0, 15)
        left = gathered[index, 0:64, :]
        right = gathered[index, 64:128, :]
        values = jnp.concatenate([left, right], axis=1).astype(jnp.float32)
        values = jnp.where(inside, values, 0.0)
        blank = jnp.zeros((8, 256), jnp.float32)
        for col_tap in range(3):
            moved = shifted_rows(values, col_tap - 1, 8)
            for row_tap in range(3):
                if row_tap == 0:
                    cells = jnp.concatenate([blank, moved[:56]], axis=0)
                elif row_tap == 1:
                    cells = moved
                else:
                    cells = jnp.concatenate([moved[8:], blank], axis=0)
                lane = (row_tap * 3 + col_tap) * 256
                near[plane, :, lane : lane + 256] = cells.astype(jnp.bfloat16)
    pre_six = jnp.zeros((192, 256), jnp.float32)
    for depth_tap in range(3):
        taps = kernel[depth_tap * 9 : depth_tap * 9 + 9].reshape(2304, 256)
        cells = near[depth_tap : depth_tap + 3].reshape(192, 2304)
        pre_six += jnp.dot(cells, taps, preferred_element_type=jnp.float32)
    _, slant = both_of(pre_six)
    cell = lax.broadcasted_iota(jnp.int32, (192, 128), 0)
    lanes = lax.broadcasted_iota(jnp.int32, (192, 128), 1)
    depth = cell // 64 + position[0] - 1
    small = (depth >> 1) * 16 + ((cell % 64) >> 4) * 4 + ((cell % 8) >> 1)
    hit = (small == lanes) & (depth >= 0) & (depth < 16)
    grow = jnp.where(hit, 1.0, 0.0).astype(jnp.bfloat16)
    cot = gathered[:, 128:144, :].reshape(256, 128)
    upstream = lax.dot_general(grow, cot, NT, preferred_element_type=jnp.float32)
    grad_six = (upstream * slant).astype(jnp.bfloat16).astype(jnp.float32)
    grad_pooled = jnp.zeros((64, 256), jnp.float32)
    blank = jnp.zeros((8, 256), jnp.float32)
    for depth_tap in range(3):
        values = grad_six[(2 - depth_tap) * 64 : (3 - depth_tap) * 64]
        for col_tap in range(3):
            moved = shifted_rows(values, 1 - col_tap, 8)
            for row_tap in range(3):
                if row_tap == 0:
                    cells = jnp.concatenate([moved[8:], blank], axis=0)
                elif row_tap == 1:
                    cells = moved
                else:
                    cells = jnp.concatenate([blank, moved[:56]], axis=0)
                grad_pooled += lax.dot_general(
                    cells.astype(jnp.bfloat16),
                    kernel[depth_tap * 9 + row_tap * 3 + col_tap],
                    NT,
                    preferred_element_type=jnp.float32,
                )
    for side in range(2):
        tall[side, pl.ds(0, 64, stride=2), :] = grad_pooled[:, side * 128 : (side + 1) * 128]
        tall[side, pl.ds(1, 64, stride=2), :] = grad_pooled[:, side * 128 : (side + 1) * 128]
    both = jnp.concatenate([tall[0], tall[1]], axis=1)
    wide = jnp.broadcast_to(both.reshape(8, 1, 16, 256), (8, 2, 16, 256)).reshape(256, 256)
    for plane in range(2):
        grad = wide * slope[plane * 256 : (plane + 1) * 256, :]
        rows_out[:, plane * 256 : (plane + 1) * 256] = grad.T.astype(jnp.bfloat16)


def half_of_five(first, rows, padded, out, got=None):
    for step in range(HALF_TAPS):
        tap = jnp.minimum(first + step, 26)
        depth_tap, row_tap, col_tap = tap // 9, (tap // 3) % 3, tap % 3
        total = jnp.zeros((256, 128), jnp.float32)
        for plane in range(2):
            cells = padded[
                plane + depth_tap,
                pl.ds(pl.multiple_of(row_tap * 16, 16), 256),
                pl.ds(pl.multiple_of(col_tap * 128, 128), 128),
            ]
            total += jnp.dot(
                rows[:, plane * 256 : (plane + 1) * 256],
                cells,
                preferred_element_type=jnp.float32,
            )
        if got is not None:
            total += got[:, step].reshape(256, 128).astype(jnp.float32)
        out[:, step] = total.astype(jnp.bfloat16).reshape(16, 16, 128)


def back_kernel(position, half, gathered, kernel, slope, padded, rows, theirs, near, tall):
    six_to_five(position, gathered, kernel, slope, rows, near, tall)
    half_of_five((1 - half[0]) * HALF_TAPS, rows, padded, theirs)


def back_five(gathered, kernel, slope, padded, position, half):
    return call(
        back_kernel,
        (shape((256, 512), jnp.bfloat16), shape((16, HALF_TAPS, 16, 128), jnp.bfloat16)),
        [VMEM((5, 64, 2304), jnp.bfloat16), VMEM((2, 128, 128), jnp.float32)],
        (gathered, kernel.reshape(27, 256, 256), slope, padded),
        (position, half),
        flops=3_000_000_000,
    )


def mine_kernel(half, rows, padded, got, mine):
    half_of_five(half[0] * HALF_TAPS, rows, padded, mine, got)


def mine_of_five(rows, padded, got, half):
    return call(
        mine_kernel,
        shape((16, HALF_TAPS, 16, 128), jnp.bfloat16),
        [],
        (rows, padded, got),
        (half,),
        flops=900_000_000,
    )


def shifted_lanes(values, step, period, inner):
    if step == 0:
        return values
    count = values.shape[1]
    place = (lax.broadcasted_iota(jnp.int32, values.shape, 1) // inner) % period
    rolled = pltpu.roll(values, (-step * inner) % count, 1)
    inside = (place + step >= 0) & (place + step < period)
    return jnp.where(inside, rolled, 0.0)


def six_kernel(half, gathered, own, cot, next_rows, mine, theirs, cells, grads, whole):
    blank = jnp.zeros((64, 256), jnp.bfloat16)
    cells[0:64, :] = blank
    cells[1088:1152, :] = blank
    cells[64:1088, 0:128] = gathered[:, 0:64, :].reshape(1024, 128)
    cells[64:1088, 128:256] = gathered[:, 64:128, :].reshape(1024, 128)
    taps = jnp.zeros((144, 1024), jnp.float32)
    for depth_tap in range(3):
        taps += lax.dot_general(
            own[depth_tap * 9 : depth_tap * 9 + 9].reshape(144, 256),
            cells[depth_tap * 64 : depth_tap * 64 + 1024, :],
            NT,
            preferred_element_type=jnp.float32,
        )
    pre = jnp.zeros((16, 1024), jnp.float32)
    for row_tap in range(3):
        line = jnp.zeros((16, 1024), jnp.float32)
        for col_tap in range(3):
            start = (row_tap * 3 + col_tap) * 16
            line += shifted_lanes(taps[start : start + 16], col_tap - 1, 8, 1)
        pre += shifted_lanes(line, row_tap - 1, 8, 8)
    act, slant = both_of(pre)
    small = lax.broadcasted_iota(jnp.int32, (128, 1024), 0)
    cell = lax.broadcasted_iota(jnp.int32, (128, 1024), 1)
    target = (cell >> 7) * 16 + ((cell % 64) >> 4) * 4 + ((cell % 8) >> 1)
    grow = jnp.where(small == target, 1.0, 0.0).astype(jnp.bfloat16)
    upstream = jnp.dot(cot[...], grow, preferred_element_type=jnp.float32)
    high = act.astype(jnp.bfloat16)
    rest = act - high.astype(jnp.float32)
    middle = rest.astype(jnp.bfloat16)
    low = (rest - middle.astype(jnp.float32)).astype(jnp.bfloat16)
    sums = lax.dot_general(
        jnp.concatenate([high, middle, low], axis=0), grow, NT, preferred_element_type=jnp.float32
    )
    next_rows[...] = ((sums[0:16] + sums[16:32] + sums[32:48]) * 0.125).astype(jnp.bfloat16)
    grad = (upstream * slant).astype(jnp.bfloat16).astype(jnp.float32)
    for row_tap in range(3):
        line = shifted_lanes(grad, 1 - row_tap, 8, 8)
        for col_tap in range(3):
            start = (row_tap * 3 + col_tap) * 16
            moved = shifted_lanes(line, 1 - col_tap, 8, 1)
            grads[start : start + 16, :] = moved.astype(jnp.bfloat16)
    for depth_tap in range(3):
        part = jnp.dot(
            grads[...],
            cells[depth_tap * 64 : depth_tap * 64 + 1024, :],
            preferred_element_type=jnp.float32,
        )
        whole[depth_tap * 9 : depth_tap * 9 + 9] = part.astype(jnp.bfloat16).reshape(9, 16, 256)
    whole[27] = whole[26]
    mine[...] = whole[pl.ds(half[0] * HALF_TAPS, HALF_TAPS)]
    theirs[...] = whole[pl.ds((1 - half[0]) * HALF_TAPS, HALF_TAPS)]


def six_own(gathered, own, cot_rows, half):
    part = shape((HALF_TAPS, 16, 256), jnp.bfloat16)
    return call(
        six_kernel,
        (shape((16, 128), jnp.bfloat16), part, part),
        [
            VMEM((1152, 256), jnp.bfloat16),
            VMEM((144, 1024), jnp.bfloat16),
            VMEM((28, 16, 256), jnp.bfloat16),
        ],
        (gathered, own, cot_rows),
        (half,),
        flops=2_000_000_000,
    )


def halves_kernel(half, mine_five, other_five, mine_six, other_six, five, six):
    for step in range(HALF_TAPS):
        for first, part_five, part_six in (
            (half[0] * HALF_TAPS, mine_five, mine_six),
            ((1 - half[0]) * HALF_TAPS, other_five, other_six),
        ):
            tap = jnp.minimum(first + step, 26)
            five[tap] = part_five[step].astype(jnp.float32)
            six[tap] = part_six[step].astype(jnp.float32)


def both_halves(half, mine_five, other_five, mine_six, other_six):
    return call(
        halves_kernel,
        (shape((27, 16, 128), jnp.float32), shape((27, 16, 256), jnp.float32)),
        [],
        (mine_five, other_five, mine_six, other_six),
        (half,),
    )


def shift_perm(axis, step):
    count = lax.axis_size(axis)
    return [(i, i + step) for i in range(count) if 0 <= i + step < count]


def core_swap(values):
    count = lax.axis_size("dp")
    return lax.ppermute(values, "dp", [(i, i ^ 1) for i in range(count)])


def from_chips(values):
    count = lax.axis_size("dp")
    got = []
    for step in range(1, count // 2):
        pairs = [(i, (i + 2 * step) % count) for i in range(count)]
        got.append(lax.ppermute(values, "dp", pairs))
    return got


def total_of(values, others):
    total = values.astype(jnp.float32)
    for other in others:
        total = total + other.astype(jnp.float32)
    return total


def exchange(values):
    return lax.all_to_all(values, "wide", split_axis=0, concat_axis=0, tiled=True)


def shards(volume, kernel_five, kernel_six, cotangent):
    position = lax.axis_index("wide").astype(jnp.int32).reshape(1)
    half = (lax.axis_index("dp") % 2).astype(jnp.int32).reshape(1)
    low = lax.ppermute(volume, "wide", shift_perm("wide", 1))
    high = lax.ppermute(volume, "wide", shift_perm("wide", -1))
    cot_rows = cotangent[0].reshape(128, 16).T
    part, inner, near_kernel = inner_five(volume, kernel_five)
    message, slope, padded = outer_five(low, high, near_kernel, part, inner, cot_rows)
    message, position, half, slope, padded = lax.optimization_barrier(
        (message, position, half, slope, padded)
    )
    gathered = exchange(message)
    gathered, position, half, slope, padded = lax.optimization_barrier(
        (gathered, position, half, slope, padded)
    )
    rows, theirs_five = back_five(gathered, kernel_six, slope, padded, position, half)
    got_five = core_swap(theirs_five)
    own = own_taps(kernel_six, position)
    next_rows, mine_six, theirs_six = six_own(gathered, own, cot_rows, half)
    got_six = core_swap(theirs_six)
    pair_five = mine_of_five(rows, padded, got_five, half)
    pair_six = total_of(mine_six, [got_six]).astype(jnp.bfloat16)
    chips_six = from_chips(pair_six)
    pair_five, pair_six, next_rows = lax.optimization_barrier((pair_five, pair_six, next_rows))
    spread = exchange(pair_five)
    spread, chips_six = lax.optimization_barrier((spread, chips_six))
    depth_five = spread.astype(jnp.float32).sum(0).astype(jnp.bfloat16)
    total_six = total_of(pair_six, chips_six).astype(jnp.bfloat16)
    total_five = total_of(depth_five, from_chips(depth_five)).astype(jnp.bfloat16)
    other_five, other_six = core_swap(total_five), core_swap(total_six)
    out_five, out_six = both_halves(half, total_five, other_five, total_six, other_six)
    out_five = out_five.transpose(0, 2, 1).reshape(3, 3, 3, 128, 16)
    out_six = out_six.transpose(0, 2, 1).reshape(3, 3, 3, 256, 16)
    return (next_rows.T.reshape(1, 8, 4, 4, 16), out_five, out_six)


def solution(mesh):
    in_specs = (P("dp", "wide", None, None, None), P(), P(), P("dp", None, None, None, "wide"))
    out_specs = (
        P("dp", None, None, None, "wide"),
        P(None, None, None, None, "wide"),
        P(None, None, None, None, "wide"),
    )
    return jax.shard_map(shards, mesh=mesh, in_specs=in_specs, out_specs=out_specs, check_vma=False)
```

```python
import jax
import jax.numpy as jnp
from jax import lax
from jax.experimental import pallas as pl
from jax.experimental.pallas import tpu as pltpu
from jax.sharding import PartitionSpec as P

SLOPE = 0.3
HALF_TAPS = 14
VMEM = pltpu.VMEM
NT = (((1,), (1,)), ((), ()))


def both_of(value):
    sigma = 1.0 / (1.0 + jnp.exp(-value))
    act = value * (SLOPE + (1.0 - SLOPE) * sigma)
    slope = 0.125 * SLOPE + (0.125 * (1.0 - SLOPE)) * (sigma + value * sigma * (1.0 - sigma))
    return act, slope


def call(body, out_shape, scratch, operands, scalars=(), flops=0, limit=16, far=()):
    specs = [pl.BlockSpec(memory_space=pltpu.SMEM)] * len(scalars)
    specs += [
        pl.BlockSpec(memory_space=pltpu.HBM if index in far else VMEM)
        for index in range(len(operands))
    ]
    outs = jax.tree.map(lambda _: pl.BlockSpec(memory_space=VMEM), out_shape)
    return pl.pallas_call(
        body,
        out_shape=out_shape,
        in_specs=specs,
        out_specs=outs,
        scratch_shapes=scratch,
        compiler_params=pltpu.CompilerParams(vmem_limit_bytes=int(limit * 1024 * 1024)),
        cost_estimate=pl.CostEstimate(flops=flops, bytes_accessed=4_000_000, transcendentals=0),
    )(*scalars, *operands)


def shape(dims, kind):
    return jax.ShapeDtypeStruct(dims, kind)


def shifted_rows(values, step, period):
    if step == 0:
        return values
    count = values.shape[0]
    column = lax.broadcasted_iota(jnp.int32, values.shape, 0) % period
    rolled = pltpu.roll(values, (-step) % count, 0)
    inside = (column + step >= 0) & (column + step < period)
    return jnp.where(inside, rolled, 0.0)


def columns_of(padded, index, source):
    values = source.astype(jnp.float32)
    padded[index, 0:16, :] = jnp.zeros((16, 384), jnp.bfloat16)
    padded[index, 272:288, :] = jnp.zeros((16, 384), jnp.bfloat16)
    padded[index, 16:272, 0:128] = shifted_rows(values, -1, 16).astype(jnp.bfloat16)
    padded[index, 16:272, 128:256] = source
    padded[index, 16:272, 256:384] = shifted_rows(values, 1, 16).astype(jnp.bfloat16)


def depth_term(padded, index, kernel, depth_tap):
    total = jnp.zeros((256, 256), jnp.float32)
    for row_tap in range(3):
        start = (depth_tap * 3 + row_tap) * 384
        total += jnp.dot(
            padded[index, 16 * row_tap : 16 * row_tap + 256, :],
            kernel[start : start + 384, :],
            preferred_element_type=jnp.float32,
        )
    return total


def inner_kernel(slab, kernel_far, part, padded, kernel, marks):
    loads = {}
    for depth_tap in (1, 2, 0):
        rows = pl.ds(depth_tap * 1152, 1152)
        loads[depth_tap] = pltpu.make_async_copy(
            kernel_far.at[rows], kernel.at[rows], marks.at[depth_tap]
        )
        loads[depth_tap].start()
    for plane in range(2):
        columns_of(padded, plane, slab[plane])
    loads[1].wait()
    for plane in range(2):
        part[plane * 256 : (plane + 1) * 256, :] = depth_term(padded, plane, kernel, 1)
    loads[2].wait()
    part[0:256, :] += depth_term(padded, 1, kernel, 2)
    loads[0].wait()
    part[256:512, :] += depth_term(padded, 0, kernel, 0)


def inner_five(slab, kernel):
    return call(
        inner_kernel,
        (
            shape((512, 256), jnp.float32),
            shape((2, 288, 384), jnp.bfloat16),
            shape((3456, 256), jnp.bfloat16),
        ),
        [pltpu.SemaphoreType.DMA((3,))],
        (slab.reshape(2, 256, 128), kernel.reshape(3456, 256)),
        flops=600_000_000,
        limit=51,
        far=(1,),
    )


def outer_kernel(position, low, high, kernel, part, inner, cot, message, slope, padded, tall):
    columns_of(padded, 0, jnp.where(position[0] == 0, jnp.zeros((256, 128), jnp.bfloat16), low[1]))
    columns_of(padded, 3, jnp.where(position[0] == 15, jnp.zeros((256, 128), jnp.bfloat16), high[0]))
    padded[1:3] = inner[...]
    acts = []
    for plane in range(2):
        total = part[plane * 256 : (plane + 1) * 256, :]
        total += depth_term(padded, 3 * plane, kernel, 2 * plane)
        act, slant = both_of(total)
        slope[plane * 256 : (plane + 1) * 256, :] = slant
        acts.append(act)
    two = (acts[0] + acts[1]).reshape(8, 2, 16, 256)
    pairs = (two[:, 0] + two[:, 1]).reshape(128, 256)
    pooled = []
    for side in range(2):
        tall[side] = pairs[:, side * 128 : (side + 1) * 128]
        even = tall[side, pl.ds(0, 64, stride=2), :]
        odd = tall[side, pl.ds(1, 64, stride=2), :]
        pooled.append(((even + odd) * 0.125).astype(jnp.bfloat16))
    marks = cot[...]
    for target in range(16):
        message[target, 0:64, :] = pooled[0]
        message[target, 64:128, :] = pooled[1]
        message[target, 128:144, :] = marks


def outer_five(low, high, kernel, part, inner, cot_rows, position):
    return call(
        outer_kernel,
        (
            shape((16, 144, 128), jnp.bfloat16),
            shape((512, 256), jnp.float32),
            shape((4, 288, 384), jnp.bfloat16),
        ),
        [VMEM((2, 128, 128), jnp.float32)],
        (
            low.reshape(2, 256, 128),
            high.reshape(2, 256, 128),
            kernel,
            part,
            inner,
            cot_rows,
        ),
        (position,),
        flops=300_000_000,
    )


def six_to_five(position, gathered, kernel, slope, rows_out, near, tall):
    for plane in range(5):
        where = position[0] + (plane - 2)
        inside = (where >= 0) & (where < 16)
        index = jnp.clip(where, 0, 15)
        left = gathered[index, 0:64, :]
        right = gathered[index, 64:128, :]
        values = jnp.concatenate([left, right], axis=1).astype(jnp.float32)
        values = jnp.where(inside, values, 0.0)
        blank = jnp.zeros((8, 256), jnp.float32)
        for col_tap in range(3):
            moved = shifted_rows(values, col_tap - 1, 8)
            for row_tap in range(3):
                if row_tap == 0:
                    cells = jnp.concatenate([blank, moved[:56]], axis=0)
                elif row_tap == 1:
                    cells = moved
                else:
                    cells = jnp.concatenate([moved[8:], blank], axis=0)
                lane = (row_tap * 3 + col_tap) * 256
                near[plane, :, lane : lane + 256] = cells.astype(jnp.bfloat16)
    pre_six = jnp.zeros((192, 256), jnp.float32)
    for depth_tap in range(3):
        taps = kernel[depth_tap * 9 : depth_tap * 9 + 9].reshape(2304, 256)
        cells = near[depth_tap : depth_tap + 3].reshape(192, 2304)
        pre_six += jnp.dot(cells, taps, preferred_element_type=jnp.float32)
    _, slant = both_of(pre_six)
    cell = lax.broadcasted_iota(jnp.int32, (192, 128), 0)
    lanes = lax.broadcasted_iota(jnp.int32, (192, 128), 1)
    depth = cell // 64 + position[0] - 1
    small = (depth >> 1) * 16 + ((cell % 64) >> 4) * 4 + ((cell % 8) >> 1)
    hit = (small == lanes) & (depth >= 0) & (depth < 16)
    grow = jnp.where(hit, 1.0, 0.0).astype(jnp.bfloat16)
    cot = gathered[:, 128:144, :].reshape(256, 128)
    upstream = lax.dot_general(grow, cot, NT, preferred_element_type=jnp.float32)
    grad_six = (upstream * slant).astype(jnp.bfloat16).astype(jnp.float32)
    grad_pooled = jnp.zeros((64, 256), jnp.float32)
    blank = jnp.zeros((8, 256), jnp.float32)
    for depth_tap in range(3):
        values = grad_six[(2 - depth_tap) * 64 : (3 - depth_tap) * 64]
        for col_tap in range(3):
            moved = shifted_rows(values, 1 - col_tap, 8)
            for row_tap in range(3):
                if row_tap == 0:
                    cells = jnp.concatenate([moved[8:], blank], axis=0)
                elif row_tap == 1:
                    cells = moved
                else:
                    cells = jnp.concatenate([blank, moved[:56]], axis=0)
                grad_pooled += lax.dot_general(
                    cells.astype(jnp.bfloat16),
                    kernel[depth_tap * 9 + row_tap * 3 + col_tap],
                    NT,
                    preferred_element_type=jnp.float32,
                )
    for side in range(2):
        tall[side, pl.ds(0, 64, stride=2), :] = grad_pooled[:, side * 128 : (side + 1) * 128]
        tall[side, pl.ds(1, 64, stride=2), :] = grad_pooled[:, side * 128 : (side + 1) * 128]
    both = jnp.concatenate([tall[0], tall[1]], axis=1)
    wide = jnp.broadcast_to(both.reshape(8, 1, 16, 256), (8, 2, 16, 256)).reshape(256, 256)
    for plane in range(2):
        grad = wide * slope[plane * 256 : (plane + 1) * 256, :]
        rows_out[:, plane * 256 : (plane + 1) * 256] = grad.T.astype(jnp.bfloat16)


def half_of_five(first, rows, padded, out, got=None):
    for step in range(HALF_TAPS):
        tap = jnp.minimum(first + step, 26)
        depth_tap, row_tap, col_tap = tap // 9, (tap // 3) % 3, tap % 3
        total = jnp.zeros((256, 128), jnp.float32)
        for plane in range(2):
            cells = padded[
                plane + depth_tap,
                pl.ds(pl.multiple_of(row_tap * 16, 16), 256),
                pl.ds(pl.multiple_of(col_tap * 128, 128), 128),
            ]
            total += jnp.dot(
                rows[:, plane * 256 : (plane + 1) * 256],
                cells,
                preferred_element_type=jnp.float32,
            )
        if got is not None:
            total += got[:, step].reshape(256, 128).astype(jnp.float32)
        out[:, step] = total.astype(jnp.bfloat16).reshape(16, 16, 128)


def back_kernel(position, half, gathered, kernel, slope, padded, rows, theirs, near, tall):
    six_to_five(position, gathered, kernel, slope, rows, near, tall)
    half_of_five((1 - half[0]) * HALF_TAPS, rows, padded, theirs)


def back_five(gathered, kernel, slope, padded, position, half):
    return call(
        back_kernel,
        (shape((256, 512), jnp.bfloat16), shape((16, HALF_TAPS, 16, 128), jnp.bfloat16)),
        [VMEM((5, 64, 2304), jnp.bfloat16), VMEM((2, 128, 128), jnp.float32)],
        (gathered, kernel.reshape(27, 256, 256), slope, padded),
        (position, half),
        flops=3_000_000_000,
    )


def mine_kernel(half, rows, padded, got, mine):
    half_of_five(half[0] * HALF_TAPS, rows, padded, mine, got)


def mine_of_five(rows, padded, got, half):
    return call(
        mine_kernel,
        shape((16, HALF_TAPS, 16, 128), jnp.bfloat16),
        [],
        (rows, padded, got),
        (half,),
        flops=900_000_000,
    )


def shifted_lanes(values, step, period, inner):
    if step == 0:
        return values
    count = values.shape[1]
    place = (lax.broadcasted_iota(jnp.int32, values.shape, 1) // inner) % period
    rolled = pltpu.roll(values, (-step * inner) % count, 1)
    inside = (place + step >= 0) & (place + step < period)
    return jnp.where(inside, rolled, 0.0)


def six_kernel(
    position, half, gathered, kernel, cot, next_rows, mine, theirs, own, cells, grads, whole
):
    rows = lax.broadcasted_iota(jnp.int32, (16, 256), 0) + position[0] * 16
    lanes = lax.broadcasted_iota(jnp.int32, (16, 256), 1)
    pick = jnp.where(rows == lanes, 1.0, 0.0).astype(jnp.bfloat16)
    for tap in range(27):
        chosen = lax.dot_general(pick, kernel[tap], NT, preferred_element_type=jnp.float32)
        own[tap] = chosen.astype(jnp.bfloat16)
    blank = jnp.zeros((64, 256), jnp.bfloat16)
    cells[0:64, :] = blank
    cells[1088:1152, :] = blank
    cells[64:1088, 0:128] = gathered[:, 0:64, :].reshape(1024, 128)
    cells[64:1088, 128:256] = gathered[:, 64:128, :].reshape(1024, 128)
    taps = jnp.zeros((144, 1024), jnp.float32)
    for depth_tap in range(3):
        taps += lax.dot_general(
            own[depth_tap * 9 : depth_tap * 9 + 9].reshape(144, 256),
            cells[depth_tap * 64 : depth_tap * 64 + 1024, :],
            NT,
            preferred_element_type=jnp.float32,
        )
    pre = jnp.zeros((16, 1024), jnp.float32)
    for row_tap in range(3):
        line = jnp.zeros((16, 1024), jnp.float32)
        for col_tap in range(3):
            start = (row_tap * 3 + col_tap) * 16
            line += shifted_lanes(taps[start : start + 16], col_tap - 1, 8, 1)
        pre += shifted_lanes(line, row_tap - 1, 8, 8)
    act, slant = both_of(pre)
    small = lax.broadcasted_iota(jnp.int32, (128, 1024), 0)
    cell = lax.broadcasted_iota(jnp.int32, (128, 1024), 1)
    target = (cell >> 7) * 16 + ((cell % 64) >> 4) * 4 + ((cell % 8) >> 1)
    grow = jnp.where(small == target, 1.0, 0.0).astype(jnp.bfloat16)
    upstream = jnp.dot(cot[...], grow, preferred_element_type=jnp.float32)
    high = act.astype(jnp.bfloat16)
    rest = act - high.astype(jnp.float32)
    middle = rest.astype(jnp.bfloat16)
    low = (rest - middle.astype(jnp.float32)).astype(jnp.bfloat16)
    sums = lax.dot_general(
        jnp.concatenate([high, middle, low], axis=0), grow, NT, preferred_element_type=jnp.float32
    )
    next_rows[...] = ((sums[0:16] + sums[16:32] + sums[32:48]) * 0.125).astype(jnp.bfloat16)
    grad = (upstream * slant).astype(jnp.bfloat16).astype(jnp.float32)
    for row_tap in range(3):
        line = shifted_lanes(grad, 1 - row_tap, 8, 8)
        for col_tap in range(3):
            start = (row_tap * 3 + col_tap) * 16
            moved = shifted_lanes(line, 1 - col_tap, 8, 1)
            grads[start : start + 16, :] = moved.astype(jnp.bfloat16)
    for depth_tap in range(3):
        part = jnp.dot(
            grads[...],
            cells[depth_tap * 64 : depth_tap * 64 + 1024, :],
            preferred_element_type=jnp.float32,
        )
        whole[depth_tap * 9 : depth_tap * 9 + 9] = part.astype(jnp.bfloat16).reshape(9, 16, 256)
    whole[27] = whole[26]
    mine[...] = whole[pl.ds(half[0] * HALF_TAPS, HALF_TAPS)]
    theirs[...] = whole[pl.ds((1 - half[0]) * HALF_TAPS, HALF_TAPS)]


def six_own(gathered, kernel, cot_rows, position, half):
    part = shape((HALF_TAPS, 16, 256), jnp.bfloat16)
    return call(
        six_kernel,
        (shape((16, 128), jnp.bfloat16), part, part),
        [
            VMEM((27, 16, 256), jnp.bfloat16),
            VMEM((1152, 256), jnp.bfloat16),
            VMEM((144, 1024), jnp.bfloat16),
            VMEM((28, 16, 256), jnp.bfloat16),
        ],
        (gathered, kernel.reshape(27, 256, 256), cot_rows),
        (position, half),
        flops=2_000_000_000,
    )


def halves_kernel(half, mine_five, other_five, mine_six, other_six, five, six):
    for step in range(HALF_TAPS):
        for first, part_five, part_six in (
            (half[0] * HALF_TAPS, mine_five, mine_six),
            ((1 - half[0]) * HALF_TAPS, other_five, other_six),
        ):
            tap = jnp.minimum(first + step, 26)
            five[tap] = part_five[step].astype(jnp.float32)
            six[tap] = part_six[step].astype(jnp.float32)


def both_halves(half, mine_five, other_five, mine_six, other_six):
    return call(
        halves_kernel,
        (shape((27, 16, 128), jnp.float32), shape((27, 16, 256), jnp.float32)),
        [],
        (mine_five, other_five, mine_six, other_six),
        (half,),
    )


def ring_perm(axis, step):
    count = lax.axis_size(axis)
    return [(i, (i + step) % count) for i in range(count)]


def core_swap(values):
    count = lax.axis_size("dp")
    return lax.ppermute(values, "dp", [(i, i ^ 1) for i in range(count)])


def from_chips(values):
    count = lax.axis_size("dp")
    got = []
    for step in range(1, count // 2):
        pairs = [(i, (i + 2 * step) % count) for i in range(count)]
        got.append(lax.ppermute(values, "dp", pairs))
    return got


def total_of(values, others):
    total = values.astype(jnp.float32)
    for other in others:
        total = total + other.astype(jnp.float32)
    return total


def exchange(values):
    flat = values.reshape(values.shape[0], -1, values.shape[-1])
    got = lax.all_to_all(flat, "wide", split_axis=0, concat_axis=0, tiled=True)
    return got.reshape(values.shape)


def shards(volume, kernel_five, kernel_six, cotangent):
    position = lax.axis_index("wide").astype(jnp.int32).reshape(1)
    half = (lax.axis_index("dp") % 2).astype(jnp.int32).reshape(1)
    low = lax.ppermute(volume, "wide", ring_perm("wide", 1))
    high = lax.ppermute(volume, "wide", ring_perm("wide", -1))
    cot_rows = cotangent[0].reshape(128, 16).T
    part, inner, near_kernel = inner_five(volume, kernel_five)
    message, slope, padded = outer_five(low, high, near_kernel, part, inner, cot_rows, position)
    message, position, half, slope, padded = lax.optimization_barrier(
        (message, position, half, slope, padded)
    )
    gathered = exchange(message)
    gathered, position, half, slope, padded = lax.optimization_barrier(
        (gathered, position, half, slope, padded)
    )
    rows, theirs_five = back_five(gathered, kernel_six, slope, padded, position, half)
    got_five = core_swap(theirs_five)
    next_rows, mine_six, theirs_six = six_own(gathered, kernel_six, cot_rows, position, half)
    got_six = core_swap(theirs_six)
    pair_five = mine_of_five(rows, padded, got_five, half)
    pair_five, got_six, mine_six, next_rows = lax.optimization_barrier(
        (pair_five, got_six, mine_six, next_rows)
    )
    pair_six = total_of(mine_six, [got_six]).astype(jnp.bfloat16)
    chips_six = from_chips(pair_six)
    spread = exchange(pair_five)
    spread, chips_six = lax.optimization_barrier((spread, chips_six))
    depth_five = spread.astype(jnp.float32).sum(0).astype(jnp.bfloat16)
    total_six = total_of(pair_six, chips_six).astype(jnp.bfloat16)
    total_five = total_of(depth_five, from_chips(depth_five)).astype(jnp.bfloat16)
    other_five, other_six = core_swap(total_five), core_swap(total_six)
    out_five, out_six = both_halves(half, total_five, other_five, total_six, other_six)
    out_five = out_five.transpose(0, 2, 1).reshape(3, 3, 3, 128, 16)
    out_six = out_six.transpose(0, 2, 1).reshape(3, 3, 3, 256, 16)
    return (next_rows.T.reshape(1, 8, 4, 4, 16), out_five, out_six)


def solution(mesh):
    in_specs = (P("dp", "wide", None, None, None), P(), P(), P("dp", None, None, None, "wide"))
    out_specs = (
        P("dp", None, None, None, "wide"),
        P(None, None, None, None, "wide"),
        P(None, None, None, None, "wide"),
    )
    return jax.shard_map(shards, mesh=mesh, in_specs=in_specs, out_specs=out_specs, check_vma=False)
```

```python
import jax
import jax.numpy as jnp
from jax import lax
from jax.experimental import pallas as pl
from jax.experimental.pallas import tpu as pltpu
from jax.sharding import PartitionSpec as P

SLOPE = 0.3
HALF_TAPS = 14
VMEM = pltpu.VMEM
NT = (((1,), (1,)), ((), ()))


def both_of(value):
    sigma = 1.0 / (1.0 + jnp.exp(-value))
    act = value * (SLOPE + (1.0 - SLOPE) * sigma)
    slope = 0.125 * SLOPE + (0.125 * (1.0 - SLOPE)) * (sigma + value * sigma * (1.0 - sigma))
    return act, slope


def call(body, out_shape, scratch, operands, scalars=(), flops=0, limit=16, far=()):
    specs = [pl.BlockSpec(memory_space=pltpu.SMEM)] * len(scalars)
    specs += [
        pl.BlockSpec(memory_space=pltpu.HBM if index in far else VMEM)
        for index in range(len(operands))
    ]
    outs = jax.tree.map(lambda _: pl.BlockSpec(memory_space=VMEM), out_shape)
    return pl.pallas_call(
        body,
        out_shape=out_shape,
        in_specs=specs,
        out_specs=outs,
        scratch_shapes=scratch,
        compiler_params=pltpu.CompilerParams(vmem_limit_bytes=int(limit * 1024 * 1024)),
        cost_estimate=pl.CostEstimate(flops=flops, bytes_accessed=4_000_000, transcendentals=0),
    )(*scalars, *operands)


def shape(dims, kind):
    return jax.ShapeDtypeStruct(dims, kind)


def shifted_rows(values, step, period):
    if step == 0:
        return values
    count = values.shape[0]
    column = lax.broadcasted_iota(jnp.int32, values.shape, 0) % period
    rolled = pltpu.roll(values, (-step) % count, 0)
    inside = (column + step >= 0) & (column + step < period)
    return jnp.where(inside, rolled, 0.0)


def columns_of(padded, index, source):
    values = source.astype(jnp.float32)
    padded[index, 0:16, :] = jnp.zeros((16, 384), jnp.bfloat16)
    padded[index, 272:288, :] = jnp.zeros((16, 384), jnp.bfloat16)
    padded[index, 16:272, 0:128] = shifted_rows(values, -1, 16).astype(jnp.bfloat16)
    padded[index, 16:272, 128:256] = source
    padded[index, 16:272, 256:384] = shifted_rows(values, 1, 16).astype(jnp.bfloat16)


def depth_term(padded, index, kernel, depth_tap):
    total = jnp.zeros((256, 256), jnp.float32)
    for row_tap in range(3):
        start = (depth_tap * 3 + row_tap) * 384
        total += jnp.dot(
            padded[index, 16 * row_tap : 16 * row_tap + 256, :],
            kernel[start : start + 384, :],
            preferred_element_type=jnp.float32,
        )
    return total


def inner_kernel(slab, kernel_far, part, padded, kernel, marks):
    loads = {}
    for depth_tap in (1, 2, 0):
        rows = pl.ds(depth_tap * 1152, 1152)
        loads[depth_tap] = pltpu.make_async_copy(
            kernel_far.at[rows], kernel.at[rows], marks.at[depth_tap]
        )
        loads[depth_tap].start()
    for plane in range(2):
        columns_of(padded, plane, slab[plane])
    loads[1].wait()
    for plane in range(2):
        part[plane * 256 : (plane + 1) * 256, :] = depth_term(padded, plane, kernel, 1)
    loads[2].wait()
    part[0:256, :] += depth_term(padded, 1, kernel, 2)
    loads[0].wait()
    part[256:512, :] += depth_term(padded, 0, kernel, 0)


def inner_five(slab, kernel):
    return call(
        inner_kernel,
        (
            shape((512, 256), jnp.float32),
            shape((2, 288, 384), jnp.bfloat16),
            shape((3456, 256), jnp.bfloat16),
        ),
        [pltpu.SemaphoreType.DMA((3,))],
        (slab.reshape(2, 256, 128), kernel.reshape(3456, 256)),
        flops=600_000_000,
        limit=51,
        far=(1,),
    )


def outer_kernel(position, low, high, kernel, part, inner, cot, message, slope, padded, tall):
    columns_of(padded, 0, jnp.where(position[0] == 0, jnp.zeros((256, 128), jnp.bfloat16), low[1]))
    columns_of(padded, 3, jnp.where(position[0] == 15, jnp.zeros((256, 128), jnp.bfloat16), high[0]))
    padded[1:3] = inner[...]
    acts = []
    for plane in range(2):
        total = part[plane * 256 : (plane + 1) * 256, :]
        total += depth_term(padded, 3 * plane, kernel, 2 * plane)
        act, slant = both_of(total)
        slope[plane * 256 : (plane + 1) * 256, :] = slant
        acts.append(act)
    two = (acts[0] + acts[1]).reshape(8, 2, 16, 256)
    pairs = (two[:, 0] + two[:, 1]).reshape(128, 256)
    pooled = []
    for side in range(2):
        tall[side] = pairs[:, side * 128 : (side + 1) * 128]
        even = tall[side, pl.ds(0, 64, stride=2), :]
        odd = tall[side, pl.ds(1, 64, stride=2), :]
        pooled.append(((even + odd) * 0.125).astype(jnp.bfloat16))
    marks = cot[...]
    for target in range(16):
        message[target, 0:64, :] = pooled[0]
        message[target, 64:128, :] = pooled[1]
        message[target, 128:144, :] = marks


def outer_five(low, high, kernel, part, inner, cot_rows, position):
    return call(
        outer_kernel,
        (
            shape((16, 144, 128), jnp.bfloat16),
            shape((512, 256), jnp.float32),
            shape((4, 288, 384), jnp.bfloat16),
        ),
        [VMEM((2, 128, 128), jnp.float32)],
        (
            low.reshape(2, 256, 128),
            high.reshape(2, 256, 128),
            kernel,
            part,
            inner,
            cot_rows,
        ),
        (position,),
        flops=300_000_000,
    )


def six_to_five(position, gathered, kernel, slope, rows_out, near, tall):
    for plane in range(5):
        where = position[0] + (plane - 2)
        inside = (where >= 0) & (where < 16)
        index = jnp.clip(where, 0, 15)
        left = gathered[index, 0:64, :]
        right = gathered[index, 64:128, :]
        values = jnp.concatenate([left, right], axis=1).astype(jnp.float32)
        values = jnp.where(inside, values, 0.0)
        blank = jnp.zeros((8, 256), jnp.float32)
        for col_tap in range(3):
            moved = shifted_rows(values, col_tap - 1, 8)
            for row_tap in range(3):
                if row_tap == 0:
                    cells = jnp.concatenate([blank, moved[:56]], axis=0)
                elif row_tap == 1:
                    cells = moved
                else:
                    cells = jnp.concatenate([moved[8:], blank], axis=0)
                lane = (row_tap * 3 + col_tap) * 256
                near[plane, :, lane : lane + 256] = cells.astype(jnp.bfloat16)
    pre_six = jnp.zeros((192, 256), jnp.float32)
    for depth_tap in range(3):
        taps = kernel[depth_tap * 9 : depth_tap * 9 + 9].reshape(2304, 256)
        cells = near[depth_tap : depth_tap + 3].reshape(192, 2304)
        pre_six += jnp.dot(cells, taps, preferred_element_type=jnp.float32)
    _, slant = both_of(pre_six)
    cell = lax.broadcasted_iota(jnp.int32, (192, 128), 0)
    lanes = lax.broadcasted_iota(jnp.int32, (192, 128), 1)
    depth = cell // 64 + position[0] - 1
    small = (depth >> 1) * 16 + ((cell % 64) >> 4) * 4 + ((cell % 8) >> 1)
    hit = (small == lanes) & (depth >= 0) & (depth < 16)
    grow = jnp.where(hit, 1.0, 0.0).astype(jnp.bfloat16)
    cot = gathered[:, 128:144, :].reshape(256, 128)
    upstream = lax.dot_general(grow, cot, NT, preferred_element_type=jnp.float32)
    grad_six = (upstream * slant).astype(jnp.bfloat16).astype(jnp.float32)
    blank = jnp.zeros((8, 256), jnp.float32)
    for depth_tap in range(3):
        values = grad_six[(2 - depth_tap) * 64 : (3 - depth_tap) * 64]
        for col_tap in range(3):
            moved = shifted_rows(values, 1 - col_tap, 8)
            for row_tap in range(3):
                if row_tap == 0:
                    cells = jnp.concatenate([moved[8:], blank], axis=0)
                elif row_tap == 1:
                    cells = moved
                else:
                    cells = jnp.concatenate([blank, moved[:56]], axis=0)
                lane = (row_tap * 3 + col_tap) * 256
                near[depth_tap, :, lane : lane + 256] = cells.astype(jnp.bfloat16)

    def depth_of(depth_tap, total):
        for tap in range(9):
            total += lax.dot_general(
                near[depth_tap, :, tap * 256 : tap * 256 + 256],
                kernel[depth_tap * 9 + tap],
                NT,
                preferred_element_type=jnp.float32,
            )
        return total

    grad_pooled = lax.fori_loop(0, 3, depth_of, jnp.zeros((64, 256), jnp.float32))
    for side in range(2):
        tall[side, pl.ds(0, 64, stride=2), :] = grad_pooled[:, side * 128 : (side + 1) * 128]
        tall[side, pl.ds(1, 64, stride=2), :] = grad_pooled[:, side * 128 : (side + 1) * 128]
    both = jnp.concatenate([tall[0], tall[1]], axis=1)
    wide = jnp.broadcast_to(both.reshape(8, 1, 16, 256), (8, 2, 16, 256)).reshape(256, 256)
    for plane in range(2):
        grad = wide * slope[plane * 256 : (plane + 1) * 256, :]
        rows_out[:, plane * 256 : (plane + 1) * 256] = grad.T.astype(jnp.bfloat16)


def tap_cells(padded, plane, tap):
    depth_tap, row_tap, col_tap = tap // 9, (tap // 3) % 3, tap % 3
    return padded[
        plane + depth_tap,
        pl.ds(pl.multiple_of(row_tap * 16, 16), 256),
        pl.ds(pl.multiple_of(col_tap * 128, 128), 128),
    ]


def half_of_five(first, rows, padded, out, got=None):
    for step in range(0, HALF_TAPS, 2):
        taps = [jnp.minimum(first + step + other, 26) for other in range(2)]
        total = jnp.zeros((256, 256), jnp.float32)
        for plane in range(2):
            cells = jnp.concatenate([tap_cells(padded, plane, tap) for tap in taps], axis=1)
            total += jnp.dot(
                rows[:, plane * 256 : (plane + 1) * 256],
                cells,
                preferred_element_type=jnp.float32,
            )
        for other in range(2):
            part = total[:, other * 128 : (other + 1) * 128]
            if got is not None:
                part += got[:, step + other].reshape(256, 128).astype(jnp.float32)
            out[:, step + other] = part.astype(jnp.bfloat16).reshape(16, 16, 128)


def back_kernel(position, half, gathered, kernel, slope, padded, rows, theirs, near, tall):
    six_to_five(position, gathered, kernel, slope, rows, near, tall)
    half_of_five((1 - half[0]) * HALF_TAPS, rows, padded, theirs)


def back_five(gathered, kernel, slope, padded, position, half):
    return call(
        back_kernel,
        (shape((256, 512), jnp.bfloat16), shape((16, HALF_TAPS, 16, 128), jnp.bfloat16)),
        [VMEM((5, 64, 2304), jnp.bfloat16), VMEM((2, 128, 128), jnp.float32)],
        (gathered, kernel.reshape(27, 256, 256), slope, padded),
        (position, half),
        flops=3_000_000_000,
    )


def mine_kernel(half, rows, padded, got, mine):
    half_of_five(half[0] * HALF_TAPS, rows, padded, mine, got)


def mine_of_five(rows, padded, got, half):
    return call(
        mine_kernel,
        shape((16, HALF_TAPS, 16, 128), jnp.bfloat16),
        [],
        (rows, padded, got),
        (half,),
        flops=900_000_000,
    )


def shifted_lanes(values, step, period, inner):
    if step == 0:
        return values
    count = values.shape[1]
    place = (lax.broadcasted_iota(jnp.int32, values.shape, 1) // inner) % period
    rolled = pltpu.roll(values, (-step * inner) % count, 1)
    inside = (place + step >= 0) & (place + step < period)
    return jnp.where(inside, rolled, 0.0)


def six_kernel(
    position, half, gathered, kernel, cot, next_rows, mine, theirs, own, cells, grads, whole
):
    rows = lax.broadcasted_iota(jnp.int32, (16, 256), 0) + position[0] * 16
    lanes = lax.broadcasted_iota(jnp.int32, (16, 256), 1)
    pick = jnp.where(rows == lanes, 1.0, 0.0).astype(jnp.bfloat16)
    for tap in range(27):
        chosen = lax.dot_general(pick, kernel[tap], NT, preferred_element_type=jnp.float32)
        own[tap] = chosen.astype(jnp.bfloat16)
    blank = jnp.zeros((64, 256), jnp.bfloat16)
    cells[0:64, :] = blank
    cells[1088:1152, :] = blank
    cells[64:1088, 0:128] = gathered[:, 0:64, :].reshape(1024, 128)
    cells[64:1088, 128:256] = gathered[:, 64:128, :].reshape(1024, 128)
    products = lax.dot_general(
        own[...].reshape(432, 256), cells[...], NT, preferred_element_type=jnp.float32
    )
    taps = products[0:144, 0:1024] + products[144:288, 64:1088] + products[288:432, 128:1152]
    pre = jnp.zeros((16, 1024), jnp.float32)
    for row_tap in range(3):
        line = jnp.zeros((16, 1024), jnp.float32)
        for col_tap in range(3):
            start = (row_tap * 3 + col_tap) * 16
            line += shifted_lanes(taps[start : start + 16], col_tap - 1, 8, 1)
        pre += shifted_lanes(line, row_tap - 1, 8, 8)
    act, slant = both_of(pre)
    small = lax.broadcasted_iota(jnp.int32, (128, 1024), 0)
    cell = lax.broadcasted_iota(jnp.int32, (128, 1024), 1)
    target = (cell >> 7) * 16 + ((cell % 64) >> 4) * 4 + ((cell % 8) >> 1)
    grow = jnp.where(small == target, 1.0, 0.0).astype(jnp.bfloat16)
    upstream = jnp.dot(cot[...], grow, preferred_element_type=jnp.float32)
    high = act.astype(jnp.bfloat16)
    rest = act - high.astype(jnp.float32)
    middle = rest.astype(jnp.bfloat16)
    low = (rest - middle.astype(jnp.float32)).astype(jnp.bfloat16)
    sums = lax.dot_general(
        jnp.concatenate([high, middle, low], axis=0), grow, NT, preferred_element_type=jnp.float32
    )
    next_rows[...] = ((sums[0:16] + sums[16:32] + sums[32:48]) * 0.125).astype(jnp.bfloat16)
    grad = (upstream * slant).astype(jnp.bfloat16).astype(jnp.float32)
    for row_tap in range(3):
        line = shifted_lanes(grad, 1 - row_tap, 8, 8)
        for col_tap in range(3):
            start = (row_tap * 3 + col_tap) * 16
            moved = shifted_lanes(line, 1 - col_tap, 8, 1)
            grads[start : start + 16, :] = moved.astype(jnp.bfloat16)
    for depth_tap in range(3):
        part = jnp.dot(
            grads[...],
            cells[depth_tap * 64 : depth_tap * 64 + 1024, :],
            preferred_element_type=jnp.float32,
        )
        whole[depth_tap * 9 : depth_tap * 9 + 9] = part.astype(jnp.bfloat16).reshape(9, 16, 256)
    whole[27] = whole[26]
    mine[...] = whole[pl.ds(half[0] * HALF_TAPS, HALF_TAPS)]
    theirs[...] = whole[pl.ds((1 - half[0]) * HALF_TAPS, HALF_TAPS)]


def six_own(gathered, kernel, cot_rows, position, half):
    part = shape((HALF_TAPS, 16, 256), jnp.bfloat16)
    return call(
        six_kernel,
        (shape((16, 128), jnp.bfloat16), part, part),
        [
            VMEM((27, 16, 256), jnp.bfloat16),
            VMEM((1152, 256), jnp.bfloat16),
            VMEM((144, 1024), jnp.bfloat16),
            VMEM((28, 16, 256), jnp.bfloat16),
        ],
        (gathered, kernel.reshape(27, 256, 256), cot_rows),
        (position, half),
        flops=2_000_000_000,
    )


def halves_kernel(half, mine_five, other_five, mine_six, other_six, five, six):
    for step in range(HALF_TAPS):
        for first, part_five, part_six in (
            (half[0] * HALF_TAPS, mine_five, mine_six),
            ((1 - half[0]) * HALF_TAPS, other_five, other_six),
        ):
            tap = jnp.minimum(first + step, 26)
            five[tap] = part_five[step].astype(jnp.float32)
            six[tap] = part_six[step].astype(jnp.float32)


def both_halves(half, mine_five, other_five, mine_six, other_six):
    return call(
        halves_kernel,
        (shape((27, 16, 128), jnp.float32), shape((27, 16, 256), jnp.float32)),
        [],
        (mine_five, other_five, mine_six, other_six),
        (half,),
    )


def ring_perm(axis, step):
    count = lax.axis_size(axis)
    return [(i, (i + step) % count) for i in range(count)]


def core_swap(values):
    count = lax.axis_size("dp")
    return lax.ppermute(values, "dp", [(i, i ^ 1) for i in range(count)])


def from_chips(values):
    count = lax.axis_size("dp")
    got = []
    for step in range(1, count // 2):
        pairs = [(i, (i + 2 * step) % count) for i in range(count)]
        got.append(lax.ppermute(values, "dp", pairs))
    return got


def total_of(values, others):
    total = values.astype(jnp.float32)
    for other in others:
        total = total + other.astype(jnp.float32)
    return total


def exchange(values):
    flat = values.reshape(values.shape[0], -1, values.shape[-1])
    got = lax.all_to_all(flat, "wide", split_axis=0, concat_axis=0, tiled=True)
    return got.reshape(values.shape)


def shards(volume, kernel_five, kernel_six, cotangent):
    position = lax.axis_index("wide").astype(jnp.int32).reshape(1)
    half = (lax.axis_index("dp") % 2).astype(jnp.int32).reshape(1)
    low = lax.ppermute(volume, "wide", ring_perm("wide", 1))
    high = lax.ppermute(volume, "wide", ring_perm("wide", -1))
    cot_rows = cotangent[0].reshape(128, 16).T
    part, inner, near_kernel = inner_five(volume, kernel_five)
    message, slope, padded = outer_five(low, high, near_kernel, part, inner, cot_rows, position)
    message, position, half, slope, padded = lax.optimization_barrier(
        (message, position, half, slope, padded)
    )
    gathered = exchange(message)
    gathered, position, half, slope, padded = lax.optimization_barrier(
        (gathered, position, half, slope, padded)
    )
    rows, theirs_five = back_five(gathered, kernel_six, slope, padded, position, half)
    got_five = core_swap(theirs_five)
    next_rows, mine_six, theirs_six = six_own(gathered, kernel_six, cot_rows, position, half)
    got_six = core_swap(theirs_six)
    pair_five = mine_of_five(rows, padded, got_five, half)
    pair_five, got_six, mine_six, next_rows = lax.optimization_barrier(
        (pair_five, got_six, mine_six, next_rows)
    )
    pair_six = total_of(mine_six, [got_six]).astype(jnp.bfloat16)
    chips_six = from_chips(pair_six)
    spread = exchange(pair_five)
    spread, chips_six = lax.optimization_barrier((spread, chips_six))
    depth_five = spread.astype(jnp.float32).sum(0).astype(jnp.bfloat16)
    total_six = total_of(pair_six, chips_six).astype(jnp.bfloat16)
    total_five = total_of(depth_five, from_chips(depth_five)).astype(jnp.bfloat16)
    other_five, other_six = core_swap(total_five), core_swap(total_six)
    out_five, out_six = both_halves(half, total_five, other_five, total_six, other_six)
    out_five = out_five.transpose(0, 2, 1).reshape(3, 3, 3, 128, 16)
    out_six = out_six.transpose(0, 2, 1).reshape(3, 3, 3, 256, 16)
    return (next_rows.T.reshape(1, 8, 4, 4, 16), out_five, out_six)


def solution(mesh):
    in_specs = (P("dp", "wide", None, None, None), P(), P(), P("dp", None, None, None, "wide"))
    out_specs = (
        P("dp", None, None, None, "wide"),
        P(None, None, None, None, "wide"),
        P(None, None, None, None, "wide"),
    )
    return jax.shard_map(shards, mesh=mesh, in_specs=in_specs, out_specs=out_specs, check_vma=False)
```

```python
import jax
import jax.numpy as jnp
from jax import lax
from jax.experimental import pallas as pl
from jax.experimental.pallas import tpu as pltpu
from jax.sharding import PartitionSpec as P

SLOPE = 0.3
HALF_TAPS = 14
VMEM = pltpu.VMEM
NT = (((1,), (1,)), ((), ()))


def both_of(value):
    sigma = 1.0 / (1.0 + jnp.exp(-value))
    act = value * (SLOPE + (1.0 - SLOPE) * sigma)
    slope = 0.125 * SLOPE + (0.125 * (1.0 - SLOPE)) * (sigma + value * sigma * (1.0 - sigma))
    return act, slope


def call(body, out_shape, scratch, operands, scalars=(), flops=0, limit=16, far=(), far_out=False):
    specs = [pl.BlockSpec(memory_space=pltpu.SMEM)] * len(scalars)
    specs += [
        pl.BlockSpec(memory_space=pltpu.HBM if index in far else VMEM)
        for index in range(len(operands))
    ]
    place = pltpu.HBM if far_out else VMEM
    outs = jax.tree.map(lambda _: pl.BlockSpec(memory_space=place), out_shape)
    return pl.pallas_call(
        body,
        out_shape=out_shape,
        in_specs=specs,
        out_specs=outs,
        scratch_shapes=scratch,
        compiler_params=pltpu.CompilerParams(vmem_limit_bytes=int(limit * 1024 * 1024)),
        cost_estimate=pl.CostEstimate(flops=flops, bytes_accessed=4_000_000, transcendentals=0),
    )(*scalars, *operands)


def shape(dims, kind):
    return jax.ShapeDtypeStruct(dims, kind)


def shifted_rows(values, step, period):
    if step == 0:
        return values
    count = values.shape[0]
    column = lax.broadcasted_iota(jnp.int32, values.shape, 0) % period
    rolled = pltpu.roll(values, (-step) % count, 0)
    inside = (column + step >= 0) & (column + step < period)
    return jnp.where(inside, rolled, 0.0)


def columns_of(padded, index, source):
    values = source.astype(jnp.float32)
    padded[index, 0:16, :] = jnp.zeros((16, 384), jnp.bfloat16)
    padded[index, 272:288, :] = jnp.zeros((16, 384), jnp.bfloat16)
    padded[index, 16:272, 0:128] = shifted_rows(values, -1, 16).astype(jnp.bfloat16)
    padded[index, 16:272, 128:256] = source
    padded[index, 16:272, 256:384] = shifted_rows(values, 1, 16).astype(jnp.bfloat16)


def depth_term(padded, first, planes, kernel, depth_tap):
    cells = jnp.concatenate(
        [
            padded[first : first + planes, 16 * row_tap : 16 * row_tap + 256, :].reshape(
                256 * planes, 384
            )
            for row_tap in range(3)
        ],
        axis=1,
    )
    taps = kernel[depth_tap * 1152 : depth_tap * 1152 + 1152, :]
    return jnp.dot(cells, taps, preferred_element_type=jnp.float32)


def inner_kernel(slab, kernel_far, part, padded, kernel, marks):
    loads = {}
    for depth_tap in (1, 2, 0):
        rows = pl.ds(depth_tap * 1152, 1152)
        loads[depth_tap] = pltpu.make_async_copy(
            kernel_far.at[rows], kernel.at[rows], marks.at[depth_tap]
        )
        loads[depth_tap].start()
    for plane in range(2):
        columns_of(padded, plane, slab[plane])
    loads[1].wait()
    for plane in range(2):
        part[plane * 256 : (plane + 1) * 256, :] = depth_term(padded, plane, 1, kernel, 1)
    loads[2].wait()
    part[0:256, :] += depth_term(padded, 1, 1, kernel, 2)
    loads[0].wait()
    part[256:512, :] += depth_term(padded, 0, 1, kernel, 0)


def inner_five(slab, kernel):
    return call(
        inner_kernel,
        (
            shape((512, 256), jnp.float32),
            shape((2, 288, 384), jnp.bfloat16),
            shape((3456, 256), jnp.bfloat16),
        ),
        [pltpu.SemaphoreType.DMA((3,))],
        (slab.reshape(2, 256, 128), kernel.reshape(3456, 256)),
        flops=600_000_000,
        limit=51,
        far=(1,),
    )


def outer_kernel(position, low, high, kernel, part, inner, cot, message, slope, padded, tall):
    columns_of(padded, 0, jnp.where(position[0] == 0, jnp.zeros((256, 128), jnp.bfloat16), low[1]))
    columns_of(padded, 3, jnp.where(position[0] == 15, jnp.zeros((256, 128), jnp.bfloat16), high[0]))
    padded[1:3] = inner[...]
    acts = []
    for plane in range(2):
        total = part[plane * 256 : (plane + 1) * 256, :]
        total += depth_term(padded, 3 * plane, 1, kernel, 2 * plane)
        act, slant = both_of(total)
        slope[plane * 256 : (plane + 1) * 256, :] = slant
        acts.append(act)
    two = (acts[0] + acts[1]).reshape(8, 2, 16, 256)
    pairs = (two[:, 0] + two[:, 1]).reshape(128, 256)
    pooled = []
    for side in range(2):
        tall[side] = pairs[:, side * 128 : (side + 1) * 128]
        even = tall[side, pl.ds(0, 64, stride=2), :]
        odd = tall[side, pl.ds(1, 64, stride=2), :]
        pooled.append(((even + odd) * 0.125).astype(jnp.bfloat16))
    cells = cot[...].astype(jnp.float32).reshape(128, 16)
    same = lax.broadcasted_iota(jnp.int32, (16, 16), 0) == lax.broadcasted_iota(
        jnp.int32, (16, 16), 1
    )
    unit = jnp.where(same, 1.0, 0.0)
    marks = lax.dot_general(
        unit.astype(jnp.bfloat16),
        cells.astype(jnp.bfloat16),
        NT,
        preferred_element_type=jnp.float32,
    ).astype(jnp.bfloat16)
    for target in range(16):
        message[target, 0:64, :] = pooled[0]
        message[target, 64:128, :] = pooled[1]
        message[target, 128:144, :] = marks


def outer_five(low, high, kernel, part, inner, cot_rows, position):
    return call(
        outer_kernel,
        (
            shape((16, 144, 128), jnp.bfloat16),
            shape((512, 256), jnp.float32),
            shape((4, 288, 384), jnp.bfloat16),
        ),
        [VMEM((2, 128, 128), jnp.float32)],
        (
            low.reshape(2, 256, 128),
            high.reshape(2, 256, 128),
            kernel,
            part,
            inner,
            cot_rows,
        ),
        (position,),
        flops=300_000_000,
    )


def six_to_five(position, gathered, kernel, slope, rows_out, near, tall):
    for plane in range(5):
        where = position[0] + (plane - 2)
        inside = (where >= 0) & (where < 16)
        index = jnp.clip(where, 0, 15)
        left = gathered[index, 0:64, :]
        right = gathered[index, 64:128, :]
        values = jnp.concatenate([left, right], axis=1).astype(jnp.float32)
        values = jnp.where(inside, values, 0.0)
        blank = jnp.zeros((8, 256), jnp.float32)
        for col_tap in range(3):
            moved = shifted_rows(values, col_tap - 1, 8)
            for row_tap in range(3):
                if row_tap == 0:
                    cells = jnp.concatenate([blank, moved[:56]], axis=0)
                elif row_tap == 1:
                    cells = moved
                else:
                    cells = jnp.concatenate([moved[8:], blank], axis=0)
                lane = (row_tap * 3 + col_tap) * 256
                near[plane, :, lane : lane + 256] = cells.astype(jnp.bfloat16)
    pre_six = jnp.zeros((192, 256), jnp.float32)
    for depth_tap in range(3):
        taps = kernel[depth_tap * 9 : depth_tap * 9 + 9].reshape(2304, 256)
        cells = near[depth_tap : depth_tap + 3].reshape(192, 2304)
        pre_six += jnp.dot(cells, taps, preferred_element_type=jnp.float32)
    _, slant = both_of(pre_six)
    cell = lax.broadcasted_iota(jnp.int32, (192, 128), 0)
    lanes = lax.broadcasted_iota(jnp.int32, (192, 128), 1)
    depth = cell // 64 + position[0] - 1
    small = (depth >> 1) * 16 + ((cell % 64) >> 4) * 4 + ((cell % 8) >> 1)
    hit = (small == lanes) & (depth >= 0) & (depth < 16)
    grow = jnp.where(hit, 1.0, 0.0).astype(jnp.bfloat16)
    cot = gathered[:, 128:144, :].reshape(256, 128)
    upstream = lax.dot_general(grow, cot, NT, preferred_element_type=jnp.float32)
    grad_six = (upstream * slant).astype(jnp.bfloat16).astype(jnp.float32)
    blank = jnp.zeros((8, 256), jnp.float32)
    for depth_tap in range(3):
        values = grad_six[(2 - depth_tap) * 64 : (3 - depth_tap) * 64]
        for col_tap in range(3):
            moved = shifted_rows(values, 1 - col_tap, 8)
            for row_tap in range(3):
                if row_tap == 0:
                    cells = jnp.concatenate([moved[8:], blank], axis=0)
                elif row_tap == 1:
                    cells = moved
                else:
                    cells = jnp.concatenate([blank, moved[:56]], axis=0)
                lane = (row_tap * 3 + col_tap) * 256
                near[depth_tap, :, lane : lane + 256] = cells.astype(jnp.bfloat16)

    def depth_of(depth_tap, total):
        for tap in range(9):
            total += lax.dot_general(
                near[depth_tap, :, tap * 256 : tap * 256 + 256],
                kernel[depth_tap * 9 + tap],
                NT,
                preferred_element_type=jnp.float32,
            )
        return total

    grad_pooled = lax.fori_loop(0, 3, depth_of, jnp.zeros((64, 256), jnp.float32))
    for side in range(2):
        tall[side, pl.ds(0, 64, stride=2), :] = grad_pooled[:, side * 128 : (side + 1) * 128]
        tall[side, pl.ds(1, 64, stride=2), :] = grad_pooled[:, side * 128 : (side + 1) * 128]
    both = jnp.concatenate([tall[0], tall[1]], axis=1)
    wide = jnp.broadcast_to(both.reshape(8, 1, 16, 256), (8, 2, 16, 256)).reshape(256, 256)
    for plane in range(2):
        grad = wide * slope[plane * 256 : (plane + 1) * 256, :]
        rows_out[:, plane * 256 : (plane + 1) * 256] = grad.T.astype(jnp.bfloat16)


def tap_cells(padded, plane, tap):
    depth_tap, row_tap, col_tap = tap // 9, (tap // 3) % 3, tap % 3
    return padded[
        plane + depth_tap,
        pl.ds(pl.multiple_of(row_tap * 16, 16), 256),
        pl.ds(pl.multiple_of(col_tap * 128, 128), 128),
    ]


def half_of_five(first, rows, padded, out, got=None, send=None):
    for step in range(0, HALF_TAPS, 2):
        taps = [jnp.minimum(first + step + other, 26) for other in range(2)]
        total = jnp.zeros((256, 256), jnp.float32)
        for plane in range(2):
            cells = jnp.concatenate([tap_cells(padded, plane, tap) for tap in taps], axis=1)
            total += jnp.dot(
                rows[:, plane * 256 : (plane + 1) * 256],
                cells,
                preferred_element_type=jnp.float32,
            )
        for other in range(2):
            part = total[:, other * 128 : (other + 1) * 128]
            if got is not None:
                part += got[:, step + other].reshape(256, 128).astype(jnp.float32)
            out[:, step + other] = part.astype(jnp.bfloat16).reshape(16, 16, 128)
        if send is not None:
            send(step)


def back_kernel(position, half, gathered, kernel, slope, padded, rows, theirs, near, tall):
    six_to_five(position, gathered, kernel, slope, rows, near, tall)
    half_of_five((1 - half[0]) * HALF_TAPS, rows, padded, theirs)


def back_five(gathered, kernel, slope, padded, position, half):
    return call(
        back_kernel,
        (shape((256, 512), jnp.bfloat16), shape((16, HALF_TAPS, 16, 128), jnp.bfloat16)),
        [VMEM((5, 64, 2304), jnp.bfloat16), VMEM((2, 128, 128), jnp.float32)],
        (gathered, kernel.reshape(27, 256, 256), slope, padded),
        (position, half),
        flops=3_000_000_000,
    )


def mine_kernel(half, rows, padded, got, mine, staged, marks):
    sends = []

    def send(step):
        pair = pl.ds(step, 2)
        sends.append(
            pltpu.make_async_copy(staged.at[:, pair], mine.at[:, pair], marks.at[step // 2])
        )
        sends[-1].start()

    half_of_five(half[0] * HALF_TAPS, rows, padded, staged, got, send)
    for copy in sends:
        copy.wait()


def mine_of_five(rows, padded, got, half):
    return call(
        mine_kernel,
        shape((16, HALF_TAPS, 16, 128), jnp.bfloat16),
        [
            VMEM((16, HALF_TAPS, 16, 128), jnp.bfloat16),
            pltpu.SemaphoreType.DMA((HALF_TAPS // 2,)),
        ],
        (rows, padded, got),
        (half,),
        flops=900_000_000,
        far_out=True,
    )


def shifted_lanes(values, step, period, inner):
    if step == 0:
        return values
    count = values.shape[1]
    place = (lax.broadcasted_iota(jnp.int32, values.shape, 1) // inner) % period
    rolled = pltpu.roll(values, (-step * inner) % count, 1)
    inside = (place + step >= 0) & (place + step < period)
    return jnp.where(inside, rolled, 0.0)


def six_kernel(
    position, half, gathered, kernel, next_rows, mine, theirs, own, cells, grads, whole
):
    rows = lax.broadcasted_iota(jnp.int32, (16, 256), 0) + position[0] * 16
    lanes = lax.broadcasted_iota(jnp.int32, (16, 256), 1)
    pick = jnp.where(rows == lanes, 1.0, 0.0).astype(jnp.bfloat16)
    for tap in range(27):
        chosen = lax.dot_general(pick, kernel[tap], NT, preferred_element_type=jnp.float32)
        own[tap] = chosen.astype(jnp.bfloat16)
    blank = jnp.zeros((64, 256), jnp.bfloat16)
    cells[0:64, :] = blank
    cells[1088:1152, :] = blank
    cells[64:1088, 0:128] = gathered[:, 0:64, :].reshape(1024, 128)
    cells[64:1088, 128:256] = gathered[:, 64:128, :].reshape(1024, 128)
    products = lax.dot_general(
        own[...].reshape(432, 256), cells[...], NT, preferred_element_type=jnp.float32
    )
    taps = products[0:144, 0:1024] + products[144:288, 64:1088] + products[288:432, 128:1152]
    pre = jnp.zeros((16, 1024), jnp.float32)
    for row_tap in range(3):
        line = jnp.zeros((16, 1024), jnp.float32)
        for col_tap in range(3):
            start = (row_tap * 3 + col_tap) * 16
            line += shifted_lanes(taps[start : start + 16], col_tap - 1, 8, 1)
        pre += shifted_lanes(line, row_tap - 1, 8, 8)
    act, slant = both_of(pre)
    small = lax.broadcasted_iota(jnp.int32, (128, 1024), 0)
    cell = lax.broadcasted_iota(jnp.int32, (128, 1024), 1)
    target = (cell >> 7) * 16 + ((cell % 64) >> 4) * 4 + ((cell % 8) >> 1)
    grow = jnp.where(small == target, 1.0, 0.0).astype(jnp.bfloat16)
    cot = gathered[position[0], 128:144, :]
    upstream = jnp.dot(cot, grow, preferred_element_type=jnp.float32)
    high = act.astype(jnp.bfloat16)
    rest = act - high.astype(jnp.float32)
    middle = rest.astype(jnp.bfloat16)
    low = (rest - middle.astype(jnp.float32)).astype(jnp.bfloat16)
    sums = lax.dot_general(
        jnp.concatenate([high, middle, low], axis=0), grow, NT, preferred_element_type=jnp.float32
    )
    next_rows[...] = ((sums[0:16] + sums[16:32] + sums[32:48]) * 0.125).astype(jnp.bfloat16)
    grad = (upstream * slant).astype(jnp.bfloat16).astype(jnp.float32)
    for row_tap in range(3):
        line = shifted_lanes(grad, 1 - row_tap, 8, 8)
        for col_tap in range(3):
            start = (row_tap * 3 + col_tap) * 16
            moved = shifted_lanes(line, 1 - col_tap, 8, 1)
            grads[start : start + 16, :] = moved.astype(jnp.bfloat16)
    for depth_tap in range(3):
        part = jnp.dot(
            grads[...],
            cells[depth_tap * 64 : depth_tap * 64 + 1024, :],
            preferred_element_type=jnp.float32,
        )
        whole[depth_tap * 9 : depth_tap * 9 + 9] = part.astype(jnp.bfloat16).reshape(9, 16, 256)
    whole[27] = whole[26]
    mine[...] = whole[pl.ds(half[0] * HALF_TAPS, HALF_TAPS)]
    theirs[...] = whole[pl.ds((1 - half[0]) * HALF_TAPS, HALF_TAPS)]


def six_own(gathered, kernel, position, half):
    part = shape((HALF_TAPS, 16, 256), jnp.bfloat16)
    return call(
        six_kernel,
        (shape((16, 128), jnp.bfloat16), part, part),
        [
            VMEM((27, 16, 256), jnp.bfloat16),
            VMEM((1152, 256), jnp.bfloat16),
            VMEM((144, 1024), jnp.bfloat16),
            VMEM((28, 16, 256), jnp.bfloat16),
        ],
        (gathered, kernel.reshape(27, 256, 256)),
        (position, half),
        flops=2_000_000_000,
    )


def halves_kernel(half, mine_five, other_five, mine_six, other_six, five, six):
    for step in range(HALF_TAPS):
        for first, part_five, part_six in (
            (half[0] * HALF_TAPS, mine_five, mine_six),
            ((1 - half[0]) * HALF_TAPS, other_five, other_six),
        ):
            tap = jnp.minimum(first + step, 26)
            five[tap] = part_five[step].astype(jnp.float32)
            six[tap] = part_six[step].astype(jnp.float32)


def both_halves(half, mine_five, other_five, mine_six, other_six):
    return call(
        halves_kernel,
        (shape((27, 16, 128), jnp.float32), shape((27, 16, 256), jnp.float32)),
        [],
        (mine_five, other_five, mine_six, other_six),
        (half,),
    )


def ring_perm(axis, step):
    count = lax.axis_size(axis)
    return [(i, (i + step) % count) for i in range(count)]


def core_swap(values):
    count = lax.axis_size("dp")
    return lax.ppermute(values, "dp", [(i, i ^ 1) for i in range(count)])


def from_chips(values):
    count = lax.axis_size("dp")
    got = []
    for step in range(1, count // 2):
        pairs = [(i, (i + 2 * step) % count) for i in range(count)]
        got.append(lax.ppermute(values, "dp", pairs))
    return got


def total_of(values, others):
    total = values.astype(jnp.float32)
    for other in others:
        total = total + other.astype(jnp.float32)
    return total


def exchange(values):
    flat = values.reshape(values.shape[0], -1, values.shape[-1])
    got = lax.all_to_all(flat, "wide", split_axis=0, concat_axis=0, tiled=True)
    return got.reshape(values.shape)


def shards(volume, kernel_five, kernel_six, cotangent):
    position = lax.axis_index("wide").astype(jnp.int32).reshape(1)
    half = (lax.axis_index("dp") % 2).astype(jnp.int32).reshape(1)
    low = lax.ppermute(volume, "wide", ring_perm("wide", 1))
    high = lax.ppermute(volume, "wide", ring_perm("wide", -1))
    cot_rows = cotangent.reshape(32, 4, 16)
    part, inner, near_kernel = inner_five(volume, kernel_five)
    message, slope, padded = outer_five(low, high, near_kernel, part, inner, cot_rows, position)
    message, position, half, slope, padded = lax.optimization_barrier(
        (message, position, half, slope, padded)
    )
    gathered = exchange(message)
    gathered, position, half, slope, padded = lax.optimization_barrier(
        (gathered, position, half, slope, padded)
    )
    rows, theirs_five = back_five(gathered, kernel_six, slope, padded, position, half)
    got_five = core_swap(theirs_five)
    next_rows, mine_six, theirs_six = six_own(gathered, kernel_six, position, half)
    got_six = core_swap(theirs_six)
    pair_five = mine_of_five(rows, padded, got_five, half)
    pair_five, got_six, mine_six, next_rows = lax.optimization_barrier(
        (pair_five, got_six, mine_six, next_rows)
    )
    pair_six = total_of(mine_six, [got_six]).astype(jnp.bfloat16)
    chips_six = from_chips(pair_six)
    spread = exchange(pair_five)
    spread, chips_six = lax.optimization_barrier((spread, chips_six))
    depth_five = spread.astype(jnp.float32).sum(0).astype(jnp.bfloat16)
    total_six = total_of(pair_six, chips_six).astype(jnp.bfloat16)
    total_five = total_of(depth_five, from_chips(depth_five)).astype(jnp.bfloat16)
    other_five, other_six = core_swap(total_five), core_swap(total_six)
    out_five, out_six = both_halves(half, total_five, other_five, total_six, other_six)
    out_five = out_five.transpose(0, 2, 1).reshape(3, 3, 3, 128, 16)
    out_six = out_six.transpose(0, 2, 1).reshape(3, 3, 3, 256, 16)
    return (next_rows.T.reshape(1, 8, 4, 4, 16), out_five, out_six)


def solution(mesh):
    in_specs = (P("dp", "wide", None, None, None), P(), P(), P("dp", None, None, None, "wide"))
    out_specs = (
        P("dp", None, None, None, "wide"),
        P(None, None, None, None, "wide"),
        P(None, None, None, None, "wide"),
    )
    return jax.shard_map(shards, mesh=mesh, in_specs=in_specs, out_specs=out_specs, check_vma=False)
```

```python
import jax
import jax.numpy as jnp
from jax import lax
from jax.experimental import pallas as pl
from jax.experimental.pallas import tpu as pltpu
from jax.sharding import PartitionSpec as P

SLOPE = 0.3
HALF_TAPS = 14
VMEM = pltpu.VMEM
NT = (((1,), (1,)), ((), ()))


def both_of(value):
    sigma = 1.0 / (1.0 + jnp.exp(-value))
    act = value * (SLOPE + (1.0 - SLOPE) * sigma)
    slope = 0.125 * SLOPE + (0.125 * (1.0 - SLOPE)) * (sigma + value * sigma * (1.0 - sigma))
    return act, slope


def call(body, out_shape, scratch, operands, scalars=(), flops=0, limit=16, far=(), far_out=False):
    specs = [pl.BlockSpec(memory_space=pltpu.SMEM)] * len(scalars)
    specs += [
        pl.BlockSpec(memory_space=pltpu.HBM if index in far else VMEM)
        for index in range(len(operands))
    ]
    place = pltpu.HBM if far_out else VMEM
    outs = jax.tree.map(lambda _: pl.BlockSpec(memory_space=place), out_shape)
    return pl.pallas_call(
        body,
        out_shape=out_shape,
        in_specs=specs,
        out_specs=outs,
        scratch_shapes=scratch,
        compiler_params=pltpu.CompilerParams(vmem_limit_bytes=int(limit * 1024 * 1024)),
        cost_estimate=pl.CostEstimate(flops=flops, bytes_accessed=4_000_000, transcendentals=0),
    )(*scalars, *operands)


def shape(dims, kind):
    return jax.ShapeDtypeStruct(dims, kind)


def shifted_rows(values, step, period):
    if step == 0:
        return values
    count = values.shape[0]
    column = lax.broadcasted_iota(jnp.int32, values.shape, 0) % period
    rolled = pltpu.roll(values, (-step) % count, 0)
    inside = (column + step >= 0) & (column + step < period)
    return jnp.where(inside, rolled, 0.0)


def columns_of(padded, index, source):
    values = source.astype(jnp.float32)
    padded[index, 0:16, :] = jnp.zeros((16, 384), jnp.bfloat16)
    padded[index, 272:288, :] = jnp.zeros((16, 384), jnp.bfloat16)
    padded[index, 16:272, 0:128] = shifted_rows(values, -1, 16).astype(jnp.bfloat16)
    padded[index, 16:272, 128:256] = source
    padded[index, 16:272, 256:384] = shifted_rows(values, 1, 16).astype(jnp.bfloat16)


def depth_term(padded, first, planes, kernel, depth_tap):
    cells = jnp.concatenate(
        [
            padded[first : first + planes, 16 * row_tap : 16 * row_tap + 256, :].reshape(
                256 * planes, 384
            )
            for row_tap in range(3)
        ],
        axis=1,
    )
    taps = kernel[depth_tap * 1152 : depth_tap * 1152 + 1152, :]
    return jnp.dot(cells, taps, preferred_element_type=jnp.float32)


def inner_kernel(slab, kernel_far, part, padded, kernel, marks):
    loads = {}
    for depth_tap in (1, 2, 0):
        rows = pl.ds(depth_tap * 1152, 1152)
        loads[depth_tap] = pltpu.make_async_copy(
            kernel_far.at[rows], kernel.at[rows], marks.at[depth_tap]
        )
        loads[depth_tap].start()
    for plane in range(2):
        columns_of(padded, plane, slab[plane])
    loads[1].wait()
    for plane in range(2):
        part[plane * 256 : (plane + 1) * 256, :] = depth_term(padded, plane, 1, kernel, 1)
    loads[2].wait()
    part[0:256, :] += depth_term(padded, 1, 1, kernel, 2)
    loads[0].wait()
    part[256:512, :] += depth_term(padded, 0, 1, kernel, 0)


def inner_five(slab, kernel):
    return call(
        inner_kernel,
        (
            shape((512, 256), jnp.float32),
            shape((2, 288, 384), jnp.bfloat16),
            shape((3456, 256), jnp.bfloat16),
        ),
        [pltpu.SemaphoreType.DMA((3,))],
        (slab.reshape(2, 256, 128), kernel.reshape(3456, 256)),
        flops=600_000_000,
        limit=51,
        far=(1,),
    )


def outer_kernel(position, odds, evens, kernel, part, inner, cot, message, slope, padded, tall):
    even = position[0] % 2 == 0
    blank = jnp.zeros((256, 128), jnp.bfloat16)
    low = jnp.where(even, odds[1], evens[1])
    high = jnp.where(even, evens[0], odds[0])
    columns_of(padded, 0, jnp.where(position[0] == 0, blank, low))
    columns_of(padded, 3, jnp.where(position[0] == 15, blank, high))
    padded[1:3] = inner[...]
    acts = []
    for plane in range(2):
        total = part[plane * 256 : (plane + 1) * 256, :]
        total += depth_term(padded, 3 * plane, 1, kernel, 2 * plane)
        act, slant = both_of(total)
        slope[plane * 256 : (plane + 1) * 256, :] = slant
        acts.append(act)
    two = (acts[0] + acts[1]).reshape(8, 2, 16, 256)
    pairs = (two[:, 0] + two[:, 1]).reshape(128, 256)
    pooled = []
    for side in range(2):
        tall[side] = pairs[:, side * 128 : (side + 1) * 128]
        even = tall[side, pl.ds(0, 64, stride=2), :]
        odd = tall[side, pl.ds(1, 64, stride=2), :]
        pooled.append(((even + odd) * 0.125).astype(jnp.bfloat16))
    cells = cot[...].astype(jnp.float32).reshape(128, 16)
    same = lax.broadcasted_iota(jnp.int32, (16, 16), 0) == lax.broadcasted_iota(
        jnp.int32, (16, 16), 1
    )
    unit = jnp.where(same, 1.0, 0.0)
    marks = lax.dot_general(
        unit.astype(jnp.bfloat16),
        cells.astype(jnp.bfloat16),
        NT,
        preferred_element_type=jnp.float32,
    ).astype(jnp.bfloat16)
    for target in range(16):
        message[target, 0:64, :] = pooled[0]
        message[target, 64:128, :] = pooled[1]
        message[target, 128:144, :] = marks


def outer_five(odds, evens, kernel, part, inner, cot_rows, position):
    return call(
        outer_kernel,
        (
            shape((16, 144, 128), jnp.bfloat16),
            shape((512, 256), jnp.float32),
            shape((4, 288, 384), jnp.bfloat16),
        ),
        [VMEM((2, 128, 128), jnp.float32)],
        (
            odds.reshape(2, 256, 128),
            evens.reshape(2, 256, 128),
            kernel,
            part,
            inner,
            cot_rows,
        ),
        (position,),
        flops=300_000_000,
    )


def six_to_five(position, gathered, kernel, slope, rows_out, near, tall):
    for plane in range(5):
        where = position[0] + (plane - 2)
        inside = (where >= 0) & (where < 16)
        index = jnp.clip(where, 0, 15)
        left = gathered[index, 0:64, :]
        right = gathered[index, 64:128, :]
        values = jnp.concatenate([left, right], axis=1).astype(jnp.float32)
        values = jnp.where(inside, values, 0.0)
        blank = jnp.zeros((8, 256), jnp.float32)
        for col_tap in range(3):
            moved = shifted_rows(values, col_tap - 1, 8)
            for row_tap in range(3):
                if row_tap == 0:
                    cells = jnp.concatenate([blank, moved[:56]], axis=0)
                elif row_tap == 1:
                    cells = moved
                else:
                    cells = jnp.concatenate([moved[8:], blank], axis=0)
                lane = (row_tap * 3 + col_tap) * 256
                near[plane, :, lane : lane + 256] = cells.astype(jnp.bfloat16)
    pre_six = jnp.zeros((192, 256), jnp.float32)
    for depth_tap in range(3):
        taps = kernel[depth_tap * 9 : depth_tap * 9 + 9].reshape(2304, 256)
        cells = near[depth_tap : depth_tap + 3].reshape(192, 2304)
        pre_six += jnp.dot(cells, taps, preferred_element_type=jnp.float32)
    _, slant = both_of(pre_six)
    cell = lax.broadcasted_iota(jnp.int32, (192, 128), 0)
    lanes = lax.broadcasted_iota(jnp.int32, (192, 128), 1)
    depth = cell // 64 + position[0] - 1
    small = (depth >> 1) * 16 + ((cell % 64) >> 4) * 4 + ((cell % 8) >> 1)
    hit = (small == lanes) & (depth >= 0) & (depth < 16)
    grow = jnp.where(hit, 1.0, 0.0).astype(jnp.bfloat16)
    cot = gathered[:, 128:144, :].reshape(256, 128)
    upstream = lax.dot_general(grow, cot, NT, preferred_element_type=jnp.float32)
    grad_six = (upstream * slant).astype(jnp.bfloat16).astype(jnp.float32)
    blank = jnp.zeros((8, 256), jnp.float32)
    for depth_tap in range(3):
        values = grad_six[(2 - depth_tap) * 64 : (3 - depth_tap) * 64]
        for col_tap in range(3):
            moved = shifted_rows(values, 1 - col_tap, 8)
            for row_tap in range(3):
                if row_tap == 0:
                    cells = jnp.concatenate([moved[8:], blank], axis=0)
                elif row_tap == 1:
                    cells = moved
                else:
                    cells = jnp.concatenate([blank, moved[:56]], axis=0)
                lane = (row_tap * 3 + col_tap) * 256
                near[depth_tap, :, lane : lane + 256] = cells.astype(jnp.bfloat16)

    def depth_of(depth_tap, total):
        for tap in range(9):
            total += lax.dot_general(
                near[depth_tap, :, tap * 256 : tap * 256 + 256],
                kernel[depth_tap * 9 + tap],
                NT,
                preferred_element_type=jnp.float32,
            )
        return total

    grad_pooled = lax.fori_loop(0, 3, depth_of, jnp.zeros((64, 256), jnp.float32))
    for side in range(2):
        tall[side, pl.ds(0, 64, stride=2), :] = grad_pooled[:, side * 128 : (side + 1) * 128]
        tall[side, pl.ds(1, 64, stride=2), :] = grad_pooled[:, side * 128 : (side + 1) * 128]
    both = jnp.concatenate([tall[0], tall[1]], axis=1)
    wide = jnp.broadcast_to(both.reshape(8, 1, 16, 256), (8, 2, 16, 256)).reshape(256, 256)
    for plane in range(2):
        grad = wide * slope[plane * 256 : (plane + 1) * 256, :]
        rows_out[:, plane * 256 : (plane + 1) * 256] = grad.T.astype(jnp.bfloat16)


def tap_cells(padded, plane, tap):
    depth_tap, row_tap, col_tap = tap // 9, (tap // 3) % 3, tap % 3
    return padded[
        plane + depth_tap,
        pl.ds(pl.multiple_of(row_tap * 16, 16), 256),
        pl.ds(pl.multiple_of(col_tap * 128, 128), 128),
    ]


def half_of_five(first, rows, padded, out, got=None, send=None):
    for step in range(0, HALF_TAPS, 2):
        taps = [jnp.minimum(first + step + other, 26) for other in range(2)]
        total = jnp.zeros((256, 256), jnp.float32)
        for plane in range(2):
            cells = jnp.concatenate([tap_cells(padded, plane, tap) for tap in taps], axis=1)
            total += jnp.dot(
                rows[:, plane * 256 : (plane + 1) * 256],
                cells,
                preferred_element_type=jnp.float32,
            )
        for other in range(2):
            part = total[:, other * 128 : (other + 1) * 128]
            if got is not None:
                part += got[:, step + other].reshape(256, 128).astype(jnp.float32)
            out[:, step + other] = part.astype(jnp.bfloat16).reshape(16, 16, 128)
        if send is not None:
            send(step)


def back_kernel(position, half, gathered, kernel, slope, padded, rows, theirs, near, tall):
    six_to_five(position, gathered, kernel, slope, rows, near, tall)
    half_of_five((1 - half[0]) * HALF_TAPS, rows, padded, theirs)


def back_five(gathered, kernel, slope, padded, position, half):
    return call(
        back_kernel,
        (shape((256, 512), jnp.bfloat16), shape((16, HALF_TAPS, 16, 128), jnp.bfloat16)),
        [VMEM((5, 64, 2304), jnp.bfloat16), VMEM((2, 128, 128), jnp.float32)],
        (gathered, kernel.reshape(27, 256, 256), slope, padded),
        (position, half),
        flops=3_000_000_000,
    )


def mine_kernel(half, rows, padded, got, mine, staged, marks):
    sends = []

    def send(step):
        pair = pl.ds(step, 2)
        sends.append(
            pltpu.make_async_copy(staged.at[:, pair], mine.at[:, pair], marks.at[step // 2])
        )
        sends[-1].start()

    half_of_five(half[0] * HALF_TAPS, rows, padded, staged, got, send)
    for copy in sends:
        copy.wait()


def mine_of_five(rows, padded, got, half):
    return call(
        mine_kernel,
        shape((16, HALF_TAPS, 16, 128), jnp.bfloat16),
        [
            VMEM((16, HALF_TAPS, 16, 128), jnp.bfloat16),
            pltpu.SemaphoreType.DMA((HALF_TAPS // 2,)),
        ],
        (rows, padded, got),
        (half,),
        flops=900_000_000,
        far_out=True,
    )


def shifted_lanes(values, step, period, inner):
    if step == 0:
        return values
    count = values.shape[1]
    place = (lax.broadcasted_iota(jnp.int32, values.shape, 1) // inner) % period
    rolled = pltpu.roll(values, (-step * inner) % count, 1)
    inside = (place + step >= 0) & (place + step < period)
    return jnp.where(inside, rolled, 0.0)


def six_kernel(
    position, half, gathered, kernel, next_rows, mine, theirs, own, cells, grads, whole
):
    rows = lax.broadcasted_iota(jnp.int32, (16, 256), 0) + position[0] * 16
    lanes = lax.broadcasted_iota(jnp.int32, (16, 256), 1)
    pick = jnp.where(rows == lanes, 1.0, 0.0).astype(jnp.bfloat16)
    for tap in range(27):
        chosen = lax.dot_general(pick, kernel[tap], NT, preferred_element_type=jnp.float32)
        own[tap] = chosen.astype(jnp.bfloat16)
    blank = jnp.zeros((64, 256), jnp.bfloat16)
    cells[0:64, :] = blank
    cells[1088:1152, :] = blank
    cells[64:1088, 0:128] = gathered[:, 0:64, :].reshape(1024, 128)
    cells[64:1088, 128:256] = gathered[:, 64:128, :].reshape(1024, 128)
    products = lax.dot_general(
        own[...].reshape(432, 256), cells[...], NT, preferred_element_type=jnp.float32
    )
    taps = products[0:144, 0:1024] + products[144:288, 64:1088] + products[288:432, 128:1152]
    pre = jnp.zeros((16, 1024), jnp.float32)
    for row_tap in range(3):
        line = jnp.zeros((16, 1024), jnp.float32)
        for col_tap in range(3):
            start = (row_tap * 3 + col_tap) * 16
            line += shifted_lanes(taps[start : start + 16], col_tap - 1, 8, 1)
        pre += shifted_lanes(line, row_tap - 1, 8, 8)
    act, slant = both_of(pre)
    small = lax.broadcasted_iota(jnp.int32, (128, 1024), 0)
    cell = lax.broadcasted_iota(jnp.int32, (128, 1024), 1)
    target = (cell >> 7) * 16 + ((cell % 64) >> 4) * 4 + ((cell % 8) >> 1)
    grow = jnp.where(small == target, 1.0, 0.0).astype(jnp.bfloat16)
    cot = gathered[position[0], 128:144, :]
    upstream = jnp.dot(cot, grow, preferred_element_type=jnp.float32)
    high = act.astype(jnp.bfloat16)
    rest = act - high.astype(jnp.float32)
    middle = rest.astype(jnp.bfloat16)
    low = (rest - middle.astype(jnp.float32)).astype(jnp.bfloat16)
    sums = lax.dot_general(
        jnp.concatenate([high, middle, low], axis=0), grow, NT, preferred_element_type=jnp.float32
    )
    next_rows[...] = ((sums[0:16] + sums[16:32] + sums[32:48]) * 0.125).astype(jnp.bfloat16)
    grad = (upstream * slant).astype(jnp.bfloat16).astype(jnp.float32)
    for row_tap in range(3):
        line = shifted_lanes(grad, 1 - row_tap, 8, 8)
        for col_tap in range(3):
            start = (row_tap * 3 + col_tap) * 16
            moved = shifted_lanes(line, 1 - col_tap, 8, 1)
            grads[start : start + 16, :] = moved.astype(jnp.bfloat16)
    for depth_tap in range(3):
        part = jnp.dot(
            grads[...],
            cells[depth_tap * 64 : depth_tap * 64 + 1024, :],
            preferred_element_type=jnp.float32,
        )
        whole[depth_tap * 9 : depth_tap * 9 + 9] = part.astype(jnp.bfloat16).reshape(9, 16, 256)
    whole[27] = whole[26]
    mine[...] = whole[pl.ds(half[0] * HALF_TAPS, HALF_TAPS)]
    theirs[...] = whole[pl.ds((1 - half[0]) * HALF_TAPS, HALF_TAPS)]


def six_own(gathered, kernel, position, half):
    part = shape((HALF_TAPS, 16, 256), jnp.bfloat16)
    return call(
        six_kernel,
        (shape((16, 128), jnp.bfloat16), part, part),
        [
            VMEM((27, 16, 256), jnp.bfloat16),
            VMEM((1152, 256), jnp.bfloat16),
            VMEM((144, 1024), jnp.bfloat16),
            VMEM((28, 16, 256), jnp.bfloat16),
        ],
        (gathered, kernel.reshape(27, 256, 256)),
        (position, half),
        flops=2_000_000_000,
    )


def halves_kernel(half, mine, other, out):
    for step in range(HALF_TAPS):
        for first, part in ((half[0] * HALF_TAPS, mine), ((1 - half[0]) * HALF_TAPS, other)):
            tap = jnp.minimum(first + step, 26)
            out[tap] = part[step].astype(jnp.float32)


def both_halves(half, mine, other):
    return call(
        halves_kernel,
        shape((27,) + mine.shape[1:], jnp.float32),
        [],
        (mine, other),
        (half,),
    )


def pair_perm(first):
    volumes, count = lax.axis_size("dp"), lax.axis_size("wide")
    pairs = []
    for volume in range(volumes):
        for place in range(count):
            other = place + 1 if place % 2 == first else place - 1
            if 0 <= other < count:
                pairs.append((volume * count + place, volume * count + other))
            else:
                pairs.append((volume * count + place, (volume ^ 1) * count + place))
    return pairs


def core_swap(values):
    count = lax.axis_size("dp")
    return lax.ppermute(values, "dp", [(i, i ^ 1) for i in range(count)])


def from_chips(values):
    count = lax.axis_size("dp")
    got = []
    for step in range(1, count // 2):
        pairs = [(i, (i + 2 * step) % count) for i in range(count)]
        got.append(lax.ppermute(values, "dp", pairs))
    return got


def total_of(values, others):
    total = values.astype(jnp.float32)
    for other in others:
        total = total + other.astype(jnp.float32)
    return total


def exchange(values):
    flat = values.reshape(values.shape[0], -1, values.shape[-1])
    got = lax.all_to_all(flat, "wide", split_axis=0, concat_axis=0, tiled=True)
    return got.reshape(values.shape)


def shards(volume, kernel_five, kernel_six, cotangent):
    position = lax.axis_index("wide").astype(jnp.int32).reshape(1)
    half = (lax.axis_index("dp") % 2).astype(jnp.int32).reshape(1)
    odds = lax.ppermute(volume, ("dp", "wide"), pair_perm(1))
    evens = lax.ppermute(volume, ("dp", "wide"), pair_perm(0))
    cot_rows = cotangent.reshape(32, 4, 16)
    part, inner, near_kernel = inner_five(volume, kernel_five)
    message, slope, padded = outer_five(odds, evens, near_kernel, part, inner, cot_rows, position)
    message, position, half, slope, padded = lax.optimization_barrier(
        (message, position, half, slope, padded)
    )
    gathered = exchange(message)
    gathered, position, half, slope, padded = lax.optimization_barrier(
        (gathered, position, half, slope, padded)
    )
    rows, theirs_five = back_five(gathered, kernel_six, slope, padded, position, half)
    got_five = core_swap(theirs_five)
    next_rows, mine_six, theirs_six = six_own(gathered, kernel_six, position, half)
    got_six = core_swap(theirs_six)
    pair_five = mine_of_five(rows, padded, got_five, half)
    pair_five, got_six, mine_six, next_rows = lax.optimization_barrier(
        (pair_five, got_six, mine_six, next_rows)
    )
    pair_six = total_of(mine_six, [got_six]).astype(jnp.bfloat16)
    chips_six = from_chips(pair_six)
    spread = exchange(pair_five)
    total_six = total_of(pair_six, chips_six).astype(jnp.bfloat16)
    out_six = both_halves(half, total_six, core_swap(total_six))
    next_input = next_rows.T.reshape(1, 8, 4, 4, 16)
    spread, out_six, next_input = lax.optimization_barrier((spread, out_six, next_input))
    depth_five = spread.astype(jnp.float32).sum(0).astype(jnp.bfloat16)
    total_five = total_of(depth_five, from_chips(depth_five)).astype(jnp.bfloat16)
    out_five = both_halves(half, total_five, core_swap(total_five))
    out_five = out_five.transpose(0, 2, 1).reshape(3, 3, 3, 128, 16)
    out_six = out_six.transpose(0, 2, 1).reshape(3, 3, 3, 256, 16)
    return (next_input, out_five, out_six)


def solution(mesh):
    in_specs = (P("dp", "wide", None, None, None), P(), P(), P("dp", None, None, None, "wide"))
    out_specs = (
        P("dp", None, None, None, "wide"),
        P(None, None, None, None, "wide"),
        P(None, None, None, None, "wide"),
    )
    return jax.shard_map(shards, mesh=mesh, in_specs=in_specs, out_specs=out_specs, check_vma=False)
```

```python
import jax
import jax.numpy as jnp
from jax import lax
from jax.experimental import pallas as pl
from jax.experimental.pallas import tpu as pltpu
from jax.sharding import PartitionSpec as P

SLOPE = 0.3
HALF_TAPS = 14
VMEM = pltpu.VMEM
NT = (((1,), (1,)), ((), ()))


def both_of(value):
    sigma = 1.0 / (1.0 + jnp.exp(-value))
    act = value * (SLOPE + (1.0 - SLOPE) * sigma)
    slope = 0.125 * SLOPE + (0.125 * (1.0 - SLOPE)) * (sigma + value * sigma * (1.0 - sigma))
    return act, slope


def call(body, out_shape, scratch, operands, scalars=(), flops=0, limit=16, far=(), far_out=False):
    specs = [pl.BlockSpec(memory_space=pltpu.SMEM)] * len(scalars)
    specs += [
        pl.BlockSpec(memory_space=pltpu.HBM if index in far else VMEM)
        for index in range(len(operands))
    ]
    place = pltpu.HBM if far_out else VMEM
    outs = jax.tree.map(lambda _: pl.BlockSpec(memory_space=place), out_shape)
    return pl.pallas_call(
        body,
        out_shape=out_shape,
        in_specs=specs,
        out_specs=outs,
        scratch_shapes=scratch,
        compiler_params=pltpu.CompilerParams(vmem_limit_bytes=int(limit * 1024 * 1024)),
        cost_estimate=pl.CostEstimate(flops=flops, bytes_accessed=4_000_000, transcendentals=0),
    )(*scalars, *operands)


def shape(dims, kind):
    return jax.ShapeDtypeStruct(dims, kind)


def shifted_rows(values, step, period):
    if step == 0:
        return values
    count = values.shape[0]
    column = lax.broadcasted_iota(jnp.int32, values.shape, 0) % period
    rolled = pltpu.roll(values, (-step) % count, 0)
    inside = (column + step >= 0) & (column + step < period)
    return jnp.where(inside, rolled, 0.0)


def columns_of(padded, index, source):
    values = source.astype(jnp.float32)
    padded[index, 0:16, :] = jnp.zeros((16, 384), jnp.bfloat16)
    padded[index, 272:288, :] = jnp.zeros((16, 384), jnp.bfloat16)
    padded[index, 16:272, 0:128] = shifted_rows(values, -1, 16).astype(jnp.bfloat16)
    padded[index, 16:272, 128:256] = source
    padded[index, 16:272, 256:384] = shifted_rows(values, 1, 16).astype(jnp.bfloat16)


def depth_term(padded, first, planes, kernel, depth_tap):
    cells = jnp.concatenate(
        [
            padded[first : first + planes, 16 * row_tap : 16 * row_tap + 256, :].reshape(
                256 * planes, 384
            )
            for row_tap in range(3)
        ],
        axis=1,
    )
    taps = kernel[depth_tap * 1152 : depth_tap * 1152 + 1152, :]
    return jnp.dot(cells, taps, preferred_element_type=jnp.float32)


def rims_kernel(position, slab, for_odds, for_evens, near):
    even = position[0] % 2 == 0
    near[...] = slab[...]
    for_odds[...] = jnp.where(even, slab[0], slab[1])
    for_evens[...] = jnp.where(even, slab[1], slab[0])


def rims_of(slab, position):
    rim = shape((256, 128), jnp.bfloat16)
    near = shape((2, 256, 128), jnp.bfloat16)
    return call(rims_kernel, (rim, rim, near), [], (slab.reshape(2, 256, 128),), (position,))


def inner_kernel(slab, kernel_far, part, padded, kernel, marks):
    loads = {}
    for depth_tap in (1, 2, 0):
        rows = pl.ds(depth_tap * 1152, 1152)
        loads[depth_tap] = pltpu.make_async_copy(
            kernel_far.at[rows], kernel.at[rows], marks.at[depth_tap]
        )
        loads[depth_tap].start()
    for plane in range(2):
        columns_of(padded, plane, slab[plane])
    loads[1].wait()
    for plane in range(2):
        part[plane * 256 : (plane + 1) * 256, :] = depth_term(padded, plane, 1, kernel, 1)
    loads[2].wait()
    part[0:256, :] += depth_term(padded, 1, 1, kernel, 2)
    loads[0].wait()
    part[256:512, :] += depth_term(padded, 0, 1, kernel, 0)


def inner_five(slab, kernel):
    return call(
        inner_kernel,
        (
            shape((512, 256), jnp.float32),
            shape((2, 288, 384), jnp.bfloat16),
            shape((3456, 256), jnp.bfloat16),
        ),
        [pltpu.SemaphoreType.DMA((3,))],
        (slab.reshape(2, 256, 128), kernel.reshape(3456, 256)),
        flops=600_000_000,
        limit=51,
        far=(1,),
    )


def outer_kernel(position, odds, evens, kernel, part, inner, cot, message, slope, padded, tall):
    even = position[0] % 2 == 0
    blank = jnp.zeros((256, 128), jnp.bfloat16)
    low = jnp.where(even, odds[...], evens[...])
    high = jnp.where(even, evens[...], odds[...])
    columns_of(padded, 0, jnp.where(position[0] == 0, blank, low))
    columns_of(padded, 3, jnp.where(position[0] == 15, blank, high))
    padded[1:3] = inner[...]
    acts = []
    for plane in range(2):
        total = part[plane * 256 : (plane + 1) * 256, :]
        total += depth_term(padded, 3 * plane, 1, kernel, 2 * plane)
        act, slant = both_of(total)
        slope[plane * 256 : (plane + 1) * 256, :] = slant
        acts.append(act)
    two = (acts[0] + acts[1]).reshape(8, 2, 16, 256)
    pairs = (two[:, 0] + two[:, 1]).reshape(128, 256)
    pooled = []
    for side in range(2):
        tall[side] = pairs[:, side * 128 : (side + 1) * 128]
        even = tall[side, pl.ds(0, 64, stride=2), :]
        odd = tall[side, pl.ds(1, 64, stride=2), :]
        pooled.append(((even + odd) * 0.125).astype(jnp.bfloat16))
    cells = cot[...].astype(jnp.float32).reshape(128, 16)
    same = lax.broadcasted_iota(jnp.int32, (16, 16), 0) == lax.broadcasted_iota(
        jnp.int32, (16, 16), 1
    )
    unit = jnp.where(same, 1.0, 0.0)
    marks = lax.dot_general(
        unit.astype(jnp.bfloat16),
        cells.astype(jnp.bfloat16),
        NT,
        preferred_element_type=jnp.float32,
    ).astype(jnp.bfloat16)
    for target in range(16):
        message[target, 0:64, :] = pooled[0]
        message[target, 64:128, :] = pooled[1]
        message[target, 128:144, :] = marks


def outer_five(odds, evens, kernel, part, inner, cot_rows, position):
    return call(
        outer_kernel,
        (
            shape((16, 144, 128), jnp.bfloat16),
            shape((512, 256), jnp.float32),
            shape((4, 288, 384), jnp.bfloat16),
        ),
        [VMEM((2, 128, 128), jnp.float32)],
        (
            odds,
            evens,
            kernel,
            part,
            inner,
            cot_rows,
        ),
        (position,),
        flops=300_000_000,
    )


def six_to_five(position, gathered, kernel, slope, rows_out, near, tall):
    for plane in range(5):
        where = position[0] + (plane - 2)
        inside = (where >= 0) & (where < 16)
        index = jnp.clip(where, 0, 15)
        left = gathered[index, 0:64, :]
        right = gathered[index, 64:128, :]
        values = jnp.concatenate([left, right], axis=1).astype(jnp.float32)
        values = jnp.where(inside, values, 0.0)
        blank = jnp.zeros((8, 256), jnp.float32)
        for col_tap in range(3):
            moved = shifted_rows(values, col_tap - 1, 8)
            for row_tap in range(3):
                if row_tap == 0:
                    cells = jnp.concatenate([blank, moved[:56]], axis=0)
                elif row_tap == 1:
                    cells = moved
                else:
                    cells = jnp.concatenate([moved[8:], blank], axis=0)
                lane = (row_tap * 3 + col_tap) * 256
                near[plane, :, lane : lane + 256] = cells.astype(jnp.bfloat16)
    pre_six = jnp.zeros((192, 256), jnp.float32)
    for depth_tap in range(3):
        taps = kernel[depth_tap * 9 : depth_tap * 9 + 9].reshape(2304, 256)
        cells = near[depth_tap : depth_tap + 3].reshape(192, 2304)
        pre_six += jnp.dot(cells, taps, preferred_element_type=jnp.float32)
    _, slant = both_of(pre_six)
    cell = lax.broadcasted_iota(jnp.int32, (192, 128), 0)
    lanes = lax.broadcasted_iota(jnp.int32, (192, 128), 1)
    depth = cell // 64 + position[0] - 1
    small = (depth >> 1) * 16 + ((cell % 64) >> 4) * 4 + ((cell % 8) >> 1)
    hit = (small == lanes) & (depth >= 0) & (depth < 16)
    grow = jnp.where(hit, 1.0, 0.0).astype(jnp.bfloat16)
    cot = gathered[:, 128:144, :].reshape(256, 128)
    upstream = lax.dot_general(grow, cot, NT, preferred_element_type=jnp.float32)
    grad_six = (upstream * slant).astype(jnp.bfloat16).astype(jnp.float32)
    blank = jnp.zeros((8, 256), jnp.float32)
    for depth_tap in range(3):
        values = grad_six[(2 - depth_tap) * 64 : (3 - depth_tap) * 64]
        for col_tap in range(3):
            moved = shifted_rows(values, 1 - col_tap, 8)
            for row_tap in range(3):
                if row_tap == 0:
                    cells = jnp.concatenate([moved[8:], blank], axis=0)
                elif row_tap == 1:
                    cells = moved
                else:
                    cells = jnp.concatenate([blank, moved[:56]], axis=0)
                lane = (row_tap * 3 + col_tap) * 256
                near[depth_tap, :, lane : lane + 256] = cells.astype(jnp.bfloat16)

    def depth_of(depth_tap, total):
        for tap in range(9):
            total += lax.dot_general(
                near[depth_tap, :, tap * 256 : tap * 256 + 256],
                kernel[depth_tap * 9 + tap],
                NT,
                preferred_element_type=jnp.float32,
            )
        return total

    grad_pooled = lax.fori_loop(0, 3, depth_of, jnp.zeros((64, 256), jnp.float32))
    for side in range(2):
        tall[side, pl.ds(0, 64, stride=2), :] = grad_pooled[:, side * 128 : (side + 1) * 128]
        tall[side, pl.ds(1, 64, stride=2), :] = grad_pooled[:, side * 128 : (side + 1) * 128]
    both = jnp.concatenate([tall[0], tall[1]], axis=1)
    wide = jnp.broadcast_to(both.reshape(8, 1, 16, 256), (8, 2, 16, 256)).reshape(256, 256)
    for plane in range(2):
        grad = wide * slope[plane * 256 : (plane + 1) * 256, :]
        rows_out[:, plane * 256 : (plane + 1) * 256] = grad.T.astype(jnp.bfloat16)


def tap_cells(padded, plane, tap):
    depth_tap, row_tap, col_tap = tap // 9, (tap // 3) % 3, tap % 3
    return padded[
        plane + depth_tap,
        pl.ds(pl.multiple_of(row_tap * 16, 16), 256),
        pl.ds(pl.multiple_of(col_tap * 128, 128), 128),
    ]


def half_of_five(first, rows, padded, out, got=None, send=None):
    for step in range(0, HALF_TAPS, 2):
        taps = [jnp.minimum(first + step + other, 26) for other in range(2)]
        total = jnp.zeros((256, 256), jnp.float32)
        for plane in range(2):
            cells = jnp.concatenate([tap_cells(padded, plane, tap) for tap in taps], axis=1)
            total += jnp.dot(
                rows[:, plane * 256 : (plane + 1) * 256],
                cells,
                preferred_element_type=jnp.float32,
            )
        for other in range(2):
            part = total[:, other * 128 : (other + 1) * 128]
            if got is not None:
                part += got[:, step + other].reshape(256, 128).astype(jnp.float32)
            out[:, step + other] = part.astype(jnp.bfloat16).reshape(16, 16, 128)
        if send is not None:
            send(step)


def back_kernel(position, half, gathered, kernel, slope, padded, rows, theirs, near, tall):
    six_to_five(position, gathered, kernel, slope, rows, near, tall)
    half_of_five((1 - half[0]) * HALF_TAPS, rows, padded, theirs)


def back_five(gathered, kernel, slope, padded, position, half):
    return call(
        back_kernel,
        (shape((256, 512), jnp.bfloat16), shape((16, HALF_TAPS, 16, 128), jnp.bfloat16)),
        [VMEM((5, 64, 2304), jnp.bfloat16), VMEM((2, 128, 128), jnp.float32)],
        (gathered, kernel.reshape(27, 256, 256), slope, padded),
        (position, half),
        flops=3_000_000_000,
    )


def mine_kernel(half, rows, padded, got, mine, staged, marks):
    sends = []

    def send(step):
        pair = pl.ds(step, 2)
        sends.append(
            pltpu.make_async_copy(staged.at[:, pair], mine.at[:, pair], marks.at[step // 2])
        )
        sends[-1].start()

    half_of_five(half[0] * HALF_TAPS, rows, padded, staged, got, send)
    for copy in sends:
        copy.wait()


def mine_of_five(rows, padded, got, half):
    return call(
        mine_kernel,
        shape((16, HALF_TAPS, 16, 128), jnp.bfloat16),
        [
            VMEM((16, HALF_TAPS, 16, 128), jnp.bfloat16),
            pltpu.SemaphoreType.DMA((HALF_TAPS // 2,)),
        ],
        (rows, padded, got),
        (half,),
        flops=900_000_000,
        far_out=True,
    )


def shifted_lanes(values, step, period, inner):
    if step == 0:
        return values
    count = values.shape[1]
    place = (lax.broadcasted_iota(jnp.int32, values.shape, 1) // inner) % period
    rolled = pltpu.roll(values, (-step * inner) % count, 1)
    inside = (place + step >= 0) & (place + step < period)
    return jnp.where(inside, rolled, 0.0)


def six_kernel(
    position, half, gathered, kernel, next_rows, mine, theirs, own, cells, grads, whole
):
    rows = lax.broadcasted_iota(jnp.int32, (16, 256), 0) + position[0] * 16
    lanes = lax.broadcasted_iota(jnp.int32, (16, 256), 1)
    pick = jnp.where(rows == lanes, 1.0, 0.0).astype(jnp.bfloat16)
    for tap in range(27):
        chosen = lax.dot_general(pick, kernel[tap], NT, preferred_element_type=jnp.float32)
        own[tap] = chosen.astype(jnp.bfloat16)
    blank = jnp.zeros((64, 256), jnp.bfloat16)
    cells[0:64, :] = blank
    cells[1088:1152, :] = blank
    cells[64:1088, 0:128] = gathered[:, 0:64, :].reshape(1024, 128)
    cells[64:1088, 128:256] = gathered[:, 64:128, :].reshape(1024, 128)
    products = lax.dot_general(
        own[...].reshape(432, 256), cells[...], NT, preferred_element_type=jnp.float32
    )
    taps = products[0:144, 0:1024] + products[144:288, 64:1088] + products[288:432, 128:1152]
    pre = jnp.zeros((16, 1024), jnp.float32)
    for row_tap in range(3):
        line = jnp.zeros((16, 1024), jnp.float32)
        for col_tap in range(3):
            start = (row_tap * 3 + col_tap) * 16
            line += shifted_lanes(taps[start : start + 16], col_tap - 1, 8, 1)
        pre += shifted_lanes(line, row_tap - 1, 8, 8)
    act, slant = both_of(pre)
    small = lax.broadcasted_iota(jnp.int32, (128, 1024), 0)
    cell = lax.broadcasted_iota(jnp.int32, (128, 1024), 1)
    target = (cell >> 7) * 16 + ((cell % 64) >> 4) * 4 + ((cell % 8) >> 1)
    grow = jnp.where(small == target, 1.0, 0.0).astype(jnp.bfloat16)
    cot = gathered[position[0], 128:144, :]
    upstream = jnp.dot(cot, grow, preferred_element_type=jnp.float32)
    high = act.astype(jnp.bfloat16)
    rest = act - high.astype(jnp.float32)
    middle = rest.astype(jnp.bfloat16)
    low = (rest - middle.astype(jnp.float32)).astype(jnp.bfloat16)
    sums = lax.dot_general(
        jnp.concatenate([high, middle, low], axis=0), grow, NT, preferred_element_type=jnp.float32
    )
    next_rows[...] = ((sums[0:16] + sums[16:32] + sums[32:48]) * 0.125).astype(jnp.bfloat16)
    grad = (upstream * slant).astype(jnp.bfloat16).astype(jnp.float32)
    for row_tap in range(3):
        line = shifted_lanes(grad, 1 - row_tap, 8, 8)
        for col_tap in range(3):
            start = (row_tap * 3 + col_tap) * 16
            moved = shifted_lanes(line, 1 - col_tap, 8, 1)
            grads[start : start + 16, :] = moved.astype(jnp.bfloat16)
    for depth_tap in range(3):
        part = jnp.dot(
            grads[...],
            cells[depth_tap * 64 : depth_tap * 64 + 1024, :],
            preferred_element_type=jnp.float32,
        )
        whole[depth_tap * 9 : depth_tap * 9 + 9] = part.astype(jnp.bfloat16).reshape(9, 16, 256)
    whole[27] = whole[26]
    mine[...] = whole[pl.ds(half[0] * HALF_TAPS, HALF_TAPS)]
    theirs[...] = whole[pl.ds((1 - half[0]) * HALF_TAPS, HALF_TAPS)]


def six_own(gathered, kernel, position, half):
    part = shape((HALF_TAPS, 16, 256), jnp.bfloat16)
    return call(
        six_kernel,
        (shape((16, 128), jnp.bfloat16), part, part),
        [
            VMEM((27, 16, 256), jnp.bfloat16),
            VMEM((1152, 256), jnp.bfloat16),
            VMEM((144, 1024), jnp.bfloat16),
            VMEM((28, 16, 256), jnp.bfloat16),
        ],
        (gathered, kernel.reshape(27, 256, 256)),
        (position, half),
        flops=2_000_000_000,
    )


def halves_kernel(half, mine, other, out):
    for step in range(HALF_TAPS):
        for first, part in ((half[0] * HALF_TAPS, mine), ((1 - half[0]) * HALF_TAPS, other)):
            tap = jnp.minimum(first + step, 26)
            out[tap] = part[step].astype(jnp.float32)


def both_halves(half, mine, other):
    return call(
        halves_kernel,
        shape((27,) + mine.shape[1:], jnp.float32),
        [],
        (mine, other),
        (half,),
    )


def pair_perm(first):
    volumes, count = lax.axis_size("dp"), lax.axis_size("wide")
    pairs = []
    for volume in range(volumes):
        for place in range(count):
            other = place + 1 if place % 2 == first else place - 1
            if 0 <= other < count:
                pairs.append((volume * count + place, volume * count + other))
            else:
                pairs.append((volume * count + place, (volume ^ 1) * count + place))
    return pairs


def core_swap(values):
    count = lax.axis_size("dp")
    return lax.ppermute(values, "dp", [(i, i ^ 1) for i in range(count)])


def from_chips(values):
    count = lax.axis_size("dp")
    return [
        lax.ppermute(values, "dp", [(i, i ^ step) for i in range(count)]) for step in (2, 6, 4)
    ]


def sum_of_chips(values, others):
    beside, across, ahead = [other.astype(jnp.float32) for other in others]
    return ((values.astype(jnp.float32) + beside) + (across + ahead)).astype(jnp.bfloat16)


def exchange(values):
    flat = values.reshape(values.shape[0], -1, values.shape[-1])
    got = lax.all_to_all(flat, "wide", split_axis=0, concat_axis=0, tiled=True)
    return got.reshape(values.shape)


def shards(volume, kernel_five, kernel_six, cotangent):
    position = lax.axis_index("wide").astype(jnp.int32).reshape(1)
    half = (lax.axis_index("dp") % 2).astype(jnp.int32).reshape(1)
    for_odds, for_evens, near_slab = rims_of(volume, position)
    odds = lax.ppermute(for_odds, ("dp", "wide"), pair_perm(1))
    evens = lax.ppermute(for_evens, ("dp", "wide"), pair_perm(0))
    cot_rows = cotangent.reshape(32, 4, 16)
    part, inner, near_kernel = inner_five(near_slab, kernel_five)
    message, slope, padded = outer_five(odds, evens, near_kernel, part, inner, cot_rows, position)
    message, position, half, slope, padded = lax.optimization_barrier(
        (message, position, half, slope, padded)
    )
    gathered = exchange(message)
    gathered, position, half, slope, padded = lax.optimization_barrier(
        (gathered, position, half, slope, padded)
    )
    rows, theirs_five = back_five(gathered, kernel_six, slope, padded, position, half)
    got_five = core_swap(theirs_five)
    next_rows, mine_six, theirs_six = six_own(gathered, kernel_six, position, half)
    got_six = core_swap(theirs_six)
    pair_five = mine_of_five(rows, padded, got_five, half)
    pair_five, got_six, mine_six, next_rows = lax.optimization_barrier(
        (pair_five, got_six, mine_six, next_rows)
    )
    pair_six = (mine_six.astype(jnp.float32) + got_six.astype(jnp.float32)).astype(jnp.bfloat16)
    chips_six = from_chips(pair_six)
    spread = exchange(pair_five)
    total_six = sum_of_chips(pair_six, chips_six)
    out_six = both_halves(half, total_six, core_swap(total_six))
    next_input = next_rows.T.reshape(1, 8, 4, 4, 16)
    spread, out_six, next_input = lax.optimization_barrier((spread, out_six, next_input))
    depth_five = spread.astype(jnp.float32).sum(0).astype(jnp.bfloat16)
    total_five = sum_of_chips(depth_five, from_chips(depth_five))
    out_five = both_halves(half, total_five, core_swap(total_five))
    out_five = out_five.transpose(0, 2, 1).reshape(3, 3, 3, 128, 16)
    out_six = out_six.transpose(0, 2, 1).reshape(3, 3, 3, 256, 16)
    return (next_input, out_five, out_six)


def solution(mesh):
    in_specs = (P("dp", "wide", None, None, None), P(), P(), P("dp", None, None, None, "wide"))
    out_specs = (
        P("dp", None, None, None, "wide"),
        P(None, None, None, None, "wide"),
        P(None, None, None, None, "wide"),
    )
    return jax.shard_map(shards, mesh=mesh, in_specs=in_specs, out_specs=out_specs, check_vma=False)
```

```python
import jax
import jax.numpy as jnp
from jax import lax
from jax.experimental import pallas as pl
from jax.experimental.pallas import tpu as pltpu
from jax.sharding import PartitionSpec as P

SLOPE = 0.3
HALF_TAPS = 14
VMEM = pltpu.VMEM
NT = (((1,), (1,)), ((), ()))


def both_of(value):
    sigma = 1.0 / (1.0 + jnp.exp(-value))
    act = value * (SLOPE + (1.0 - SLOPE) * sigma)
    slope = 0.125 * SLOPE + (0.125 * (1.0 - SLOPE)) * (sigma + value * sigma * (1.0 - sigma))
    return act, slope


def call(body, out_shape, scratch, operands, scalars=(), flops=0, limit=16, far=(), far_out=False):
    specs = [pl.BlockSpec(memory_space=pltpu.SMEM)] * len(scalars)
    specs += [
        pl.BlockSpec(memory_space=pltpu.HBM if index in far else VMEM)
        for index in range(len(operands))
    ]
    place = pltpu.HBM if far_out else VMEM
    outs = jax.tree.map(lambda _: pl.BlockSpec(memory_space=place), out_shape)
    return pl.pallas_call(
        body,
        out_shape=out_shape,
        in_specs=specs,
        out_specs=outs,
        scratch_shapes=scratch,
        compiler_params=pltpu.CompilerParams(vmem_limit_bytes=int(limit * 1024 * 1024)),
        cost_estimate=pl.CostEstimate(flops=flops, bytes_accessed=4_000_000, transcendentals=0),
    )(*scalars, *operands)


def shape(dims, kind):
    return jax.ShapeDtypeStruct(dims, kind)


def shifted_rows(values, step, period):
    if step == 0:
        return values
    count = values.shape[0]
    column = lax.broadcasted_iota(jnp.int32, values.shape, 0) % period
    rolled = pltpu.roll(values, (-step) % count, 0)
    inside = (column + step >= 0) & (column + step < period)
    return jnp.where(inside, rolled, 0.0)


def columns_of(padded, index, source):
    values = source.astype(jnp.float32)
    padded[index, 0:16, :] = jnp.zeros((16, 384), jnp.bfloat16)
    padded[index, 272:288, :] = jnp.zeros((16, 384), jnp.bfloat16)
    padded[index, 16:272, 0:128] = shifted_rows(values, -1, 16).astype(jnp.bfloat16)
    padded[index, 16:272, 128:256] = source
    padded[index, 16:272, 256:384] = shifted_rows(values, 1, 16).astype(jnp.bfloat16)


def depth_term(padded, first, planes, kernel, depth_tap):
    cells = jnp.concatenate(
        [
            padded[first : first + planes, 16 * row_tap : 16 * row_tap + 256, :].reshape(
                256 * planes, 384
            )
            for row_tap in range(3)
        ],
        axis=1,
    )
    taps = kernel[depth_tap * 1152 : depth_tap * 1152 + 1152, :]
    return jnp.dot(cells, taps, preferred_element_type=jnp.float32)


def rims_kernel(position, slab, for_odds, for_evens, near):
    even = position[0] % 2 == 0
    near[...] = slab[...]
    for_odds[...] = jnp.where(even, slab[0], slab[1])
    for_evens[...] = jnp.where(even, slab[1], slab[0])


def rims_of(slab, position):
    rim = shape((256, 128), jnp.bfloat16)
    near = shape((2, 256, 128), jnp.bfloat16)
    return call(rims_kernel, (rim, rim, near), [], (slab.reshape(2, 256, 128),), (position,))


def inner_kernel(slab, kernel_far, part, padded, kernel, marks):
    loads = {}
    for depth_tap in (1, 2, 0):
        rows = pl.ds(depth_tap * 1152, 1152)
        loads[depth_tap] = pltpu.make_async_copy(
            kernel_far.at[rows], kernel.at[rows], marks.at[depth_tap]
        )
        loads[depth_tap].start()
    for plane in range(2):
        columns_of(padded, plane, slab[plane])
    loads[1].wait()
    for plane in range(2):
        part[plane * 256 : (plane + 1) * 256, :] = depth_term(padded, plane, 1, kernel, 1)
    loads[2].wait()
    part[0:256, :] += depth_term(padded, 1, 1, kernel, 2)
    loads[0].wait()
    part[256:512, :] += depth_term(padded, 0, 1, kernel, 0)


def inner_five(slab, kernel):
    return call(
        inner_kernel,
        (
            shape((512, 256), jnp.float32),
            shape((2, 288, 384), jnp.bfloat16),
            shape((3456, 256), jnp.bfloat16),
        ),
        [pltpu.SemaphoreType.DMA((3,))],
        (slab.reshape(2, 256, 128), kernel.reshape(3456, 256)),
        flops=600_000_000,
        limit=51,
        far=(1,),
    )


def outer_kernel(position, odds, evens, kernel, part, inner, cot, message, slope, padded, tall):
    even = position[0] % 2 == 0
    blank = jnp.zeros((256, 128), jnp.bfloat16)
    low = jnp.where(even, odds[...], evens[...])
    high = jnp.where(even, evens[...], odds[...])
    columns_of(padded, 0, jnp.where(position[0] == 0, blank, low))
    columns_of(padded, 3, jnp.where(position[0] == 15, blank, high))
    padded[1:3] = inner[...]
    acts = []
    for plane in range(2):
        total = part[plane * 256 : (plane + 1) * 256, :]
        total += depth_term(padded, 3 * plane, 1, kernel, 2 * plane)
        act, slant = both_of(total)
        slope[plane * 256 : (plane + 1) * 256, :] = slant
        acts.append(act)
    two = (acts[0] + acts[1]).reshape(8, 2, 16, 256)
    pairs = (two[:, 0] + two[:, 1]).reshape(128, 256)
    pooled = []
    for side in range(2):
        tall[side] = pairs[:, side * 128 : (side + 1) * 128]
        even = tall[side, pl.ds(0, 64, stride=2), :]
        odd = tall[side, pl.ds(1, 64, stride=2), :]
        pooled.append(((even + odd) * 0.125).astype(jnp.bfloat16))
    cells = cot[...].astype(jnp.float32).reshape(128, 16)
    same = lax.broadcasted_iota(jnp.int32, (16, 16), 0) == lax.broadcasted_iota(
        jnp.int32, (16, 16), 1
    )
    unit = jnp.where(same, 1.0, 0.0)
    marks = lax.dot_general(
        unit.astype(jnp.bfloat16),
        cells.astype(jnp.bfloat16),
        NT,
        preferred_element_type=jnp.float32,
    ).astype(jnp.bfloat16)
    for target in range(16):
        message[target, 0:64, :] = pooled[0]
        message[target, 64:128, :] = pooled[1]
        message[target, 128:144, :] = marks


def outer_five(odds, evens, kernel, part, inner, cot_rows, position):
    return call(
        outer_kernel,
        (
            shape((16, 144, 128), jnp.bfloat16),
            shape((512, 256), jnp.float32),
            shape((4, 288, 384), jnp.bfloat16),
        ),
        [VMEM((2, 128, 128), jnp.float32)],
        (
            odds,
            evens,
            kernel,
            part,
            inner,
            cot_rows,
        ),
        (position,),
        flops=300_000_000,
    )


def six_to_five(position, gathered, kernel, slope, rows_out, own, near, tall):
    for plane in range(5):
        where = position[0] + (plane - 2)
        inside = (where >= 0) & (where < 16)
        index = jnp.clip(where, 0, 15)
        left = gathered[index, 0:64, :]
        right = gathered[index, 64:128, :]
        values = jnp.concatenate([left, right], axis=1).astype(jnp.float32)
        values = jnp.where(inside, values, 0.0)
        blank = jnp.zeros((8, 256), jnp.float32)
        for col_tap in range(3):
            moved = shifted_rows(values, col_tap - 1, 8)
            for row_tap in range(3):
                if row_tap == 0:
                    cells = jnp.concatenate([blank, moved[:56]], axis=0)
                elif row_tap == 1:
                    cells = moved
                else:
                    cells = jnp.concatenate([moved[8:], blank], axis=0)
                lane = (row_tap * 3 + col_tap) * 256
                near[plane, :, lane : lane + 256] = cells.astype(jnp.bfloat16)
    pre_six = jnp.zeros((192, 256), jnp.float32)
    for depth_tap in range(3):
        taps = kernel[depth_tap * 9 : depth_tap * 9 + 9].reshape(2304, 256)
        cells = near[depth_tap : depth_tap + 3].reshape(192, 2304)
        pre_six += jnp.dot(cells, taps, preferred_element_type=jnp.float32)
    _, slant = both_of(pre_six)
    cell = lax.broadcasted_iota(jnp.int32, (192, 128), 0)
    lanes = lax.broadcasted_iota(jnp.int32, (192, 128), 1)
    depth = cell // 64 + position[0] - 1
    small = (depth >> 1) * 16 + ((cell % 64) >> 4) * 4 + ((cell % 8) >> 1)
    hit = (small == lanes) & (depth >= 0) & (depth < 16)
    grow = jnp.where(hit, 1.0, 0.0).astype(jnp.bfloat16)
    cot = gathered[:, 128:144, :].reshape(256, 128)
    upstream = lax.dot_general(grow, cot, NT, preferred_element_type=jnp.float32)
    grad_six = (upstream * slant).astype(jnp.bfloat16).astype(jnp.float32)
    blank = jnp.zeros((8, 256), jnp.float32)
    for depth_tap in range(3):
        values = grad_six[(2 - depth_tap) * 64 : (3 - depth_tap) * 64]
        for col_tap in range(3):
            moved = shifted_rows(values, 1 - col_tap, 8)
            for row_tap in range(3):
                if row_tap == 0:
                    cells = jnp.concatenate([moved[8:], blank], axis=0)
                elif row_tap == 1:
                    cells = moved
                else:
                    cells = jnp.concatenate([blank, moved[:56]], axis=0)
                lane = (row_tap * 3 + col_tap) * 256
                near[depth_tap, :, lane : lane + 256] = cells.astype(jnp.bfloat16)

    filters = lax.broadcasted_iota(jnp.int32, (16, 256), 0) + position[0] * 16
    lanes = lax.broadcasted_iota(jnp.int32, (16, 256), 1)
    pick = jnp.where(filters == lanes, 1.0, 0.0).astype(jnp.bfloat16)

    def depth_of(depth_tap, total):
        for tap in range(9):
            both = lax.dot_general(
                jnp.concatenate([near[depth_tap, :, tap * 256 : tap * 256 + 256], pick], axis=0),
                kernel[depth_tap * 9 + tap],
                NT,
                preferred_element_type=jnp.float32,
            )
            total += both[:64]
            own[depth_tap * 9 + tap] = both[64:].astype(jnp.bfloat16)
        return total

    grad_pooled = lax.fori_loop(0, 3, depth_of, jnp.zeros((64, 256), jnp.float32))
    for side in range(2):
        tall[side, pl.ds(0, 64, stride=2), :] = grad_pooled[:, side * 128 : (side + 1) * 128]
        tall[side, pl.ds(1, 64, stride=2), :] = grad_pooled[:, side * 128 : (side + 1) * 128]
    both = jnp.concatenate([tall[0], tall[1]], axis=1)
    wide = jnp.broadcast_to(both.reshape(8, 1, 16, 256), (8, 2, 16, 256)).reshape(256, 256)
    for plane in range(2):
        grad = wide * slope[plane * 256 : (plane + 1) * 256, :]
        rows_out[:, plane * 256 : (plane + 1) * 256] = grad.T.astype(jnp.bfloat16)


def tap_cells(padded, plane, tap):
    depth_tap, row_tap, col_tap = tap // 9, (tap // 3) % 3, tap % 3
    return padded[
        plane + depth_tap,
        pl.ds(pl.multiple_of(row_tap * 16, 16), 256),
        pl.ds(pl.multiple_of(col_tap * 128, 128), 128),
    ]


def half_of_five(first, rows, padded, out, got=None, send=None):
    for step in range(0, HALF_TAPS, 2):
        taps = [jnp.minimum(first + step + other, 26) for other in range(2)]
        total = jnp.zeros((256, 256), jnp.float32)
        for plane in range(2):
            cells = jnp.concatenate([tap_cells(padded, plane, tap) for tap in taps], axis=1)
            total += jnp.dot(
                rows[:, plane * 256 : (plane + 1) * 256],
                cells,
                preferred_element_type=jnp.float32,
            )
        for other in range(2):
            part = total[:, other * 128 : (other + 1) * 128]
            if got is not None:
                part += got[:, step + other].reshape(256, 128).astype(jnp.float32)
            out[:, step + other] = part.astype(jnp.bfloat16).reshape(16, 16, 128)
        if send is not None:
            send(step)


def back_kernel(
    position, half, gathered, kernel, slope, padded, rows, theirs, own, near, tall
):
    six_to_five(position, gathered, kernel, slope, rows, own, near, tall)
    half_of_five((1 - half[0]) * HALF_TAPS, rows, padded, theirs)


def back_five(gathered, kernel, slope, padded, position, half):
    return call(
        back_kernel,
        (
            shape((256, 512), jnp.bfloat16),
            shape((16, HALF_TAPS, 16, 128), jnp.bfloat16),
            shape((27, 16, 256), jnp.bfloat16),
        ),
        [VMEM((5, 64, 2304), jnp.bfloat16), VMEM((2, 128, 128), jnp.float32)],
        (gathered, kernel.reshape(27, 256, 256), slope, padded),
        (position, half),
        flops=3_000_000_000,
    )


def mine_kernel(half, rows, padded, got, mine, staged, marks):
    sends = []

    def send(step):
        pair = pl.ds(step, 2)
        sends.append(
            pltpu.make_async_copy(staged.at[:, pair], mine.at[:, pair], marks.at[step // 2])
        )
        sends[-1].start()

    half_of_five(half[0] * HALF_TAPS, rows, padded, staged, got, send)
    for copy in sends:
        copy.wait()


def mine_of_five(rows, padded, got, half):
    return call(
        mine_kernel,
        shape((16, HALF_TAPS, 16, 128), jnp.bfloat16),
        [
            VMEM((16, HALF_TAPS, 16, 128), jnp.bfloat16),
            pltpu.SemaphoreType.DMA((HALF_TAPS // 2,)),
        ],
        (rows, padded, got),
        (half,),
        flops=900_000_000,
        far_out=True,
    )


def shifted_lanes(values, step, period, inner):
    if step == 0:
        return values
    count = values.shape[1]
    place = (lax.broadcasted_iota(jnp.int32, values.shape, 1) // inner) % period
    rolled = pltpu.roll(values, (-step * inner) % count, 1)
    inside = (place + step >= 0) & (place + step < period)
    return jnp.where(inside, rolled, 0.0)


def six_kernel(
    position, half, gathered, own, next_rows, mine, theirs, cells, grads, whole
):
    blank = jnp.zeros((64, 256), jnp.bfloat16)
    cells[0:64, :] = blank
    cells[1088:1152, :] = blank
    cells[64:1088, 0:128] = gathered[:, 0:64, :].reshape(1024, 128)
    cells[64:1088, 128:256] = gathered[:, 64:128, :].reshape(1024, 128)
    products = lax.dot_general(
        own[...].reshape(432, 256), cells[...], NT, preferred_element_type=jnp.float32
    )
    taps = products[0:144, 0:1024] + products[144:288, 64:1088] + products[288:432, 128:1152]
    pre = jnp.zeros((16, 1024), jnp.float32)
    for row_tap in range(3):
        line = jnp.zeros((16, 1024), jnp.float32)
        for col_tap in range(3):
            start = (row_tap * 3 + col_tap) * 16
            line += shifted_lanes(taps[start : start + 16], col_tap - 1, 8, 1)
        pre += shifted_lanes(line, row_tap - 1, 8, 8)
    act, slant = both_of(pre)
    small = lax.broadcasted_iota(jnp.int32, (128, 1024), 0)
    cell = lax.broadcasted_iota(jnp.int32, (128, 1024), 1)
    target = (cell >> 7) * 16 + ((cell % 64) >> 4) * 4 + ((cell % 8) >> 1)
    grow = jnp.where(small == target, 1.0, 0.0).astype(jnp.bfloat16)
    cot = gathered[position[0], 128:144, :]
    upstream = jnp.dot(cot, grow, preferred_element_type=jnp.float32)
    high = act.astype(jnp.bfloat16)
    rest = act - high.astype(jnp.float32)
    middle = rest.astype(jnp.bfloat16)
    low = (rest - middle.astype(jnp.float32)).astype(jnp.bfloat16)
    sums = lax.dot_general(
        jnp.concatenate([high, middle, low], axis=0), grow, NT, preferred_element_type=jnp.float32
    )
    next_rows[...] = ((sums[0:16] + sums[16:32] + sums[32:48]) * 0.125).astype(jnp.bfloat16)
    grad = (upstream * slant).astype(jnp.bfloat16).astype(jnp.float32)
    for row_tap in range(3):
        line = shifted_lanes(grad, 1 - row_tap, 8, 8)
        for col_tap in range(3):
            start = (row_tap * 3 + col_tap) * 16
            moved = shifted_lanes(line, 1 - col_tap, 8, 1)
            grads[start : start + 16, :] = moved.astype(jnp.bfloat16)
    for depth_tap in range(3):
        part = jnp.dot(
            grads[...],
            cells[depth_tap * 64 : depth_tap * 64 + 1024, :],
            preferred_element_type=jnp.float32,
        )
        whole[depth_tap * 9 : depth_tap * 9 + 9] = part.astype(jnp.bfloat16).reshape(9, 16, 256)
    whole[27] = whole[26]
    mine[...] = whole[pl.ds(half[0] * HALF_TAPS, HALF_TAPS)]
    theirs[...] = whole[pl.ds((1 - half[0]) * HALF_TAPS, HALF_TAPS)]


def six_own(gathered, own, position, half):
    part = shape((HALF_TAPS, 16, 256), jnp.bfloat16)
    return call(
        six_kernel,
        (shape((16, 128), jnp.bfloat16), part, part),
        [
            VMEM((1152, 256), jnp.bfloat16),
            VMEM((144, 1024), jnp.bfloat16),
            VMEM((28, 16, 256), jnp.bfloat16),
        ],
        (gathered, own),
        (position, half),
        flops=2_000_000_000,
    )


def halves_kernel(half, mine, other, out):
    for step in range(HALF_TAPS):
        for first, part in ((half[0] * HALF_TAPS, mine), ((1 - half[0]) * HALF_TAPS, other)):
            tap = jnp.minimum(first + step, 26)
            out[tap] = part[step].astype(jnp.float32)


def both_halves(half, mine, other):
    return call(
        halves_kernel,
        shape((27,) + mine.shape[1:], jnp.float32),
        [],
        (mine, other),
        (half,),
    )


def pair_perm(first):
    volumes, count = lax.axis_size("dp"), lax.axis_size("wide")
    pairs = []
    for volume in range(volumes):
        for place in range(count):
            other = place + 1 if place % 2 == first else place - 1
            if 0 <= other < count:
                pairs.append((volume * count + place, volume * count + other))
            else:
                pairs.append((volume * count + place, (volume ^ 1) * count + place))
    return pairs


def core_swap(values):
    count = lax.axis_size("dp")
    return lax.ppermute(values, "dp", [(i, i ^ 1) for i in range(count)])


def from_chips(values):
    count = lax.axis_size("dp")
    return [
        lax.ppermute(values, "dp", [(i, i ^ step) for i in range(count)]) for step in (2, 6, 4)
    ]


def sum_of_chips(values, others):
    beside, across, ahead = [other.astype(jnp.float32) for other in others]
    return ((values.astype(jnp.float32) + beside) + (across + ahead)).astype(jnp.bfloat16)


def exchange(values):
    flat = values.reshape(values.shape[0], -1, values.shape[-1])
    got = lax.all_to_all(flat, "wide", split_axis=0, concat_axis=0, tiled=True)
    return got.reshape(values.shape)


def shards(volume, kernel_five, kernel_six, cotangent):
    position = lax.axis_index("wide").astype(jnp.int32).reshape(1)
    half = (lax.axis_index("dp") % 2).astype(jnp.int32).reshape(1)
    for_odds, for_evens, near_slab = rims_of(volume, position)
    odds = lax.ppermute(for_odds, ("dp", "wide"), pair_perm(1))
    evens = lax.ppermute(for_evens, ("dp", "wide"), pair_perm(0))
    cot_rows = cotangent.reshape(32, 4, 16)
    part, inner, near_kernel = inner_five(near_slab, kernel_five)
    message, slope, padded = outer_five(odds, evens, near_kernel, part, inner, cot_rows, position)
    message, position, half, slope, padded = lax.optimization_barrier(
        (message, position, half, slope, padded)
    )
    gathered = exchange(message)
    gathered, position, half, slope, padded = lax.optimization_barrier(
        (gathered, position, half, slope, padded)
    )
    rows, theirs_five, own = back_five(gathered, kernel_six, slope, padded, position, half)
    got_five = core_swap(theirs_five)
    next_rows, mine_six, theirs_six = six_own(gathered, own, position, half)
    got_six = core_swap(theirs_six)
    pair_five = mine_of_five(rows, padded, got_five, half)
    pair_five, got_six, mine_six, next_rows = lax.optimization_barrier(
        (pair_five, got_six, mine_six, next_rows)
    )
    pair_six = (mine_six.astype(jnp.float32) + got_six.astype(jnp.float32)).astype(jnp.bfloat16)
    chips_six = from_chips(pair_six)
    spread = exchange(pair_five)
    total_six = sum_of_chips(pair_six, chips_six)
    out_six = both_halves(half, total_six, core_swap(total_six))
    next_input = next_rows.T.reshape(1, 8, 4, 4, 16)
    spread, out_six, next_input = lax.optimization_barrier((spread, out_six, next_input))
    depth_five = spread.astype(jnp.float32).sum(0).astype(jnp.bfloat16)
    total_five = sum_of_chips(depth_five, from_chips(depth_five))
    out_five = both_halves(half, total_five, core_swap(total_five))
    out_five = out_five.transpose(0, 2, 1).reshape(3, 3, 3, 128, 16)
    out_six = out_six.transpose(0, 2, 1).reshape(3, 3, 3, 256, 16)
    return (next_input, out_five, out_six)


def solution(mesh):
    in_specs = (P("dp", "wide", None, None, None), P(), P(), P("dp", None, None, None, "wide"))
    out_specs = (
        P("dp", None, None, None, "wide"),
        P(None, None, None, None, "wide"),
        P(None, None, None, None, "wide"),
    )
    return jax.shard_map(shards, mesh=mesh, in_specs=in_specs, out_specs=out_specs, check_vma=False)
```

```python
import jax
import jax.numpy as jnp
from jax import lax
from jax.experimental import pallas as pl
from jax.experimental.pallas import tpu as pltpu
from jax.sharding import PartitionSpec as P

SLOPE = 0.3
HALF_TAPS = 14
VMEM = pltpu.VMEM
NT = (((1,), (1,)), ((), ()))


def both_of(value):
    sigma = 1.0 / (1.0 + jnp.exp(-value))
    act = value * (SLOPE + (1.0 - SLOPE) * sigma)
    slope = 0.125 * SLOPE + (0.125 * (1.0 - SLOPE)) * (sigma + value * sigma * (1.0 - sigma))
    return act, slope


def call(body, out_shape, scratch, operands, scalars=(), flops=0, limit=16, far=(), far_out=False):
    specs = [pl.BlockSpec(memory_space=pltpu.SMEM)] * len(scalars)
    specs += [
        pl.BlockSpec(memory_space=pltpu.HBM if index in far else VMEM)
        for index in range(len(operands))
    ]
    place = pltpu.HBM if far_out else VMEM
    outs = jax.tree.map(lambda _: pl.BlockSpec(memory_space=place), out_shape)
    return pl.pallas_call(
        body,
        out_shape=out_shape,
        in_specs=specs,
        out_specs=outs,
        scratch_shapes=scratch,
        compiler_params=pltpu.CompilerParams(vmem_limit_bytes=int(limit * 1024 * 1024)),
        cost_estimate=pl.CostEstimate(flops=flops, bytes_accessed=4_000_000, transcendentals=0),
    )(*scalars, *operands)


def shape(dims, kind):
    return jax.ShapeDtypeStruct(dims, kind)


def shifted_rows(values, step, period):
    if step == 0:
        return values
    count = values.shape[0]
    column = lax.broadcasted_iota(jnp.int32, values.shape, 0) % period
    rolled = pltpu.roll(values, (-step) % count, 0)
    inside = (column + step >= 0) & (column + step < period)
    return jnp.where(inside, rolled, 0.0)


def columns_of(padded, index, source):
    values = source.astype(jnp.float32)
    padded[index, 0:16, :] = jnp.zeros((16, 384), jnp.bfloat16)
    padded[index, 272:288, :] = jnp.zeros((16, 384), jnp.bfloat16)
    padded[index, 16:272, 0:128] = shifted_rows(values, -1, 16).astype(jnp.bfloat16)
    padded[index, 16:272, 128:256] = source
    padded[index, 16:272, 256:384] = shifted_rows(values, 1, 16).astype(jnp.bfloat16)


def depth_term(padded, first, planes, kernel, depth_tap):
    cells = jnp.concatenate(
        [
            padded[first : first + planes, 16 * row_tap : 16 * row_tap + 256, :].reshape(
                256 * planes, 384
            )
            for row_tap in range(3)
        ],
        axis=1,
    )
    taps = kernel[depth_tap * 1152 : depth_tap * 1152 + 1152, :]
    return jnp.dot(cells, taps, preferred_element_type=jnp.float32)


def rims_kernel(position, slab, for_odds, for_evens, near):
    even = position[0] % 2 == 0
    near[...] = slab[...]
    for_odds[...] = jnp.where(even, slab[0], slab[1])
    for_evens[...] = jnp.where(even, slab[1], slab[0])


def rims_of(slab, position):
    rim = shape((256, 128), jnp.bfloat16)
    near = shape((2, 256, 128), jnp.bfloat16)
    return call(rims_kernel, (rim, rim, near), [], (slab.reshape(2, 256, 128),), (position,), flops=6_000_000_000)


def inner_kernel(slab, kernel, part, padded):
    for plane in range(2):
        columns_of(padded, plane, slab[plane])
    for plane in range(2):
        total = depth_term(padded, plane, 1, kernel, 1)
        total += depth_term(padded, 1 - plane, 1, kernel, 2 - 2 * plane)
        part[plane * 256 : (plane + 1) * 256, :] = total


def inner_five(slab, kernel):
    return call(
        inner_kernel,
        (shape((512, 256), jnp.float32), shape((2, 288, 384), jnp.bfloat16)),
        [],
        (slab, kernel.reshape(3456, 256)),
        flops=600_000_000,
    )


def outer_kernel(position, odds, evens, kernel, part, inner, cot, message, slope, padded, tall):
    even = position[0] % 2 == 0
    blank = jnp.zeros((256, 128), jnp.bfloat16)
    low = jnp.where(even, odds[...], evens[...])
    high = jnp.where(even, evens[...], odds[...])
    columns_of(padded, 0, jnp.where(position[0] == 0, blank, low))
    columns_of(padded, 3, jnp.where(position[0] == 15, blank, high))
    padded[1:3] = inner[...]
    acts = []
    for plane in range(2):
        total = part[plane * 256 : (plane + 1) * 256, :]
        total += depth_term(padded, 3 * plane, 1, kernel, 2 * plane)
        act, slant = both_of(total)
        slope[plane * 256 : (plane + 1) * 256, :] = slant
        acts.append(act)
    two = (acts[0] + acts[1]).reshape(8, 2, 16, 256)
    pairs = (two[:, 0] + two[:, 1]).reshape(128, 256)
    pooled = []
    for side in range(2):
        tall[side] = pairs[:, side * 128 : (side + 1) * 128]
        even = tall[side, pl.ds(0, 64, stride=2), :]
        odd = tall[side, pl.ds(1, 64, stride=2), :]
        pooled.append(((even + odd) * 0.125).astype(jnp.bfloat16))
    cells = cot[...].astype(jnp.float32).reshape(128, 16)
    same = lax.broadcasted_iota(jnp.int32, (16, 16), 0) == lax.broadcasted_iota(
        jnp.int32, (16, 16), 1
    )
    unit = jnp.where(same, 1.0, 0.0)
    marks = lax.dot_general(
        unit.astype(jnp.bfloat16),
        cells.astype(jnp.bfloat16),
        NT,
        preferred_element_type=jnp.float32,
    ).astype(jnp.bfloat16)
    for target in range(16):
        message[target, 0:64, :] = pooled[0]
        message[target, 64:128, :] = pooled[1]
        message[target, 128:144, :] = marks


def outer_five(odds, evens, kernel, part, inner, cot_rows, position):
    return call(
        outer_kernel,
        (
            shape((16, 144, 128), jnp.bfloat16),
            shape((512, 256), jnp.float32),
            shape((4, 288, 384), jnp.bfloat16),
        ),
        [VMEM((2, 128, 128), jnp.float32)],
        (
            odds,
            evens,
            kernel,
            part,
            inner,
            cot_rows,
        ),
        (position,),
        flops=300_000_000,
    )


def six_to_five(position, gathered, kernel, slope, rows_out, own, near, tall):
    for plane in range(5):
        where = position[0] + (plane - 2)
        inside = (where >= 0) & (where < 16)
        index = jnp.clip(where, 0, 15)
        left = gathered[index, 0:64, :]
        right = gathered[index, 64:128, :]
        values = jnp.concatenate([left, right], axis=1).astype(jnp.float32)
        values = jnp.where(inside, values, 0.0)
        blank = jnp.zeros((8, 256), jnp.float32)
        for col_tap in range(3):
            moved = shifted_rows(values, col_tap - 1, 8)
            for row_tap in range(3):
                if row_tap == 0:
                    cells = jnp.concatenate([blank, moved[:56]], axis=0)
                elif row_tap == 1:
                    cells = moved
                else:
                    cells = jnp.concatenate([moved[8:], blank], axis=0)
                lane = (row_tap * 3 + col_tap) * 256
                near[plane, :, lane : lane + 256] = cells.astype(jnp.bfloat16)
    pre_six = jnp.zeros((192, 256), jnp.float32)
    for depth_tap in range(3):
        taps = kernel[depth_tap * 9 : depth_tap * 9 + 9].reshape(2304, 256)
        cells = near[depth_tap : depth_tap + 3].reshape(192, 2304)
        pre_six += jnp.dot(cells, taps, preferred_element_type=jnp.float32)
    _, slant = both_of(pre_six)
    cell = lax.broadcasted_iota(jnp.int32, (192, 128), 0)
    lanes = lax.broadcasted_iota(jnp.int32, (192, 128), 1)
    depth = cell // 64 + position[0] - 1
    small = (depth >> 1) * 16 + ((cell % 64) >> 4) * 4 + ((cell % 8) >> 1)
    hit = (small == lanes) & (depth >= 0) & (depth < 16)
    grow = jnp.where(hit, 1.0, 0.0).astype(jnp.bfloat16)
    cot = gathered[:, 128:144, :].reshape(256, 128)
    upstream = lax.dot_general(grow, cot, NT, preferred_element_type=jnp.float32)
    grad_six = (upstream * slant).astype(jnp.bfloat16).astype(jnp.float32)
    blank = jnp.zeros((8, 256), jnp.float32)
    for depth_tap in range(3):
        values = grad_six[(2 - depth_tap) * 64 : (3 - depth_tap) * 64]
        for col_tap in range(3):
            moved = shifted_rows(values, 1 - col_tap, 8)
            for row_tap in range(3):
                if row_tap == 0:
                    cells = jnp.concatenate([moved[8:], blank], axis=0)
                elif row_tap == 1:
                    cells = moved
                else:
                    cells = jnp.concatenate([blank, moved[:56]], axis=0)
                lane = (row_tap * 3 + col_tap) * 256
                near[depth_tap, :, lane : lane + 256] = cells.astype(jnp.bfloat16)

    filters = lax.broadcasted_iota(jnp.int32, (16, 256), 0) + position[0] * 16
    lanes = lax.broadcasted_iota(jnp.int32, (16, 256), 1)
    pick = jnp.where(filters == lanes, 1.0, 0.0).astype(jnp.bfloat16)

    def depth_of(depth_tap, total):
        for tap in range(9):
            both = lax.dot_general(
                jnp.concatenate([near[depth_tap, :, tap * 256 : tap * 256 + 256], pick], axis=0),
                kernel[depth_tap * 9 + tap],
                NT,
                preferred_element_type=jnp.float32,
            )
            total += both[:64]
            own[depth_tap * 9 + tap] = both[64:].astype(jnp.bfloat16)
        return total

    grad_pooled = lax.fori_loop(0, 3, depth_of, jnp.zeros((64, 256), jnp.float32))
    for side in range(2):
        tall[side, pl.ds(0, 64, stride=2), :] = grad_pooled[:, side * 128 : (side + 1) * 128]
        tall[side, pl.ds(1, 64, stride=2), :] = grad_pooled[:, side * 128 : (side + 1) * 128]
    both = jnp.concatenate([tall[0], tall[1]], axis=1)
    wide = jnp.broadcast_to(both.reshape(8, 1, 16, 256), (8, 2, 16, 256)).reshape(256, 256)
    for plane in range(2):
        grad = wide * slope[plane * 256 : (plane + 1) * 256, :]
        rows_out[:, plane * 256 : (plane + 1) * 256] = grad.T.astype(jnp.bfloat16)


def tap_cells(padded, plane, tap):
    depth_tap, row_tap, col_tap = tap // 9, (tap // 3) % 3, tap % 3
    return padded[
        plane + depth_tap,
        pl.ds(pl.multiple_of(row_tap * 16, 16), 256),
        pl.ds(pl.multiple_of(col_tap * 128, 128), 128),
    ]


def half_of_five(first, rows, padded, out, got=None, send=None):
    for step in range(0, HALF_TAPS, 2):
        taps = [jnp.minimum(first + step + other, 26) for other in range(2)]
        total = jnp.zeros((256, 256), jnp.float32)
        for plane in range(2):
            cells = jnp.concatenate([tap_cells(padded, plane, tap) for tap in taps], axis=1)
            total += jnp.dot(
                rows[:, plane * 256 : (plane + 1) * 256],
                cells,
                preferred_element_type=jnp.float32,
            )
        for other in range(2):
            part = total[:, other * 128 : (other + 1) * 128]
            if got is not None:
                part += got[:, step + other].reshape(256, 128).astype(jnp.float32)
            out[:, step + other] = part.astype(jnp.bfloat16).reshape(16, 16, 128)
        if send is not None:
            send(step)


def back_kernel(
    position, half, gathered, kernel, slope, padded, rows, theirs, own, near, tall
):
    six_to_five(position, gathered, kernel, slope, rows, own, near, tall)
    half_of_five((1 - half[0]) * HALF_TAPS, rows, padded, theirs)


def back_five(gathered, kernel, slope, padded, position, half):
    return call(
        back_kernel,
        (
            shape((256, 512), jnp.bfloat16),
            shape((16, HALF_TAPS, 16, 128), jnp.bfloat16),
            shape((27, 16, 256), jnp.bfloat16),
        ),
        [VMEM((5, 64, 2304), jnp.bfloat16), VMEM((2, 128, 128), jnp.float32)],
        (gathered, kernel.reshape(27, 256, 256), slope, padded),
        (position, half),
        flops=3_000_000_000,
    )


def mine_kernel(half, rows, padded, got, mine, staged, marks):
    sends = []

    def send(step):
        pair = pl.ds(step, 2)
        sends.append(
            pltpu.make_async_copy(staged.at[:, pair], mine.at[:, pair], marks.at[step // 2])
        )
        sends[-1].start()

    half_of_five(half[0] * HALF_TAPS, rows, padded, staged, got, send)
    for copy in sends:
        copy.wait()


def mine_of_five(rows, padded, got, half):
    return call(
        mine_kernel,
        shape((16, HALF_TAPS, 16, 128), jnp.bfloat16),
        [
            VMEM((16, HALF_TAPS, 16, 128), jnp.bfloat16),
            pltpu.SemaphoreType.DMA((HALF_TAPS // 2,)),
        ],
        (rows, padded, got),
        (half,),
        flops=900_000_000,
        far_out=True,
    )


def shifted_lanes(values, step, period, inner):
    if step == 0:
        return values
    count = values.shape[1]
    place = (lax.broadcasted_iota(jnp.int32, values.shape, 1) // inner) % period
    rolled = pltpu.roll(values, (-step * inner) % count, 1)
    inside = (place + step >= 0) & (place + step < period)
    return jnp.where(inside, rolled, 0.0)


def six_kernel(
    position, half, gathered, own, next_rows, mine, theirs, cells, grads, whole
):
    blank = jnp.zeros((64, 256), jnp.bfloat16)
    cells[0:64, :] = blank
    cells[1088:1152, :] = blank
    cells[64:1088, 0:128] = gathered[:, 0:64, :].reshape(1024, 128)
    cells[64:1088, 128:256] = gathered[:, 64:128, :].reshape(1024, 128)
    products = lax.dot_general(
        own[...].reshape(432, 256), cells[...], NT, preferred_element_type=jnp.float32
    )
    taps = products[0:144, 0:1024] + products[144:288, 64:1088] + products[288:432, 128:1152]
    pre = jnp.zeros((16, 1024), jnp.float32)
    for row_tap in range(3):
        line = jnp.zeros((16, 1024), jnp.float32)
        for col_tap in range(3):
            start = (row_tap * 3 + col_tap) * 16
            line += shifted_lanes(taps[start : start + 16], col_tap - 1, 8, 1)
        pre += shifted_lanes(line, row_tap - 1, 8, 8)
    act, slant = both_of(pre)
    small = lax.broadcasted_iota(jnp.int32, (128, 1024), 0)
    cell = lax.broadcasted_iota(jnp.int32, (128, 1024), 1)
    target = (cell >> 7) * 16 + ((cell % 64) >> 4) * 4 + ((cell % 8) >> 1)
    grow = jnp.where(small == target, 1.0, 0.0).astype(jnp.bfloat16)
    cot = gathered[position[0], 128:144, :]
    upstream = jnp.dot(cot, grow, preferred_element_type=jnp.float32)
    high = act.astype(jnp.bfloat16)
    rest = act - high.astype(jnp.float32)
    middle = rest.astype(jnp.bfloat16)
    low = (rest - middle.astype(jnp.float32)).astype(jnp.bfloat16)
    sums = lax.dot_general(
        jnp.concatenate([high, middle, low], axis=0), grow, NT, preferred_element_type=jnp.float32
    )
    next_rows[...] = ((sums[0:16] + sums[16:32] + sums[32:48]) * 0.125).astype(jnp.bfloat16)
    grad = (upstream * slant).astype(jnp.bfloat16).astype(jnp.float32)
    for row_tap in range(3):
        line = shifted_lanes(grad, 1 - row_tap, 8, 8)
        for col_tap in range(3):
            start = (row_tap * 3 + col_tap) * 16
            moved = shifted_lanes(line, 1 - col_tap, 8, 1)
            grads[start : start + 16, :] = moved.astype(jnp.bfloat16)
    for depth_tap in range(3):
        part = jnp.dot(
            grads[...],
            cells[depth_tap * 64 : depth_tap * 64 + 1024, :],
            preferred_element_type=jnp.float32,
        )
        whole[depth_tap * 9 : depth_tap * 9 + 9] = part.astype(jnp.bfloat16).reshape(9, 16, 256)
    whole[27] = whole[26]
    mine[...] = whole[pl.ds(half[0] * HALF_TAPS, HALF_TAPS)]
    theirs[...] = whole[pl.ds((1 - half[0]) * HALF_TAPS, HALF_TAPS)]


def six_own(gathered, own, position, half):
    part = shape((HALF_TAPS, 16, 256), jnp.bfloat16)
    return call(
        six_kernel,
        (shape((16, 128), jnp.bfloat16), part, part),
        [
            VMEM((1152, 256), jnp.bfloat16),
            VMEM((144, 1024), jnp.bfloat16),
            VMEM((28, 16, 256), jnp.bfloat16),
        ],
        (gathered, own),
        (position, half),
        flops=2_000_000_000,
    )


def halves_kernel(half, mine, other, out):
    for step in range(HALF_TAPS):
        for first, part in ((half[0] * HALF_TAPS, mine), ((1 - half[0]) * HALF_TAPS, other)):
            tap = jnp.minimum(first + step, 26)
            out[tap] = part[step].astype(jnp.float32)


def both_halves(half, mine, other):
    return call(
        halves_kernel,
        shape((27,) + mine.shape[1:], jnp.float32),
        [],
        (mine, other),
        (half,),
    )


def pair_perm(first):
    volumes, count = lax.axis_size("dp"), lax.axis_size("wide")
    pairs = []
    for volume in range(volumes):
        for place in range(count):
            other = place + 1 if place % 2 == first else place - 1
            if 0 <= other < count:
                pairs.append((volume * count + place, volume * count + other))
            else:
                pairs.append((volume * count + place, (volume ^ 1) * count + place))
    return pairs


def core_swap(values):
    count = lax.axis_size("dp")
    return lax.ppermute(values, "dp", [(i, i ^ 1) for i in range(count)])


def from_chips(values):
    count = lax.axis_size("dp")
    return [
        lax.ppermute(values, "dp", [(i, i ^ step) for i in range(count)]) for step in (2, 6, 4)
    ]


def sum_of_chips(values, others):
    beside, across, ahead = [other.astype(jnp.float32) for other in others]
    return ((values.astype(jnp.float32) + beside) + (across + ahead)).astype(jnp.bfloat16)


def exchange(values):
    flat = values.reshape(values.shape[0], -1, values.shape[-1])
    got = lax.all_to_all(flat, "wide", split_axis=0, concat_axis=0, tiled=True)
    return got.reshape(values.shape)


def shards(volume, kernel_five, kernel_six, cotangent):
    position = lax.axis_index("wide").astype(jnp.int32).reshape(1)
    half = (lax.axis_index("dp") % 2).astype(jnp.int32).reshape(1)
    for_odds, for_evens, near_slab = rims_of(volume, position)
    odds = lax.ppermute(for_odds, ("dp", "wide"), pair_perm(1))
    evens = lax.ppermute(for_evens, ("dp", "wide"), pair_perm(0))
    cot_rows = cotangent.reshape(32, 4, 16)
    part, inner = inner_five(near_slab, kernel_five)
    message, slope, padded = outer_five(odds, evens, kernel_five.reshape(3456, 256), part, inner, cot_rows, position)
    message, position, half, slope, padded = lax.optimization_barrier(
        (message, position, half, slope, padded)
    )
    gathered = exchange(message)
    gathered, position, half, slope, padded = lax.optimization_barrier(
        (gathered, position, half, slope, padded)
    )
    rows, theirs_five, own = back_five(gathered, kernel_six, slope, padded, position, half)
    got_five = core_swap(theirs_five)
    next_rows, mine_six, theirs_six = six_own(gathered, own, position, half)
    got_six = core_swap(theirs_six)
    pair_five = mine_of_five(rows, padded, got_five, half)
    pair_five, got_six, mine_six, next_rows = lax.optimization_barrier(
        (pair_five, got_six, mine_six, next_rows)
    )
    pair_six = (mine_six.astype(jnp.float32) + got_six.astype(jnp.float32)).astype(jnp.bfloat16)
    chips_six = from_chips(pair_six)
    spread = exchange(pair_five)
    total_six = sum_of_chips(pair_six, chips_six)
    out_six = both_halves(half, total_six, core_swap(total_six))
    next_input = next_rows.T.reshape(1, 8, 4, 4, 16)
    spread, out_six, next_input = lax.optimization_barrier((spread, out_six, next_input))
    depth_five = spread.astype(jnp.float32).sum(0).astype(jnp.bfloat16)
    total_five = sum_of_chips(depth_five, from_chips(depth_five))
    out_five = both_halves(half, total_five, core_swap(total_five))
    out_five = out_five.transpose(0, 2, 1).reshape(3, 3, 3, 128, 16)
    out_six = out_six.transpose(0, 2, 1).reshape(3, 3, 3, 256, 16)
    return (next_input, out_five, out_six)


def solution(mesh):
    in_specs = (P("dp", "wide", None, None, None), P(), P(), P("dp", None, None, None, "wide"))
    out_specs = (
        P("dp", None, None, None, "wide"),
        P(None, None, None, None, "wide"),
        P(None, None, None, None, "wide"),
    )
    return jax.shard_map(shards, mesh=mesh, in_specs=in_specs, out_specs=out_specs, check_vma=False)
```

```python
import jax
import jax.numpy as jnp
from jax import lax
from jax.experimental import pallas as pl
from jax.experimental.pallas import tpu as pltpu
from jax.sharding import PartitionSpec as P

SLOPE = 0.3
HALF_TAPS = 14
VMEM = pltpu.VMEM
NT = (((1,), (1,)), ((), ()))


def both_of(value):
    sigma = 1.0 / (1.0 + jnp.exp(-value))
    act = value * (SLOPE + (1.0 - SLOPE) * sigma)
    slope = 0.125 * SLOPE + (0.125 * (1.0 - SLOPE)) * (sigma + value * sigma * (1.0 - sigma))
    return act, slope


def call(body, out_shape, scratch, operands, scalars=(), flops=0, limit=16, far=(), far_out=False):
    specs = [pl.BlockSpec(memory_space=pltpu.SMEM)] * len(scalars)
    specs += [
        pl.BlockSpec(memory_space=pltpu.HBM if index in far else VMEM)
        for index in range(len(operands))
    ]
    place = pltpu.HBM if far_out else VMEM
    outs = jax.tree.map(lambda _: pl.BlockSpec(memory_space=place), out_shape)
    return pl.pallas_call(
        body,
        out_shape=out_shape,
        in_specs=specs,
        out_specs=outs,
        scratch_shapes=scratch,
        compiler_params=pltpu.CompilerParams(vmem_limit_bytes=int(limit * 1024 * 1024)),
        cost_estimate=pl.CostEstimate(flops=flops, bytes_accessed=4_000_000, transcendentals=0),
    )(*scalars, *operands)


def shape(dims, kind):
    return jax.ShapeDtypeStruct(dims, kind)


def shifted_rows(values, step, period):
    if step == 0:
        return values
    count = values.shape[0]
    column = lax.broadcasted_iota(jnp.int32, values.shape, 0) % period
    rolled = pltpu.roll(values, (-step) % count, 0)
    inside = (column + step >= 0) & (column + step < period)
    return jnp.where(inside, rolled, 0.0)


def columns_of(padded, index, source):
    values = source.astype(jnp.float32)
    padded[index, 0:16, :] = jnp.zeros((16, 384), jnp.bfloat16)
    padded[index, 272:288, :] = jnp.zeros((16, 384), jnp.bfloat16)
    padded[index, 16:272, 0:128] = shifted_rows(values, -1, 16).astype(jnp.bfloat16)
    padded[index, 16:272, 128:256] = source
    padded[index, 16:272, 256:384] = shifted_rows(values, 1, 16).astype(jnp.bfloat16)


def depth_term(padded, first, planes, kernel, depth_tap):
    cells = jnp.concatenate(
        [
            padded[first : first + planes, 16 * row_tap : 16 * row_tap + 256, :].reshape(
                256 * planes, 384
            )
            for row_tap in range(3)
        ],
        axis=1,
    )
    taps = kernel[depth_tap * 1152 : depth_tap * 1152 + 1152, :]
    return jnp.dot(cells, taps, preferred_element_type=jnp.float32)


def rims_kernel(position, slab, for_odds, for_evens, near):
    even = position[0] % 2 == 0
    near[...] = slab[...]
    for_odds[...] = jnp.where(even, slab[0], slab[1])
    for_evens[...] = jnp.where(even, slab[1], slab[0])


def rims_of(slab, position):
    rim = shape((256, 128), jnp.bfloat16)
    near = shape((2, 256, 128), jnp.bfloat16)
    return call(rims_kernel, (rim, rim, near), [], (slab.reshape(2, 256, 128),), (position,), flops=6_000_000_000)


def inner_kernel(slab, kernel, part, padded):
    for plane in range(2):
        columns_of(padded, plane, slab[plane])
    for plane in range(2):
        total = depth_term(padded, plane, 1, kernel, 1)
        total += depth_term(padded, 1 - plane, 1, kernel, 2 - 2 * plane)
        part[plane * 256 : (plane + 1) * 256, :] = total


def inner_five(slab, kernel):
    return call(
        inner_kernel,
        (shape((512, 256), jnp.float32), shape((2, 288, 384), jnp.bfloat16)),
        [],
        (slab, kernel.reshape(3456, 256)),
        flops=600_000_000,
    )


def outer_kernel(position, odds, evens, kernel, part, inner, cot, message, slope, padded, tall):
    even = position[0] % 2 == 0
    blank = jnp.zeros((256, 128), jnp.bfloat16)
    low = jnp.where(even, odds[...], evens[...])
    high = jnp.where(even, evens[...], odds[...])
    columns_of(padded, 0, jnp.where(position[0] == 0, blank, low))
    columns_of(padded, 3, jnp.where(position[0] == 15, blank, high))
    padded[1:3] = inner[...]
    acts = []
    for plane in range(2):
        total = part[plane * 256 : (plane + 1) * 256, :]
        total += depth_term(padded, 3 * plane, 1, kernel, 2 * plane)
        act, slant = both_of(total)
        slope[plane * 256 : (plane + 1) * 256, :] = slant
        acts.append(act)
    two = (acts[0] + acts[1]).reshape(8, 2, 16, 256)
    pairs = (two[:, 0] + two[:, 1]).reshape(128, 256)
    pooled = []
    for side in range(2):
        tall[side] = pairs[:, side * 128 : (side + 1) * 128]
        even = tall[side, pl.ds(0, 64, stride=2), :]
        odd = tall[side, pl.ds(1, 64, stride=2), :]
        pooled.append(((even + odd) * 0.125).astype(jnp.bfloat16))
    cells = cot[...].astype(jnp.float32).reshape(128, 16)
    same = lax.broadcasted_iota(jnp.int32, (16, 16), 0) == lax.broadcasted_iota(
        jnp.int32, (16, 16), 1
    )
    unit = jnp.where(same, 1.0, 0.0)
    marks = lax.dot_general(
        unit.astype(jnp.bfloat16),
        cells.astype(jnp.bfloat16),
        NT,
        preferred_element_type=jnp.float32,
    ).astype(jnp.bfloat16)
    for target in range(16):
        message[target, 0:64, :] = pooled[0]
        message[target, 64:128, :] = pooled[1]
        message[target, 128:144, :] = marks


def outer_five(odds, evens, kernel, part, inner, cot_rows, position):
    return call(
        outer_kernel,
        (
            shape((16, 144, 128), jnp.bfloat16),
            shape((512, 256), jnp.float32),
            shape((4, 288, 384), jnp.bfloat16),
        ),
        [VMEM((2, 128, 128), jnp.float32)],
        (
            odds,
            evens,
            kernel,
            part,
            inner,
            cot_rows,
        ),
        (position,),
        flops=300_000_000,
    )


def six_to_five(position, gathered, kernel, slope, rows_out, own, near, tall):
    for plane in range(5):
        where = position[0] + (plane - 2)
        inside = (where >= 0) & (where < 16)
        index = jnp.clip(where, 0, 15)
        left = gathered[index, 0:64, :]
        right = gathered[index, 64:128, :]
        values = jnp.concatenate([left, right], axis=1).astype(jnp.float32)
        values = jnp.where(inside, values, 0.0)
        blank = jnp.zeros((8, 256), jnp.float32)
        for col_tap in range(3):
            moved = shifted_rows(values, col_tap - 1, 8)
            for row_tap in range(3):
                if row_tap == 0:
                    cells = jnp.concatenate([blank, moved[:56]], axis=0)
                elif row_tap == 1:
                    cells = moved
                else:
                    cells = jnp.concatenate([moved[8:], blank], axis=0)
                lane = (row_tap * 3 + col_tap) * 256
                near[plane, :, lane : lane + 256] = cells.astype(jnp.bfloat16)
    pre_six = jnp.zeros((192, 256), jnp.float32)
    for depth_tap in range(3):
        taps = kernel[depth_tap * 9 : depth_tap * 9 + 9].reshape(2304, 256)
        cells = near[depth_tap : depth_tap + 3].reshape(192, 2304)
        pre_six += jnp.dot(cells, taps, preferred_element_type=jnp.float32)
    _, slant = both_of(pre_six)
    cell = lax.broadcasted_iota(jnp.int32, (192, 128), 0)
    lanes = lax.broadcasted_iota(jnp.int32, (192, 128), 1)
    depth = cell // 64 + position[0] - 1
    small = (depth >> 1) * 16 + ((cell % 64) >> 4) * 4 + ((cell % 8) >> 1)
    hit = (small == lanes) & (depth >= 0) & (depth < 16)
    grow = jnp.where(hit, 1.0, 0.0).astype(jnp.bfloat16)
    cot = gathered[:, 128:144, :].reshape(256, 128)
    upstream = lax.dot_general(grow, cot, NT, preferred_element_type=jnp.float32)
    grad_six = (upstream * slant).astype(jnp.bfloat16).astype(jnp.float32)
    blank = jnp.zeros((8, 256), jnp.float32)
    for depth_tap in range(3):
        values = grad_six[(2 - depth_tap) * 64 : (3 - depth_tap) * 64]
        for col_tap in range(3):
            moved = shifted_rows(values, 1 - col_tap, 8)
            for row_tap in range(3):
                if row_tap == 0:
                    cells = jnp.concatenate([moved[8:], blank], axis=0)
                elif row_tap == 1:
                    cells = moved
                else:
                    cells = jnp.concatenate([blank, moved[:56]], axis=0)
                lane = (row_tap * 3 + col_tap) * 256
                near[depth_tap, :, lane : lane + 256] = cells.astype(jnp.bfloat16)

    filters = lax.broadcasted_iota(jnp.int32, (16, 256), 0) + position[0] * 16
    lanes = lax.broadcasted_iota(jnp.int32, (16, 256), 1)
    pick = jnp.where(filters == lanes, 1.0, 0.0).astype(jnp.bfloat16)

    def depth_of(depth_tap, total):
        for tap in range(9):
            both = lax.dot_general(
                jnp.concatenate([near[depth_tap, :, tap * 256 : tap * 256 + 256], pick], axis=0),
                kernel[depth_tap * 9 + tap],
                NT,
                preferred_element_type=jnp.float32,
            )
            total += both[:64]
            own[depth_tap * 9 + tap] = both[64:].astype(jnp.bfloat16)
        return total

    grad_pooled = lax.fori_loop(0, 3, depth_of, jnp.zeros((64, 256), jnp.float32))
    for side in range(2):
        tall[side, pl.ds(0, 64, stride=2), :] = grad_pooled[:, side * 128 : (side + 1) * 128]
        tall[side, pl.ds(1, 64, stride=2), :] = grad_pooled[:, side * 128 : (side + 1) * 128]
    both = jnp.concatenate([tall[0], tall[1]], axis=1)
    wide = jnp.broadcast_to(both.reshape(8, 1, 16, 256), (8, 2, 16, 256)).reshape(256, 256)
    for plane in range(2):
        grad = wide * slope[plane * 256 : (plane + 1) * 256, :]
        rows_out[:, plane * 256 : (plane + 1) * 256] = grad.T.astype(jnp.bfloat16)


def tap_cells(padded, plane, tap):
    depth_tap, row_tap, col_tap = tap // 9, (tap // 3) % 3, tap % 3
    return padded[
        plane + depth_tap,
        pl.ds(pl.multiple_of(row_tap * 16, 16), 256),
        pl.ds(pl.multiple_of(col_tap * 128, 128), 128),
    ]


def half_of_five(first, rows, padded, out):
    for step in range(0, HALF_TAPS, 2):
        taps = [jnp.minimum(first + step + other, 26) for other in range(2)]
        total = jnp.zeros((256, 256), jnp.float32)
        for plane in range(2):
            cells = jnp.concatenate([tap_cells(padded, plane, tap) for tap in taps], axis=1)
            total += jnp.dot(
                rows[:, plane * 256 : (plane + 1) * 256],
                cells,
                preferred_element_type=jnp.float32,
            )
        for other in range(2):
            part = total[:, other * 128 : (other + 1) * 128]
            out[:, step + other] = part.astype(out.dtype).reshape(16, 16, 128)


def back_kernel(
    position, half, gathered, kernel, slope, padded, rows, theirs, own, near, tall
):
    six_to_five(position, gathered, kernel, slope, rows, own, near, tall)
    half_of_five((1 - half[0]) * HALF_TAPS, rows, padded, theirs)


def back_five(gathered, kernel, slope, padded, position, half):
    return call(
        back_kernel,
        (
            shape((256, 512), jnp.bfloat16),
            shape((16, HALF_TAPS, 16, 128), jnp.bfloat16),
            shape((27, 16, 256), jnp.bfloat16),
        ),
        [VMEM((5, 64, 2304), jnp.bfloat16), VMEM((2, 128, 128), jnp.float32)],
        (gathered, kernel.reshape(27, 256, 256), slope, padded),
        (position, half),
        flops=3_000_000_000,
    )


def mine_kernel(half, rows, padded, mine):
    half_of_five(half[0] * HALF_TAPS, rows, padded, mine)


def mine_of_five(rows, padded, half):
    return call(
        mine_kernel,
        shape((16, HALF_TAPS, 16, 128), jnp.float32),
        [],
        (rows, padded),
        (half,),
        flops=900_000_000,
    )


def pair_kernel(mine, got, out, staged, marks):
    sends = []
    for group in range(4):
        part = pl.ds(group * 4, 4)
        staged[part] = (mine[part] + got[part].astype(jnp.float32)).astype(jnp.bfloat16)
        sends.append(pltpu.make_async_copy(staged.at[part], out.at[part], marks.at[group]))
        sends[-1].start()
    for copy in sends:
        copy.wait()


def pair_of_five(mine, got):
    return call(
        pair_kernel,
        shape(got.shape, jnp.bfloat16),
        [VMEM(got.shape, jnp.bfloat16), pltpu.SemaphoreType.DMA((4,))],
        (mine, got),
        far_out=True,
    )


def shifted_lanes(values, step, period, inner):
    if step == 0:
        return values
    count = values.shape[1]
    place = (lax.broadcasted_iota(jnp.int32, values.shape, 1) // inner) % period
    rolled = pltpu.roll(values, (-step * inner) % count, 1)
    inside = (place + step >= 0) & (place + step < period)
    return jnp.where(inside, rolled, 0.0)


def six_kernel(
    position, half, gathered, own, next_rows, mine, theirs, cells, grads, whole
):
    blank = jnp.zeros((64, 256), jnp.bfloat16)
    cells[0:64, :] = blank
    cells[1088:1152, :] = blank
    cells[64:1088, 0:128] = gathered[:, 0:64, :].reshape(1024, 128)
    cells[64:1088, 128:256] = gathered[:, 64:128, :].reshape(1024, 128)
    products = lax.dot_general(
        own[...].reshape(432, 256), cells[...], NT, preferred_element_type=jnp.float32
    )
    taps = products[0:144, 0:1024] + products[144:288, 64:1088] + products[288:432, 128:1152]
    pre = jnp.zeros((16, 1024), jnp.float32)
    for row_tap in range(3):
        line = jnp.zeros((16, 1024), jnp.float32)
        for col_tap in range(3):
            start = (row_tap * 3 + col_tap) * 16
            line += shifted_lanes(taps[start : start + 16], col_tap - 1, 8, 1)
        pre += shifted_lanes(line, row_tap - 1, 8, 8)
    act, slant = both_of(pre)
    small = lax.broadcasted_iota(jnp.int32, (128, 1024), 0)
    cell = lax.broadcasted_iota(jnp.int32, (128, 1024), 1)
    target = (cell >> 7) * 16 + ((cell % 64) >> 4) * 4 + ((cell % 8) >> 1)
    grow = jnp.where(small == target, 1.0, 0.0).astype(jnp.bfloat16)
    cot = gathered[position[0], 128:144, :]
    upstream = jnp.dot(cot, grow, preferred_element_type=jnp.float32)
    high = act.astype(jnp.bfloat16)
    rest = act - high.astype(jnp.float32)
    middle = rest.astype(jnp.bfloat16)
    low = (rest - middle.astype(jnp.float32)).astype(jnp.bfloat16)
    sums = lax.dot_general(
        jnp.concatenate([high, middle, low], axis=0), grow, NT, preferred_element_type=jnp.float32
    )
    next_rows[...] = ((sums[0:16] + sums[16:32] + sums[32:48]) * 0.125).astype(jnp.bfloat16)
    grad = (upstream * slant).astype(jnp.bfloat16).astype(jnp.float32)
    for row_tap in range(3):
        line = shifted_lanes(grad, 1 - row_tap, 8, 8)
        for col_tap in range(3):
            start = (row_tap * 3 + col_tap) * 16
            moved = shifted_lanes(line, 1 - col_tap, 8, 1)
            grads[start : start + 16, :] = moved.astype(jnp.bfloat16)
    for depth_tap in range(3):
        part = jnp.dot(
            grads[...],
            cells[depth_tap * 64 : depth_tap * 64 + 1024, :],
            preferred_element_type=jnp.float32,
        )
        whole[depth_tap * 9 : depth_tap * 9 + 9] = part.astype(jnp.bfloat16).reshape(9, 16, 256)
    whole[27] = whole[26]
    mine[...] = whole[pl.ds(half[0] * HALF_TAPS, HALF_TAPS)]
    theirs[...] = whole[pl.ds((1 - half[0]) * HALF_TAPS, HALF_TAPS)]


def six_own(gathered, own, position, half):
    part = shape((HALF_TAPS, 16, 256), jnp.bfloat16)
    return call(
        six_kernel,
        (shape((16, 128), jnp.bfloat16), part, part),
        [
            VMEM((1152, 256), jnp.bfloat16),
            VMEM((144, 1024), jnp.bfloat16),
            VMEM((28, 16, 256), jnp.bfloat16),
        ],
        (gathered, own),
        (position, half),
        flops=2_000_000_000,
    )


def halves_kernel(half, mine, other, out):
    for step in range(HALF_TAPS):
        for first, part in ((half[0] * HALF_TAPS, mine), ((1 - half[0]) * HALF_TAPS, other)):
            tap = jnp.minimum(first + step, 26)
            out[tap] = part[step].astype(jnp.float32)


def both_halves(half, mine, other):
    return call(
        halves_kernel,
        shape((27,) + mine.shape[1:], jnp.float32),
        [],
        (mine, other),
        (half,),
    )


def pair_perm(first):
    volumes, count = lax.axis_size("dp"), lax.axis_size("wide")
    pairs = []
    for volume in range(volumes):
        for place in range(count):
            other = place + 1 if place % 2 == first else place - 1
            if 0 <= other < count:
                pairs.append((volume * count + place, volume * count + other))
            else:
                pairs.append((volume * count + place, (volume ^ 1) * count + place))
    return pairs


def core_swap(values):
    count = lax.axis_size("dp")
    return lax.ppermute(values, "dp", [(i, i ^ 1) for i in range(count)])


def from_chips(values):
    count = lax.axis_size("dp")
    return [
        lax.ppermute(values, "dp", [(i, i ^ step) for i in range(count)]) for step in (2, 6, 4)
    ]


def sum_of_chips(values, others):
    beside, across, ahead = [other.astype(jnp.float32) for other in others]
    return ((values.astype(jnp.float32) + beside) + (across + ahead)).astype(jnp.bfloat16)


def exchange(values):
    flat = values.reshape(values.shape[0], -1, values.shape[-1])
    got = lax.all_to_all(flat, "wide", split_axis=0, concat_axis=0, tiled=True)
    return got.reshape(values.shape)


def shards(volume, kernel_five, kernel_six, cotangent):
    position = lax.axis_index("wide").astype(jnp.int32).reshape(1)
    half = (lax.axis_index("dp") % 2).astype(jnp.int32).reshape(1)
    for_odds, for_evens, near_slab = rims_of(volume, position)
    odds = lax.ppermute(for_odds, ("dp", "wide"), pair_perm(1))
    evens = lax.ppermute(for_evens, ("dp", "wide"), pair_perm(0))
    cot_rows = cotangent.reshape(32, 4, 16)
    part, inner = inner_five(near_slab, kernel_five)
    message, slope, padded = outer_five(odds, evens, kernel_five.reshape(3456, 256), part, inner, cot_rows, position)
    message, position, half, slope, padded = lax.optimization_barrier(
        (message, position, half, slope, padded)
    )
    gathered = exchange(message)
    gathered, position, half, slope, padded = lax.optimization_barrier(
        (gathered, position, half, slope, padded)
    )
    rows, theirs_five, own = back_five(gathered, kernel_six, slope, padded, position, half)
    got_five = core_swap(theirs_five)
    next_rows, mine_six, theirs_six = six_own(gathered, own, position, half)
    mine_five = mine_of_five(rows, padded, half)
    got_five, mine_five, theirs_six, mine_six, next_rows = lax.optimization_barrier(
        (got_five, mine_five, theirs_six, mine_six, next_rows)
    )
    pair_five = pair_of_five(mine_five, got_five)
    pair_five, theirs_six, mine_six, next_rows = lax.optimization_barrier(
        (pair_five, theirs_six, mine_six, next_rows)
    )
    got_six = core_swap(theirs_six)
    pair_six = (mine_six.astype(jnp.float32) + got_six.astype(jnp.float32)).astype(jnp.bfloat16)
    chips_six = from_chips(pair_six)
    spread = exchange(pair_five)
    total_six = sum_of_chips(pair_six, chips_six)
    out_six = both_halves(half, total_six, core_swap(total_six))
    next_input = next_rows.T.reshape(1, 8, 4, 4, 16)
    spread, out_six = lax.optimization_barrier((spread, out_six))
    depth_five = spread.astype(jnp.float32).sum(0).astype(jnp.bfloat16)
    total_five = sum_of_chips(depth_five, from_chips(depth_five))
    out_five = both_halves(half, total_five, core_swap(total_five))
    out_five = out_five.transpose(0, 2, 1).reshape(3, 3, 3, 128, 16)
    out_six = out_six.transpose(0, 2, 1).reshape(3, 3, 3, 256, 16)
    return (next_input, out_five, out_six)


def solution(mesh):
    in_specs = (P("dp", "wide", None, None, None), P(), P(), P("dp", None, None, None, "wide"))
    out_specs = (
        P("dp", None, None, None, "wide"),
        P(None, None, None, None, "wide"),
        P(None, None, None, None, "wide"),
    )
    return jax.shard_map(shards, mesh=mesh, in_specs=in_specs, out_specs=out_specs, check_vma=False)
```
